32 devices in a mesh: dp: 2 (over y), blk: 16 (over z, x, core).
Axes of the slice: x: 2, y: 2, z: 4, core: 2. Of those that a mesh axis runs over, the one named last changes fastest.
Arguments:
- tokens: bfloat16 [2, 16384, 768], P(None, ('dp', 'blk')), may hold values from -6 to 6
- memory: bfloat16 [2, 8, 20, 768], P(None, 'dp'), may hold values from -6 to 6
- chain_lengths: int32 [2, 2, 4], P(None, 'dp'), may hold values from 1 to 7, 16 in all within a row
- last_fill: int32 [2, 2, 4], P(None, 'dp'), may hold values from 1 to 512
- query_proj: bfloat16 [768, 768], replicated, may hold values from -0.21875 to 0.21875
- query_bias: bfloat16 [768], replicated, may hold values from -1.75 to 1.75
- key_proj: bfloat16 [768, 768], replicated, may hold values from -0.21875 to 0.21875
- value_proj: bfloat16 [768, 768], replicated, may hold values from -0.21875 to 0.21875
- value_bias: bfloat16 [768], replicated, may hold values from -1.75 to 1.75
- output_proj: bfloat16 [768, 768], replicated, may hold values from -3.5 to 3.5
- output_bias: bfloat16 [768], replicated, may hold values from -1.75 to 1.75
- attn_gain: bfloat16 [768], replicated, may hold values from 0.5 to 1.5
- attn_shift: bfloat16 [768], replicated, may hold values from -1.75 to 1.75
- inner_proj: bfloat16 [768, 3072], replicated, may hold values from -0.21875 to 0.21875
- inner_bias: bfloat16 [3072], replicated, may hold values from -1.75 to 1.75
- outer_proj: bfloat16 [3072, 768], replicated, may hold values from -0.109375 to 0.109375
- outer_bias: bfloat16 [768], replicated, may hold values from -1.75 to 1.75
- final_gain: bfloat16 [768], replicated, may hold values from 0.5 to 1.5
- final_shift: bfloat16 [768], replicated, may hold values from -1.75 to 1.75
- token_cotangent: bfloat16 [2, 16384, 768], P(None, ('dp', 'blk')), may hold values from -6 to 6
- memory_cotangent: bfloat16 [2, 8, 20, 768], P(None, 'dp'), may hold values from -6 to 6
Outputs:
- layer_output: bfloat16 [2, 16384, 768], P(None, ('dp', 'blk'))
- memory_output: bfloat16 [2, 8, 20, 768], P(None, 'dp')
- token_grad: bfloat16 [2, 16384, 768], P(None, ('dp', 'blk'))
- memory_grad: bfloat16 [2, 8, 20, 768], P(None, 'dp')
- grad_query_proj: float32 [768, 768], replicated
- grad_query_bias: float32 [768], replicated
- grad_key_proj: float32 [768, 768], replicated
- grad_value_proj: float32 [768, 768], replicated
- grad_value_bias: float32 [768], replicated
- grad_output_proj: float32 [768, 768], replicated
- grad_output_bias: float32 [768], replicated
- grad_attn_gain: float32 [768], replicated
- grad_attn_shift: float32 [768], replicated
- grad_inner_proj: float32 [768, 3072], replicated
- grad_inner_bias: float32 [3072], replicated
- grad_outer_proj: float32 [3072, 768], replicated
- grad_outer_bias: float32 [768], replicated
- grad_final_gain: float32 [768], replicated
- grad_final_shift: float32 [768], replicated
The draws below stay inside these ranges and needn't reach their ends.
Inputs may be any that keep to these rules, and one draw needn't show every extreme that they name: `chain_lengths`: the lengths of each group's 4 chains add up to 16, and the longest chain of each group has 7 segments. The tokens of a chain's last segment after last_fill are padding.
All inputs are finite; a program needn't handle non-finite values.
Results may differ from the reference program's by a relative error of at most 0.02.
Values may be sent and summed in bfloat16 or wider, within the bound.
No kernel may reach another device: no remote copies, remote signals or barrier semaphores. Data moves between devices by JAX's collectives and lax.ppermute only.
A program may use at most 384 MiB of HBM per device.

```python
import math
import jax
import jax.numpy as jnp
import numpy as np
from jax import lax

D = 768
H = 12
HD = 64
FF = 3072
SEG = 512
MAXSEG = 7
MICRO = 2
MEMT = 20
CH_GRP = 4
CHAINS = 8
TOKENS = 16384
N_DP = 2
N_BLK = 16


def with_ends(values, stream_key, least, high):
    longest = values.shape.index(max(values.shape))
    spots = []
    for shift in (0, 1):
        where = [jax.random.randint(jax.random.fold_in(stream_key, axis), (), 0, length) for axis, length in enumerate(values.shape)]
        where[longest] = (where[longest] + shift) % values.shape[longest]
        spots.append(tuple(where))
    return values.at[spots[0]].set(least).at[spots[1]].set(high)


def block_scale(key, extent, pieces, low, top_value):
    def one(dim, shards_of):
        steps = jax.random.uniform(jax.random.fold_in(jax.random.fold_in(key, 6), dim), (shards_of,), jnp.float32, low / len(pieces), top_value / len(pieces))
        return jnp.repeat(jnp.exp(steps), extent[dim] // shards_of).reshape((-1,) + (1,) * (len(extent) - dim - 1))

    loudness = one(*pieces[0])
    for cut in pieces[1:]:
        loudness = loudness * one(*cut)
    return loudness


def split_up(amount, total, most, skew):
    loads = [(1 << 20) // math.isqrt(rank ** skew) + 1 for rank in range(2, amount + 1)]
    spare, holding = total - most - (amount - 1), [1] * (amount - 1)
    while spare > 0:
        movable = [i for i in range(amount - 1) if holding[i] < most]
        pool, left = sum([loads[i] for i in movable]), spare
        for i in movable:
            extra = min(most - holding[i], max(1, left * loads[i] // pool), spare)
            holding[i] = holding[i] + extra
            spare = spare - extra
    return np.array([most] + holding)


def uneven_parts(key, count, total, bound, skew):
    if count == 2:
        one = jax.random.randint(key, (), max(1, total - bound), min(bound, total - 1) + 1)
        return jnp.stack([one, total - one])
    tallies = jnp.asarray(split_up(count, total, bound, skew), jnp.int32)
    twos = (count - 1) // 2
    giver, receiver = tallies[1:1 + 2 * twos:2], tallies[2:2 + 2 * twos:2]
    margin = jnp.minimum(giver - 1, bound - receiver)
    shifted = jax.random.randint(jax.random.fold_in(key, 1), (twos,), 0, 1 << 20) % (margin + 1)
    tallies = tallies.at[1:1 + 2 * twos:2].set(giver - shifted).at[2:2 + 2 * twos:2].set(receiver + shifted)
    return tallies[jax.random.permutation(jax.random.fold_in(key, 2), count)]


def normal_values(key, dims, spread, reach, cuts=(), held_as=jnp.bfloat16):
    values = spread * jax.random.normal(key, dims, jnp.float32)
    if cuts:
        values = values * block_scale(key, dims, cuts, -0.22, 0.18)
    return jnp.clip(values, -reach, reach).astype(held_as)


def setup_inputs(seed: int = 0) -> dict:
    key_of = jax.random.split(jax.random.key(seed), 22)
    return {
        "tokens": normal_values(key_of[0], (MICRO, TOKENS, D), 1.0, 6.0, ((1, 32),)),
        "memory": normal_values(key_of[1], (MICRO, CHAINS, MEMT, D), 1.0, 6.0, ((1, 2),)),
        "chain_lengths": jax.vmap(lambda own: uneven_parts(own, CH_GRP, N_BLK, MAXSEG, 2))(jax.random.split(key_of[2], MICRO * N_DP)).reshape((MICRO, N_DP, CH_GRP)).astype(jnp.int32),
        "last_fill": with_ends(jax.random.randint(key_of[3], (MICRO, N_DP, CH_GRP), 1, SEG + 1), jax.random.fold_in(key_of[3], 1), 1, SEG).astype(jnp.int32),
        "query_proj": normal_values(key_of[4], (D, D), D ** -0.5, 0.21875),
        "query_bias": normal_values(key_of[5], (D,), 0.3, 1.75),
        "key_proj": normal_values(key_of[6], (D, D), D ** -0.5, 0.21875),
        "value_proj": normal_values(key_of[7], (D, D), D ** -0.5, 0.21875),
        "value_bias": normal_values(key_of[8], (D,), 0.3, 1.75),
        "output_proj": normal_values(key_of[9], (D, D), (max(D // 256, 1)) ** -0.5, 3.5),
        "output_bias": normal_values(key_of[10], (D,), 0.3, 1.75),
        "attn_gain": jnp.clip(1.0 + 0.1 * jax.random.normal(key_of[11], (D,), jnp.float32), 0.5, 1.5).astype(jnp.bfloat16),
        "attn_shift": normal_values(key_of[12], (D,), 0.3, 1.75),
        "inner_proj": normal_values(key_of[13], (D, FF), D ** -0.5, 0.21875),
        "inner_bias": normal_values(key_of[14], (FF,), 0.3, 1.75),
        "outer_proj": normal_values(key_of[15], (FF, D), FF ** -0.5, 0.109375),
        "outer_bias": normal_values(key_of[16], (D,), 0.3, 1.75),
        "final_gain": jnp.clip(1.0 + 0.1 * jax.random.normal(key_of[17], (D,), jnp.float32), 0.5, 1.5).astype(jnp.bfloat16),
        "final_shift": normal_values(key_of[18], (D,), 0.3, 1.75),
        "token_cotangent": normal_values(key_of[19], (MICRO, TOKENS, D), 1.0, 6.0, ((1, 32),)),
        "memory_cotangent": normal_values(key_of[20], (MICRO, CHAINS, MEMT, D), 1.0, 6.0, ((1, 2),)),
    }


NEG = -1e+30
EPS = 1e-05
HIGHEST = lax.Precision.HIGHEST

@jax.custom_vjp
def low(v):
    return lax.optimization_barrier(v.astype(jnp.bfloat16)).astype(jnp.float32)

@jax.custom_vjp
def low_back(v):
    return v

def low_keep(v):
    return (low(v), None)

def low_pass(kept, grad):
    return (grad,)

def back_keep(v):
    return (v, None)

def back_low(kept, grad):
    return (low(grad),)
low.defvjp(low_keep, low_pass)
low_back.defvjp(back_keep, back_low)

def normalize(values):
    centered = values - lax.optimization_barrier(jnp.mean(values, axis=-1, keepdims=True))
    return centered * lax.rsqrt(lax.optimization_barrier(jnp.mean(centered * centered, axis=-1, keepdims=True)) + EPS)

def chain_table(lengths, fill_counts, seg_len, seg_count):
    chain_ends = jnp.cumsum(lengths).astype(jnp.int32)
    segment = jnp.arange(seg_count, dtype=jnp.int32)
    chain_of = lax.optimization_barrier(jnp.sum((chain_ends[None, :] <= segment[:, None]).astype(jnp.int32), axis=1))
    member = chain_of[:, None] == jnp.arange(lengths.shape[0], dtype=jnp.int32)[None, :]
    end_of = lax.optimization_barrier(jnp.sum(jnp.where(member, chain_ends[None, :], 0), axis=1))
    fill_of = lax.optimization_barrier(jnp.sum(jnp.where(member, fill_counts[None, :], 0), axis=1))
    used_count = jnp.where(end_of - 1 == segment, fill_of, seg_len)
    key_live = jnp.arange(seg_len, dtype=jnp.int32)[None, :] < used_count[:, None]
    return (chain_of, key_live)

def attend(query_block, chain_block, key_rows, value_rows, key_chain, key_live):
    score_scale = query_block.shape[-1] ** (-0.5)
    scores = low_back(jnp.einsum('qhd,khd->hqk', query_block, key_rows, precision=HIGHEST) * score_scale)
    key_mask = (chain_block[:, None] == key_chain[None, :]) & key_live[None, :]
    masked = jnp.where(key_mask[None], scores, NEG)
    log_total = jax.nn.logsumexp(masked, axis=-1, keepdims=True)
    weights = low(jnp.exp(masked - log_total))
    return jnp.einsum('hqk,khd->qhd', weights, value_rows, precision=HIGHEST)

def layer(row_block, params, row_chain, row_live, token_count):
    query_proj, query_bias, key_proj, value_proj, value_bias, output_proj, output_bias, attn_gain, attn_shift, inner_proj, inner_bias, outer_proj, outer_bias, final_gain, final_shift = params
    row_count = row_block.shape[0]
    queries = low_back(low(jnp.dot(row_block, query_proj, precision=HIGHEST) + query_bias)).reshape(row_count, H, HD)
    key_rows = low_back(low(jnp.dot(row_block, key_proj, precision=HIGHEST))).reshape(row_count, H, HD)
    value_rows = low_back(low(jnp.dot(row_block, value_proj, precision=HIGHEST) + value_bias)).reshape(row_count, H, HD)

    def block_attend(pair):
        query_block, chain_block = pair
        return attend(query_block, chain_block, key_rows, value_rows, row_chain, row_live)
    checked = jax.checkpoint(block_attend)
    token_attn = lax.map(checked, (queries[:token_count].reshape(token_count // SEG, SEG, H, HD), row_chain[:token_count].reshape(token_count // SEG, SEG)))
    memory_attn = checked((queries[token_count:], row_chain[token_count:]))
    attended = jnp.concatenate([token_attn.reshape(token_count, D), memory_attn.reshape(row_count - token_count, D)], 0)
    attended = low_back(low(attended))
    branch = low_back(jnp.dot(attended, output_proj, precision=HIGHEST) + output_bias)
    first = normalize(row_block + branch) * attn_gain + attn_shift
    inner = low_back(jnp.dot(low(first), inner_proj, precision=HIGHEST) + inner_bias)
    active = low(jax.nn.gelu(inner, approximate=False))
    outer = low_back(jnp.dot(active, outer_proj, precision=HIGHEST) + outer_bias)
    final = normalize(first + outer) * final_gain + final_shift
    return final * row_live[:, None].astype(jnp.float32)

def reference(tokens, memory, chain_lengths, last_fill, query_proj, query_bias, key_proj, value_proj, value_bias, output_proj, output_bias, attn_gain, attn_shift, inner_proj, inner_bias, outer_proj, outer_bias, final_gain, final_shift, token_cotangent, memory_cotangent):
    batch_count = tokens.shape[0]
    group_count = chain_lengths.shape[1]
    chain_count = chain_lengths.shape[2]
    mem_rows = memory.shape[2]
    token_count = tokens.shape[1] // group_count
    seg_count = token_count // SEG
    params = tuple((p.astype(jnp.float32) for p in (query_proj, query_bias, key_proj, value_proj, value_bias, output_proj, output_bias, attn_gain, attn_shift, inner_proj, inner_bias, outer_proj, outer_bias, final_gain, final_shift)))
    flat_count = batch_count * group_count
    inputs = (tokens.reshape(flat_count, token_count, D), memory.reshape(flat_count, chain_count * mem_rows, D), chain_lengths.reshape(flat_count, chain_count), last_fill.reshape(flat_count, chain_count), token_cotangent.reshape(flat_count, token_count, D), memory_cotangent.reshape(flat_count, chain_count * mem_rows, D))

    def one_group(grad_sums, group_inputs):
        token_part, memory_part, lengths, fill_counts, token_cot, memory_cot = group_inputs
        chain_of, key_live = chain_table(lengths, fill_counts, SEG, seg_count)
        row_chain = jnp.concatenate([jnp.repeat(chain_of, SEG), jnp.repeat(jnp.arange(chain_count, dtype=jnp.int32), mem_rows)])
        row_live = jnp.concatenate([key_live.reshape(-1), jnp.ones((chain_count * mem_rows,), dtype=jnp.bool_)])
        row_block = jnp.concatenate([token_part, memory_part], 0).astype(jnp.float32)

        def apply_layer(row_input, *weights):
            return layer(row_input, weights, row_chain, row_live, token_count)
        result, pullback = jax.vjp(apply_layer, row_block, *params)
        gradients = pullback(jnp.concatenate([token_cot, memory_cot], 0).astype(jnp.float32))
        grad_sums = tuple((a + b for a, b in zip(grad_sums, gradients[1:])))
        return (grad_sums, (result[:token_count].astype(jnp.bfloat16), result[token_count:].astype(jnp.bfloat16), gradients[0][:token_count].astype(jnp.bfloat16), gradients[0][token_count:].astype(jnp.bfloat16)))
    start_sums = tuple((jnp.zeros_like(p) for p in params))
    grad_sums, stacked = lax.scan(one_group, start_sums, inputs)
    layer_output = stacked[0].reshape(batch_count, group_count * token_count, D)
    memory_output = stacked[1].reshape(batch_count, group_count * chain_count, mem_rows, D)
    token_grad = stacked[2].reshape(batch_count, group_count * token_count, D)
    memory_grad = stacked[3].reshape(batch_count, group_count * chain_count, mem_rows, D)
    return (layer_output, memory_output, token_grad, memory_grad, grad_sums[0], grad_sums[1], grad_sums[2], grad_sums[3], grad_sums[4], grad_sums[5], grad_sums[6], grad_sums[7], grad_sums[8], grad_sums[9], grad_sums[10], grad_sums[11], grad_sums[12], grad_sums[13], grad_sums[14])
```

```python
import functools

import jax
import jax.numpy as jnp
from jax import lax
from jax.experimental import pallas as pl
from jax.experimental.pallas import tpu as pltpu
from jax.sharding import PartitionSpec as P

H = 12
HD = 64
QUAD = 256
NQUAD = 3
PAIR = 128
MEMP = 32
SEG = 512
LONG = 7
NBLK = LONG + 1
CAP = NBLK * SEG
OWN = SEG + MEMP
STAT = 24
NPIECE = 14
NEG = -1e30
SHIFT_FREE = 60.0
EPS = 1e-05
F32 = jnp.float32
BF16 = jnp.bfloat16
VMEM_LIMIT = 60 * 2**20
LAST = (((1,), (1,)), ((), ()))

M_LEN, M_ROWS, M_BLOCKS, M_SPOT, M_USED, M_MEM, M_CHAIN, M_START, M_PIECE = range(9)


def plane_moves(shift_of):
    pairs = []
    for plane in range(4):
        for place in range(4):
            target = plane + shift_of(place >> 1)
            if 0 <= target < 4:
                pairs.append((4 * plane + place, 4 * target + place))
    return pairs


UP = plane_moves(lambda side: 1)
DOWN = plane_moves(lambda side: -1)
OUTWARD = plane_moves(lambda side: 1 if side else -1)
SIDE = [(i, i ^ 2) for i in range(16)]
CORE = [(i, i ^ 1) for i in range(16)]


def move(value, pairs):
    return lax.ppermute(value, "blk", pairs)


def gather_near(value):
    side = (lax.axis_index("blk") >> 1) & 1
    below = move(value, UP)
    above = move(value, DOWN)
    beside = move(value, SIDE)
    far = move(jnp.where(side == 1, below, above), OUTWARD)
    beside_below = move(beside, UP)
    beside_above = move(beside, DOWN)
    beside_far = move(far, SIDE)
    here = [value, beside, below, above, beside_below, beside_above, beside_far]
    return here + [move(part, CORE) for part in here]


def gather_all(value):
    return [lax.all_gather(value, "blk")]


def piece_of(own, other):
    plane = (other >> 2) - (own >> 2)
    same_side = ((other >> 1) & 1) == ((own >> 1) & 1)
    on_side = jnp.where(plane == 0, 0, jnp.where(plane < 0, 2, 3))
    off_side = jnp.where(plane == 0, 1, jnp.where(plane == -1, 4, jnp.where(plane == 1, 5, 6)))
    index = jnp.where(same_side, on_side, off_side)
    return index + jnp.where((other & 1) == (own & 1), 0, LONG)


def meta_body(own_ref, lengths, fills, meta, *, batches, chains, mem_rows):
    own = own_ref[0]
    for b in range(batches):
        end = jnp.int32(0)
        length, start, fill, chain = (jnp.int32(0) for _ in range(4))
        for c in range(chains):
            begin = end
            end = end + lengths[b, c]
            inside = (begin <= own) & (own < end)
            length = jnp.where(inside, lengths[b, c], length)
            start = jnp.where(inside, begin, start)
            fill = jnp.where(inside, fills[b, c], fill)
            chain = jnp.where(inside, c, chain)
        rows = MEMP + SEG * (length - 1) + fill
        spot = own - start
        meta[b, M_LEN] = length
        meta[b, M_ROWS] = rows
        meta[b, M_BLOCKS] = (rows + SEG - 1) // SEG
        meta[b, M_SPOT] = spot
        meta[b, M_USED] = jnp.where(spot == length - 1, fill, SEG)
        meta[b, M_MEM] = jnp.int32(mem_rows)
        meta[b, M_CHAIN] = chain
        meta[b, M_START] = start
        for place in range(8):
            meta[b, M_PIECE + place] = piece_of(own, start + place)


def metas_of(own, lengths, fills, mem_rows):
    smem = pl.BlockSpec(memory_space=pltpu.SMEM)
    body = functools.partial(
        meta_body, batches=lengths.shape[0], chains=lengths.shape[1], mem_rows=mem_rows
    )
    return pl.pallas_call(
        body,
        in_specs=[smem] * 3,
        out_specs=smem,
        out_shape=jax.ShapeDtypeStruct((lengths.shape[0], 16), jnp.int32),
        name="find_chain",
    )(own.reshape(1), lengths, fills)


def load_chain(meta, pieces, view_from, view_to, sems):
    length = meta[M_LEN]
    for spot in range(LONG):
        def start(source):
            pltpu.make_async_copy(view_from(source), view_to(spot), sems.at[spot]).start()

        @pl.when(spot < length)
        def _():
            if len(pieces) == 1:
                start(pieces[0].at[meta[M_START] + spot])
                return
            for index in range(len(pieces)):
                @pl.when(meta[M_PIECE + spot] == index)
                def _():
                    start(pieces[index])


def wait_chain(meta, pieces, view_from, view_to, sems):
    length = meta[M_LEN]
    source = pieces[0].at[0] if len(pieces) == 1 else pieces[0]
    for spot in range(LONG):
        @pl.when(spot < length)
        def _():
            pltpu.make_async_copy(view_from(source), view_to(spot), sems.at[spot]).wait()


def key_bias(meta):
    column = lax.broadcasted_iota(jnp.int32, (8, CAP), 1)
    dead = (column >= meta[M_ROWS]) | ((column >= meta[M_MEM]) & (column < MEMP))
    return jnp.where(dead, NEG, 0.0).astype(F32)


def by_chunks(blocks, run):
    def four(index, carry):
        run(index * 4, 4)
        return carry

    lax.fori_loop(0, blocks // 4, four, 0)

    @pl.when((blocks & 2) != 0)
    def _():
        run((blocks // 4) * 4, 2)

    @pl.when((blocks & 1) != 0)
    def _():
        run((blocks // 2) * 2, 1)


def span_of(first, count):
    return pl.ds(pl.multiple_of(first * SEG, SEG), count * SEG)


def forward_body(meta, *refs):
    pieces, refs = refs[:-16], refs[-16:]
    mem, wq, wk, wv, bq, bv, out, lse, kc, vc, qc, rows, qown, extended, acc, sems = refs
    quad = pl.program_id(0)
    width = rows.shape[1]
    length, blocks = meta[M_LEN], meta[M_BLOCKS]
    here = lambda source: source
    there = lambda spot: rows.at[pl.ds(MEMP + SEG * spot, SEG)]

    @pl.when(quad == 0)
    def _():
        load_chain(meta, pieces, here, there, sems)
        rows[0:MEMP, :] = mem[...]
        lse[...] = jnp.zeros_like(lse)

        @pl.when(blocks > length)
        def _():
            place = pl.multiple_of(MEMP + SEG * length, MEMP)
            rows[pl.ds(place, SEG - MEMP), :] = jnp.zeros((SEG - MEMP, width), BF16)

        wait_chain(meta, pieces, here, there, sems)

    def longest(values):
        halves = [
            jnp.max(jnp.sum(jnp.square(values[:, p : p + PAIR]), axis=1, keepdims=True))
            for p in range(0, QUAD, PAIR)
        ]
        return jnp.maximum(*halves)

    def project(start, count):
        span = pl.ds(pl.multiple_of(start, MEMP), count)
        part = rows[span, :]
        row = start + lax.broadcasted_iota(jnp.int32, (count, QUAD), 0)
        alive = (row < meta[M_ROWS]) & ((row < meta[M_MEM]) | (row >= MEMP))
        lower = (lax.broadcasted_iota(jnp.int32, (count, QUAD), 1) % PAIR) < HD
        key = jnp.dot(part, wk[...], preferred_element_type=F32)
        kc[span, :] = key.astype(BF16)
        value = jnp.dot(part, wv[...], preferred_element_type=F32) + bv[...].astype(F32)
        vc[span, :] = value.astype(BF16)
        value = jnp.where(alive, value, 0.0)
        one = jnp.where(alive, 1.0, 0.0)
        extended[0, span, :] = jnp.where(lower, value, one).astype(BF16)
        extended[1, span, :] = jnp.where(lower, one, value).astype(BF16)
        query = jnp.dot(part, wq[...], preferred_element_type=F32) + bq[...].astype(F32)
        query = query.astype(BF16) * jnp.asarray(HD**-0.5, BF16)
        qc[span, :] = query
        return longest(key)

    def project_block(block, top):
        return jnp.maximum(top, project(block * SEG, SEG))

    key_top = lax.fori_loop(0, blocks, project_block, jnp.float32(0.0))

    @pl.when(blocks == length)
    def _():
        project(length * SEG, MEMP)

    place = pl.multiple_of(MEMP + SEG * meta[M_SPOT], MEMP)
    qown[0:SEG, :] = qc[pl.ds(place, SEG), :]
    qown[SEG:OWN, :] = qc[0:MEMP, :]
    near = longest(qown[...].astype(F32)) * key_top <= SHIFT_FREE**2

    def head(index, carry):
        cols = pl.ds(pl.multiple_of((index // 2) * PAIR, PAIR), PAIR)
        half = index % 2
        lane = lax.broadcasted_iota(jnp.int32, (OWN, PAIR), 1)
        mine = (lane // HD) == half
        query = qown[:, cols]
        query = jnp.where(mine, query, jnp.zeros_like(query))
        acc[...] = jnp.zeros_like(acc)
        number = lane == quad * 4 + index

        def score(span):
            return lax.dot_general(query, kc[span, cols], LAST, preferred_element_type=F32)

        def gather(span, terms):
            values = extended[half, span, cols]
            return jnp.dot(terms.astype(BF16), values, preferred_element_type=F32)

        @pl.when(near)
        def _():
            def run(first, count):
                span = span_of(first, count)
                acc[...] += gather(span, jnp.exp(score(span)))

            by_chunks(blocks, run)
            lse[...] = jnp.where(number, 0.0, lse[...])

        @pl.when(jnp.logical_not(near))
        def _():
            def run(block, top):
                span = span_of(block, 1)
                column = block * SEG + lax.broadcasted_iota(jnp.int32, (OWN, SEG), 1)
                dead = (column >= meta[M_ROWS]) | ((column >= meta[M_MEM]) & (column < MEMP))
                scores = jnp.where(dead, NEG, score(span))
                new = jnp.maximum(top, jnp.max(scores, axis=1, keepdims=True))
                acc[...] = acc[...] * jnp.exp(top - new) + gather(span, jnp.exp(scores - new))
                return new

            top = lax.fori_loop(0, blocks, run, jnp.full((OWN, 1), NEG, F32))
            lse[...] = jnp.where(number, top, lse[...])

        sums = acc[...]
        total = jnp.where(mine, pltpu.roll(sums, HD, 1), sums)
        out[:, cols] = jnp.where(mine, sums * (1.0 / total), out[:, cols])
        lse[...] += jnp.where(number, jnp.log(total), 0.0)
        return carry

    lax.fori_loop(0, 4, head, 0)


def attend_forward(meta, pieces, mem, weights):
    wq, bq, wk, wv, bv = weights
    width = wq.shape[0]
    whole = lambda shape: pl.BlockSpec(shape, lambda quad, meta: (0,) * len(shape))
    column = lambda count: pl.BlockSpec((count, QUAD), lambda quad, meta: (0, quad))
    return pl.pallas_call(
        forward_body,
        grid_spec=pltpu.PrefetchScalarGridSpec(
            num_scalar_prefetch=1,
            grid=(NQUAD,),
            in_specs=[pl.BlockSpec(memory_space=pl.ANY)] * len(pieces)
            + [whole((MEMP, width))]
            + [column(width)] * 3
            + [column(1)] * 2,
            out_specs=[column(OWN), whole((OWN, PAIR))] + [column(CAP)] * 3,
            scratch_shapes=[
                pltpu.VMEM((CAP, width), BF16),
                pltpu.VMEM((OWN, QUAD), BF16),
                pltpu.VMEM((2, CAP, QUAD), BF16),
                pltpu.VMEM((OWN, PAIR), F32),
                pltpu.SemaphoreType.DMA((LONG,)),
            ],
        ),
        out_shape=[
            jax.ShapeDtypeStruct((OWN, width), F32),
            jax.ShapeDtypeStruct((OWN, PAIR), F32),
        ]
        + [jax.ShapeDtypeStruct((CAP, width), BF16)] * 3,
        compiler_params=pltpu.CompilerParams(vmem_limit_bytes=VMEM_LIMIT),
        cost_estimate=pl.CostEstimate(
            flops=40_000_000_000, bytes_accessed=30_000_000, transcendentals=23_000_000
        ),
        name="attend_forward",
    )(meta, *pieces, mem, wq, wk, wv, bq.reshape(1, -1), bv.reshape(1, -1))


def backward_body(meta, *refs):
    pieces, refs = refs[:-23], refs[-23:]
    (
        kc, vc, qc, mem_grad, mem_stats, own_lse, own_delta,
        dq, dk, dv,
        doc, stats, chain_stats, qown, kown, vown, down, bias, qacc, kacc, vacc, sems, stat_sems,
    ) = refs
    quad = pl.program_id(0)
    length = meta[M_LEN]

    @pl.when(quad == 0)
    def _():
        rows_from = lambda index: lambda ref: ref.at[0:SEG, pl.ds(index * QUAD, QUAD)]
        rows_to = lambda index: lambda spot: doc.at[index, pl.ds(MEMP + SEG * spot, SEG)]
        stat_from = lambda ref: ref.at[SEG : SEG + 2 * STAT, 0:SEG]
        stat_to = lambda spot: stats.at[spot]
        load_chain(meta, pieces, stat_from, stat_to, stat_sems)
        for index in range(NQUAD):
            load_chain(meta, pieces, rows_from(index), rows_to(index), sems.at[index])
        bias[...] = key_bias(meta)
        for index in range(NQUAD):
            doc[index, 0:MEMP, :] = mem_grad[:, index * QUAD : (index + 1) * QUAD]

            @pl.when(meta[M_BLOCKS] > length)
            def _():
                place = pl.multiple_of(MEMP + SEG * length, MEMP)
                doc[index, pl.ds(place, SEG - MEMP), :] = jnp.zeros((SEG - MEMP, QUAD), BF16)

        wait_chain(meta, pieces, stat_from, stat_to, stat_sems)
        for spot in range(NBLK):
            span = slice(SEG * spot, SEG * (spot + 1))
            if spot == LONG:
                chain_stats[:, span] = jnp.zeros((STAT, SEG), F32)
                continue

            @pl.when(spot < length)
            def _():
                pair = stats[spot].astype(F32)
                chain_stats[:, span] = pair[0:STAT] + pair[STAT : 2 * STAT]

            @pl.when(spot >= length)
            def _():
                chain_stats[:, span] = jnp.zeros((STAT, SEG), F32)

        moved = pltpu.roll(chain_stats[...], MEMP, 1)
        column = lax.broadcasted_iota(jnp.int32, (STAT, CAP), 1)
        entry = lax.broadcasted_iota(jnp.int32, (STAT, CAP), 0)
        beyond = jnp.where(entry < H, -NEG, 0.0)
        chain_stats[...] = jnp.where(column < MEMP + SEG * length, moved, beyond)
        lane = lax.broadcasted_iota(jnp.int32, (STAT, PAIR), 1)
        chain_stats[:, 0:PAIR] = jnp.where(lane < MEMP, mem_stats[...], chain_stats[:, 0:PAIR])
        for index in range(NQUAD):
            wait_chain(meta, pieces, rows_from(index), rows_to(index), sems.at[index])

    place = pl.multiple_of(MEMP + SEG * meta[M_SPOT], MEMP)
    for own, chain in ((qown, qc), (kown, kc), (vown, vc), (down, doc.at[quad])):
        own[0:SEG, :] = chain[pl.ds(place, SEG), :]
        own[SEG:OWN, :] = chain[0:MEMP, :]

    def head(index, carry):
        cols = pl.ds(pl.multiple_of((index // 2) * PAIR, PAIR), PAIR)
        number = quad * 4 + index
        lane = lax.broadcasted_iota(jnp.int32, (OWN, PAIR), 1)
        mine = (lane // HD) == (index % 2)
        masked = lambda ref: jnp.where(mine, ref[:, cols], jnp.zeros((OWN, PAIR), BF16))
        query, key, value, grad = masked(qown), masked(kown), masked(vown), masked(down)
        pick = lambda ref: jnp.sum(jnp.where(lane == number, ref[...], 0.0), axis=1, keepdims=True)
        log_total, delta = pick(own_lse), pick(own_delta)
        for acc in (qacc, kacc, vacc):
            acc[...] = jnp.zeros_like(acc)

        def run(first, count):
            span = span_of(first, count)
            keys, values = kc[span, cols], vc[span, cols]
            scores = lax.dot_general(query, keys, LAST, preferred_element_type=F32)
            weights = jnp.exp(scores + bias[0:1, span] - log_total)
            weight_grad = lax.dot_general(grad, values, LAST, preferred_element_type=F32)
            score_grad = (weights * (weight_grad - delta)).astype(BF16)
            qacc[...] += jnp.dot(score_grad, keys, preferred_element_type=F32)

            queries, grads = qc[span, cols], doc[quad, span, cols]
            scores = lax.dot_general(key, queries, LAST, preferred_element_type=F32)
            weights = jnp.exp(scores - chain_stats[pl.ds(number, 1), span])
            weight_grad = lax.dot_general(value, grads, LAST, preferred_element_type=F32)
            score_grad = (
                weights * (weight_grad - chain_stats[pl.ds(H + number, 1), span])
            ).astype(BF16)
            vacc[...] += jnp.dot(weights.astype(BF16), grads, preferred_element_type=F32)
            kacc[...] += jnp.dot(score_grad, queries, preferred_element_type=F32)

        by_chunks(meta[M_BLOCKS], run)
        row = lax.broadcasted_iota(jnp.int32, (OWN, PAIR), 0)
        alive = (row < meta[M_USED]) | ((row >= SEG) & (row < SEG + meta[M_MEM]))
        query_sum = qacc[...] * (HD**-0.5)
        key_sum = jnp.where(alive, kacc[...], 0.0)
        value_sum = jnp.where(alive, vacc[...], 0.0)
        for ref, sums in ((dq, query_sum), (dk, key_sum), (dv, value_sum)):
            ref[:, cols] = jnp.where(mine, sums.astype(BF16), ref[:, cols])
        return carry

    lax.fori_loop(0, 4, head, 0)


def attend_backward(meta, pieces, chain, mem_grad, mem_stats, own_lse, own_delta):
    width = mem_grad.shape[1]
    whole = lambda shape: pl.BlockSpec(shape, lambda quad, meta: (0,) * len(shape))
    column = lambda count: pl.BlockSpec((count, QUAD), lambda quad, meta: (0, quad))
    return pl.pallas_call(
        backward_body,
        grid_spec=pltpu.PrefetchScalarGridSpec(
            num_scalar_prefetch=1,
            grid=(NQUAD,),
            in_specs=[pl.BlockSpec(memory_space=pl.ANY)] * len(pieces)
            + [column(CAP)] * 3
            + [whole((MEMP, width)), whole((STAT, PAIR)), whole((OWN, PAIR)), whole((OWN, PAIR))],
            out_specs=[column(OWN)] * 3,
            scratch_shapes=[
                pltpu.VMEM((NQUAD, CAP, QUAD), BF16),
                pltpu.VMEM((LONG, 2 * STAT, SEG), BF16),
                pltpu.VMEM((STAT, CAP), F32),
            ]
            + [pltpu.VMEM((OWN, QUAD), BF16)] * 4
            + [
                pltpu.VMEM((8, CAP), F32),
                pltpu.VMEM((OWN, PAIR), F32),
                pltpu.VMEM((OWN, PAIR), F32),
                pltpu.VMEM((OWN, PAIR), F32),
                pltpu.SemaphoreType.DMA((NQUAD, LONG)),
                pltpu.SemaphoreType.DMA((LONG,)),
            ],
        ),
        out_shape=[jax.ShapeDtypeStruct((OWN, width), BF16)] * 3,
        compiler_params=pltpu.CompilerParams(vmem_limit_bytes=VMEM_LIMIT),
        cost_estimate=pl.CostEstimate(
            flops=90_000_000_000, bytes_accessed=30_000_000, transcendentals=46_000_000
        ),
        name="attend_backward",
    )(meta, *pieces, *chain, mem_grad, mem_stats, own_lse, own_delta)


def normalize(values):
    centered = values - jnp.mean(values, axis=-1, keepdims=True)
    scale = lax.rsqrt(jnp.mean(centered * centered, axis=-1, keepdims=True) + EPS)
    return centered * scale, scale


def norm_back(normed, scale, upstream):
    mean = jnp.mean(upstream, axis=-1, keepdims=True)
    along = jnp.mean(upstream * normed, axis=-1, keepdims=True)
    return scale * (upstream - mean - normed * along)


def gelu_both(values):
    cdf = 0.5 * (1.0 + lax.erf(values * (2.0**-0.5)))
    density = jnp.exp(-0.5 * values * values) * 0.3989422804014327
    return values * cdf, cdf + values * density


def times(left, right):
    return jnp.dot(left, right, preferred_element_type=F32)


def times_turned(left, right):
    return lax.dot_general(left, right, LAST, preferred_element_type=F32)


def weight_grad(left, right):
    return lax.dot_general(left, right, (((0,), (0,)), ((), ())), preferred_element_type=F32)


def sum_over(value, steps):
    taken = []
    for axis, bit in steps:
        count = lax.axis_size(axis)
        pairs = [(i, i ^ bit) for i in range(count)]
        half = value.shape[0] // 2
        upper = (lax.axis_index(axis) // bit) % 2
        keep = lax.dynamic_slice_in_dim(value, upper * half, half)
        send = lax.dynamic_slice_in_dim(value, (1 - upper) * half, half)
        got = lax.ppermute(send, axis, pairs)
        value = (keep.astype(F32) + got.astype(F32)).astype(value.dtype)
        taken.append((axis, pairs, upper))
    for axis, pairs, upper in reversed(taken):
        got = lax.ppermute(value, axis, pairs)
        value = jnp.where(
            upper == 0,
            jnp.concatenate([value, got], 0),
            jnp.concatenate([got, value], 0),
        )
    return value


def spread(value):
    for bit in (1, 2, 4, 8):
        value = value + lax.ppermute(value, "blk", [(i, i ^ bit) for i in range(16)])
    return value


def local(
    tokens, memory, chain_lengths, last_fill,
    query_proj, query_bias, key_proj, value_proj, value_bias, output_proj, output_bias,
    attn_gain, attn_shift, inner_proj, inner_bias, outer_proj, outer_bias,
    final_gain, final_shift, token_cotangent, memory_cotangent,
):
    own = lax.axis_index("blk").astype(jnp.int32)
    batches, _, width = tokens.shape
    chains, mem_rows = memory.shape[1:3]
    pad_mem = ((0, MEMP - mem_rows), (0, 0))
    head_of = (jnp.arange(width)[:, None] // HD == jnp.arange(PAIR)[None, :]).astype(F32)
    row = jnp.arange(OWN)

    metas = metas_of(own, chain_lengths[:, 0], last_fill[:, 0], mem_rows)
    pieces = [gather_near(tokens[0])] + [gather_all(tokens[b]) for b in range(1, batches)]

    states, token_outs, memory_outs = [], [], []
    for b in range(batches):
        meta = metas[b]
        chain, spot, used = meta[M_CHAIN], meta[M_SPOT], meta[M_USED]
        mem = jnp.pad(lax.dynamic_index_in_dim(memory[b], chain, keepdims=False), pad_mem)
        attended, lse, *chain_rows = attend_forward(
            meta, pieces[b], mem, (query_proj, query_bias, key_proj, value_proj, value_bias)
        )
        rows = jnp.concatenate([tokens[b], mem], 0)
        live = ((row < used) | ((row >= SEG) & (row < SEG + mem_rows))).astype(F32)[:, None]
        lead = (spot == 0).astype(F32)
        counted = jnp.where(row < SEG, 1.0, lead).astype(F32)[:, None]
        counted_low = counted.astype(BF16)
        attended_low = attended.astype(BF16)
        first_sum = rows.astype(F32) + times(attended_low, output_proj) + output_bias
        first_norm, first_scale = normalize(first_sum)
        first = first_norm * attn_gain + attn_shift
        first_low = first.astype(BF16)
        inner = times(first_low, inner_proj) + inner_bias
        active, slope = gelu_both(inner)
        active_low = active.astype(BF16)
        second_sum = first + times(active_low, outer_proj) + outer_bias
        final_norm, final_scale = normalize(second_sum)
        final = ((final_norm * final_gain + final_shift) * live).astype(BF16)
        token_outs.append(final[:SEG])
        hot = ((jnp.arange(chains) == chain) & (spot == 0))[:, None, None]
        to_all = lambda value, hot=hot: jnp.where(hot, value[SEG : SEG + mem_rows][None], 0).astype(BF16)
        memory_outs.append(to_all(final))

        mem_cot = jnp.pad(
            lax.dynamic_index_in_dim(memory_cotangent[b], chain, keepdims=False), pad_mem
        )
        cotangent = jnp.concatenate([token_cotangent[b], mem_cot], 0).astype(F32) * live
        weighted = cotangent * counted
        grad_final_gain = jnp.sum(weighted * final_norm, 0)
        grad_final_shift = jnp.sum(weighted, 0)
        second_grad = norm_back(final_norm, final_scale, cotangent * final_gain)
        outer_grad = second_grad.astype(BF16)
        outer_counted = outer_grad * counted_low
        inner_grad = (times_turned(outer_grad, outer_proj) * slope).astype(BF16)
        inner_counted = inner_grad * counted_low
        first_grad = second_grad + times_turned(inner_grad, inner_proj)
        weighted = first_grad * counted
        grad_attn_gain = jnp.sum(weighted * first_norm, 0)
        grad_attn_shift = jnp.sum(weighted, 0)
        res_grad = norm_back(first_norm, first_scale, first_grad * attn_gain)
        branch_grad = res_grad.astype(BF16)
        branch_counted = branch_grad * counted_low
        attended_grad = times_turned(branch_grad, output_proj).astype(BF16)
        delta = jnp.dot(
            attended_grad.astype(F32) * attended, head_of, precision=lax.Precision.HIGHEST
        )
        stats = jnp.concatenate([lse[:, :H], delta[:, :H]], 1).T
        high = lax.reduce_precision(stats[:, :SEG], 8, 7)
        both = jnp.concatenate([high, stats[:, :SEG] - high], 0).astype(BF16)
        payload = jnp.concatenate(
            [attended_grad[:SEG], jnp.pad(both, ((0, 0), (0, width - SEG)))], 0
        )
        states.append(
            dict(
                meta=meta, rows=rows, counted=counted_low, chain_rows=chain_rows, lse=lse,
                delta=delta, payload=gather_all(payload), mem_grad=attended_grad[SEG:],
                mem_stats=jnp.pad(stats[:, SEG:], ((0, 0), (0, PAIR - MEMP))),
                res_grad=res_grad, to_all=to_all,
                attended_low=attended_low, branch=branch_counted, first_low=first_low,
                inner=inner_counted, active=active_low, outer=outer_counted,
                small=[
                    jnp.sum(branch_counted.astype(F32), 0), grad_attn_gain, grad_attn_shift,
                    jnp.sum(inner_counted.astype(F32), 0), jnp.sum(outer_counted.astype(F32), 0),
                    grad_final_gain, grad_final_shift,
                ],
            )
        )

    def over_batches(left, right):
        return weight_grad(
            jnp.concatenate([s[left] for s in states], 0),
            jnp.concatenate([s[right] for s in states], 0),
        ).astype(BF16)

    small = jnp.concatenate([sum(s["small"][i] for s in states) for i in range(7)])
    early = (
        over_batches("first_low", "inner"),
        over_batches("active", "outer"),
        jnp.concatenate(
            [over_batches("attended_low", "branch"), small.astype(BF16).reshape(-1, width)], 0
        ),
    )
    grad_inner, grad_outer, grad_output = lax.psum(early, ("dp", "blk"))
    small = grad_output[width:].reshape(-1)
    grad_output = grad_output[:width]

    memory_out = spread(jnp.stack(memory_outs))

    token_grads, memory_grads = [], []
    for s in states:
        s["dq"], s["dk"], s["dv"] = attend_backward(
            s["meta"], s["payload"], s["chain_rows"], s["mem_grad"], s["mem_stats"],
            s["lse"], s["delta"],
        )
        for name in ("dq", "dk", "dv"):
            s[name + "_counted"] = s[name] * s["counted"]

    dp = lax.axis_size("dp")
    on_dp = [("dp", 1 << i) for i in range(dp.bit_length() - 1)]
    on_core, on_side, on_plane = [("blk", 1)], [("blk", 2)], [("blk", 4), ("blk", 8)]
    orders = (
        on_core + on_dp + on_side + on_plane,
        on_core + on_side + on_plane + on_dp,
        on_core + on_plane + on_dp + on_side,
    )
    grad_query, grad_key, grad_value = (
        sum_over(over_batches("rows", name + "_counted"), steps)
        for name, steps in zip(("dq", "dk", "dv"), orders)
    )
    biases = jnp.concatenate(
        [
            sum(jnp.sum(s[name + "_counted"].astype(F32), 0) for s in states)
            for name in ("dq", "dv")
        ]
    )
    for steps in (on_core, on_dp, on_side, on_plane):
        for axis, bit in steps:
            pairs = [(i, i ^ bit) for i in range(lax.axis_size(axis))]
            biases = biases + lax.ppermute(biases, axis, pairs)

    for s in states:
        grad = (
            s["res_grad"]
            + times_turned(s["dq"], query_proj)
            + times_turned(s["dk"], key_proj)
            + times_turned(s["dv"], value_proj)
        )
        token_grads.append(grad[:SEG].astype(BF16))
        memory_grads.append(s["to_all"](grad))
    memory_grad = spread(jnp.stack(memory_grads))

    wide = lambda value: value.astype(F32)
    cut = lambda first, count: wide(small[first : first + count])
    inner_width = inner_proj.shape[1]
    return (
        jnp.stack(token_outs),
        memory_out,
        jnp.stack(token_grads),
        memory_grad,
        wide(grad_query),
        biases[:width],
        wide(grad_key),
        wide(grad_value),
        biases[width:],
        wide(grad_output),
        cut(0, width),
        cut(width, width),
        cut(2 * width, width),
        wide(grad_inner),
        cut(3 * width, inner_width),
        wide(grad_outer),
        cut(3 * width + inner_width, width),
        cut(4 * width + inner_width, width),
        cut(5 * width + inner_width, width),
    )


def solution(mesh):
    row_spec = P(None, ("dp", "blk"), None)
    mem_spec = P(None, "dp", None, None)
    int_spec = P(None, "dp", None)
    in_specs = (row_spec, mem_spec, int_spec, int_spec) + (P(),) * 15 + (row_spec, mem_spec)
    out_specs = (row_spec, mem_spec, row_spec, mem_spec) + (P(),) * 15
    return jax.shard_map(local, mesh=mesh, in_specs=in_specs, out_specs=out_specs, check_vma=False)
```

```python
import functools

import jax
import jax.numpy as jnp
from jax import lax
from jax.experimental import pallas as pl
from jax.experimental.pallas import tpu as pltpu
from jax.sharding import PartitionSpec as P

H = 12
HD = 64
QUAD = 256
NQUAD = 3
PAIR = 128
MEMP = 32
SEG = 512
LONG = 7
NBLK = LONG + 1
CAP = NBLK * SEG
OWN = SEG + MEMP
STAT = 24
BACK_COST = 10_000_000_000
LATE_ROWS = 256
NPIECE = 14
ROWS = 32
COLS = 512
NEG = -1e30
SHIFT_FREE = 60.0
EPS = 1e-05
F32 = jnp.float32
BF16 = jnp.bfloat16
VMEM_LIMIT = 60 * 2**20
LAST = (((1,), (1,)), ((), ()))

M_LEN, M_ROWS, M_BLOCKS, M_SPOT, M_USED, M_MEM, M_CHAIN, M_START, M_PIECE = range(9)


def plane_moves(shift_of):
    pairs = []
    for plane in range(4):
        for place in range(4):
            target = plane + shift_of(place >> 1)
            if 0 <= target < 4:
                pairs.append((4 * plane + place, 4 * target + place))
    return pairs


UP = plane_moves(lambda side: 1)
DOWN = plane_moves(lambda side: -1)
FAR = [
    (4 * plane + place, 4 * target + (place ^ 2))
    for plane in range(4)
    for place in range(4)
    for target in [plane + (2 if place >> 1 else -2)]
    if 0 <= target < 4
]
SIDE = [(i, i ^ 2) for i in range(16)]
CORE = [(i, i ^ 1) for i in range(16)]


def move(value, pairs):
    return lax.ppermute(value, "blk", pairs)


def gather_near(value, hold=lambda stage, parts: parts):
    below, above, beside, far = (move(value, pairs) for pairs in (UP, DOWN, SIDE, FAR))
    below, above, beside, far = hold(0, [below, above, beside, far])
    moved = [move(beside, UP), move(beside, DOWN)]
    first = [move(part, CORE) for part in (value, beside, below, above, far)]
    moved_and_first = hold(1, moved + first)
    moved, first = moved_and_first[:2], moved_and_first[2:]
    second = hold(2, [move(part, CORE) for part in moved])
    return [value, beside, below, above, *moved, far] + first[:4] + second + first[4:]


def gather_all(value):
    return [lax.all_gather(value, "blk")]


def piece_of(own, other):
    plane = (other >> 2) - (own >> 2)
    same_side = ((other >> 1) & 1) == ((own >> 1) & 1)
    on_side = jnp.where(plane == 0, 0, jnp.where(plane < 0, 2, 3))
    off_side = jnp.where(plane == 0, 1, jnp.where(plane == -1, 4, jnp.where(plane == 1, 5, 6)))
    index = jnp.where(same_side, on_side, off_side)
    return index + jnp.where((other & 1) == (own & 1), 0, LONG)


def meta_body(own_ref, lengths, fills, meta, *, batches, chains, mem_rows):
    own = own_ref[0]
    for b in range(batches):
        end = jnp.int32(0)
        length, start, fill, chain = (jnp.int32(0) for _ in range(4))
        for c in range(chains):
            begin = end
            end = end + lengths[b, c]
            inside = (begin <= own) & (own < end)
            length = jnp.where(inside, lengths[b, c], length)
            start = jnp.where(inside, begin, start)
            fill = jnp.where(inside, fills[b, c], fill)
            chain = jnp.where(inside, c, chain)
        rows = MEMP + SEG * (length - 1) + fill
        spot = own - start
        meta[b, M_LEN] = length
        meta[b, M_ROWS] = rows
        meta[b, M_BLOCKS] = (rows + SEG - 1) // SEG
        meta[b, M_SPOT] = spot
        meta[b, M_USED] = jnp.where(spot == length - 1, fill, SEG)
        meta[b, M_MEM] = jnp.int32(mem_rows)
        meta[b, M_CHAIN] = chain
        meta[b, M_START] = start
        for place in range(8):
            meta[b, M_PIECE + place] = piece_of(own, start + place)


def metas_of(own, lengths, fills, mem_rows):
    smem = pl.BlockSpec(memory_space=pltpu.SMEM)
    body = functools.partial(
        meta_body, batches=lengths.shape[0], chains=lengths.shape[1], mem_rows=mem_rows
    )
    return pl.pallas_call(
        body,
        in_specs=[smem] * 3,
        out_specs=smem,
        out_shape=jax.ShapeDtypeStruct((lengths.shape[0], 16), jnp.int32),
        name="find_chain",
    )(own.reshape(1), lengths, fills)


def load_chain(meta, pieces, view_from, view_to, sems):
    length = meta[M_LEN]
    for spot in range(LONG):
        def start(source):
            pltpu.make_async_copy(view_from(source), view_to(spot), sems.at[spot]).start()

        @pl.when(spot < length)
        def _():
            if len(pieces) == 1:
                start(pieces[0].at[meta[M_START] + spot])
                return
            for index in range(len(pieces)):
                @pl.when(meta[M_PIECE + spot] == index)
                def _():
                    start(pieces[index])


def wait_chain(meta, pieces, view_from, view_to, sems):
    length = meta[M_LEN]
    source = pieces[0].at[0] if len(pieces) == 1 else pieces[0]
    for spot in range(LONG):
        @pl.when(spot < length)
        def _():
            pltpu.make_async_copy(view_from(source), view_to(spot), sems.at[spot]).wait()


def key_bias(meta):
    column = lax.broadcasted_iota(jnp.int32, (8, CAP), 1)
    dead = (column >= meta[M_ROWS]) | ((column >= meta[M_MEM]) & (column < MEMP))
    return jnp.where(dead, NEG, 0.0).astype(F32)


def by_chunks(blocks, run):
    def four(index, carry):
        run(index * 4, 4)
        return carry

    lax.fori_loop(0, blocks // 4, four, 0)
    for count in (1, 2, 3):
        @pl.when(blocks % 4 == count)
        def _():
            run((blocks // 4) * 4, count)


def span_of(first, count):
    return pl.ds(pl.multiple_of(first * SEG, SEG), count * SEG)


def forward_body(meta, *refs):
    pieces, refs = refs[:-16], refs[-16:]
    mem, wq, wk, wv, bq, bv, out, lse, kc, vc, qc, rows, qown, extended, acc, sems = refs
    quad = pl.program_id(0)
    width = rows.shape[1]
    length, blocks = meta[M_LEN], meta[M_BLOCKS]
    here = lambda source: source
    there = lambda spot: rows.at[pl.ds(MEMP + SEG * spot, SEG)]

    @pl.when(quad == 0)
    def _():
        load_chain(meta, pieces, here, there, sems)
        rows[0:MEMP, :] = mem[meta[M_CHAIN]]
        lse[...] = jnp.zeros_like(lse)

        @pl.when(blocks > length)
        def _():
            place = pl.multiple_of(MEMP + SEG * length, MEMP)
            rows[pl.ds(place, SEG - MEMP), :] = jnp.zeros((SEG - MEMP, width), BF16)

        wait_chain(meta, pieces, here, there, sems)

    def longest(values):
        halves = [
            jnp.max(jnp.sum(jnp.square(values[:, p : p + PAIR]), axis=1, keepdims=True))
            for p in range(0, QUAD, PAIR)
        ]
        return jnp.maximum(*halves)

    def project(start, count):
        span = pl.ds(pl.multiple_of(start, MEMP), count)
        part = rows[span, :]
        row = start + lax.broadcasted_iota(jnp.int32, (count, QUAD), 0)
        alive = (row < meta[M_ROWS]) & ((row < meta[M_MEM]) | (row >= MEMP))
        lower = (lax.broadcasted_iota(jnp.int32, (count, QUAD), 1) % PAIR) < HD
        key = jnp.dot(part, wk[...], preferred_element_type=F32)
        kc[span, :] = key.astype(BF16)
        value = jnp.dot(part, wv[...], preferred_element_type=F32) + bv[...].astype(F32)
        vc[span, :] = value.astype(BF16)
        value = jnp.where(alive, value, 0.0)
        one = jnp.where(alive, 1.0, 0.0)
        extended[0, span, :] = jnp.where(lower, value, one).astype(BF16)
        extended[1, span, :] = jnp.where(lower, one, value).astype(BF16)
        query = jnp.dot(part, wq[...], preferred_element_type=F32) + bq[...].astype(F32)
        query = query.astype(BF16) * jnp.asarray(HD**-0.5, BF16)
        qc[span, :] = query
        return longest(key)

    def project_block(block, top):
        return jnp.maximum(top, project(block * SEG, SEG))

    key_top = lax.fori_loop(0, blocks, project_block, jnp.float32(0.0))

    @pl.when(blocks == length)
    def _():
        project(length * SEG, MEMP)

    place = pl.multiple_of(MEMP + SEG * meta[M_SPOT], MEMP)
    qown[0:SEG, :] = qc[pl.ds(place, SEG), :]
    qown[SEG:OWN, :] = qc[0:MEMP, :]
    near = longest(qown[...].astype(F32)) * key_top <= SHIFT_FREE**2

    def head(index, carry):
        cols = pl.ds(pl.multiple_of((index // 2) * PAIR, PAIR), PAIR)
        half = index % 2
        lane = lax.broadcasted_iota(jnp.int32, (OWN, PAIR), 1)
        mine = (lane // HD) == half
        query = qown[:, cols]
        query = jnp.where(mine, query, jnp.zeros_like(query))
        acc[...] = jnp.zeros_like(acc)
        number = lane == quad * 4 + index

        def score(span):
            return lax.dot_general(query, kc[span, cols], LAST, preferred_element_type=F32)

        def gather(span, terms):
            values = extended[half, span, cols]
            return jnp.dot(terms.astype(BF16), values, preferred_element_type=F32)

        @pl.when(near)
        def _():
            def run(first, count):
                span = span_of(first, count)
                acc[...] += gather(span, jnp.exp(score(span)))

            by_chunks(blocks, run)
            lse[...] = jnp.where(number, 0.0, lse[...])

        @pl.when(jnp.logical_not(near))
        def _():
            def run(block, top):
                span = span_of(block, 1)
                column = block * SEG + lax.broadcasted_iota(jnp.int32, (OWN, SEG), 1)
                dead = (column >= meta[M_ROWS]) | ((column >= meta[M_MEM]) & (column < MEMP))
                scores = jnp.where(dead, NEG, score(span))
                new = jnp.maximum(top, jnp.max(scores, axis=1, keepdims=True))
                acc[...] = acc[...] * jnp.exp(top - new) + gather(span, jnp.exp(scores - new))
                return new

            top = lax.fori_loop(0, blocks, run, jnp.full((OWN, 1), NEG, F32))
            lse[...] = jnp.where(number, top, lse[...])

        sums = acc[...]
        total = jnp.where(mine, pltpu.roll(sums, HD, 1), sums)
        out[:, cols] = jnp.where(mine, sums * (1.0 / total), out[:, cols])
        lse[...] += jnp.where(number, jnp.log(total), 0.0)
        return carry

    lax.fori_loop(0, 4, head, 0)


def attend_forward(meta, pieces, mem, weights):
    wq, bq, wk, wv, bv = weights
    width = wq.shape[0]
    whole = lambda shape: pl.BlockSpec(shape, lambda quad, meta: (0,) * len(shape))
    column = lambda count: pl.BlockSpec((count, QUAD), lambda quad, meta: (0, quad))
    return pl.pallas_call(
        forward_body,
        grid_spec=pltpu.PrefetchScalarGridSpec(
            num_scalar_prefetch=1,
            grid=(NQUAD,),
            in_specs=[pl.BlockSpec(memory_space=pl.ANY)] * len(pieces)
            + [whole((mem.shape[0], MEMP, width))]
            + [column(width)] * 3
            + [column(1)] * 2,
            out_specs=[column(OWN), whole((OWN, PAIR))] + [column(CAP)] * 3,
            scratch_shapes=[
                pltpu.VMEM((CAP, width), BF16),
                pltpu.VMEM((OWN, QUAD), BF16),
                pltpu.VMEM((2, CAP, QUAD), BF16),
                pltpu.VMEM((OWN, PAIR), F32),
                pltpu.SemaphoreType.DMA((LONG,)),
            ],
        ),
        out_shape=[
            jax.ShapeDtypeStruct((OWN, width), F32),
            jax.ShapeDtypeStruct((OWN, PAIR), F32),
        ]
        + [jax.ShapeDtypeStruct((CAP, width), BF16)] * 3,
        compiler_params=pltpu.CompilerParams(vmem_limit_bytes=VMEM_LIMIT),
        cost_estimate=pl.CostEstimate(
            flops=40_000_000_000, bytes_accessed=30_000_000, transcendentals=23_000_000
        ),
        name="attend_forward",
    )(meta, *pieces, mem, wq, wk, wv, bq.reshape(1, -1), bv.reshape(1, -1))


def backward_body(start, count, meta, *refs):
    pieces, refs = refs[:-22], refs[-22:]
    (
        kc, vc, qc, mem_grad, mem_stats, own_stats,
        dq, dk, dv,
        doc, stats, chain_stats, qown, kown, vown, down, bias, qacc, kacc, vacc, sems, stat_sems,
    ) = refs
    step = pl.program_id(0)
    quad = start + step
    length = meta[M_LEN]

    @pl.when(step == 0)
    def _():
        rows_from = lambda index: lambda ref: ref.at[0:SEG, pl.ds((start + index) * QUAD, QUAD)]
        rows_to = lambda index: lambda spot: doc.at[index, pl.ds(MEMP + SEG * spot, SEG)]
        stat_from = lambda ref: ref.at[SEG : SEG + 2 * STAT, 0:SEG]
        stat_to = lambda spot: stats.at[spot]
        load_chain(meta, pieces, stat_from, stat_to, stat_sems)
        for index in range(count):
            load_chain(meta, pieces, rows_from(index), rows_to(index), sems.at[index])
        bias[...] = key_bias(meta)
        for index in range(count):
            doc[index, 0:MEMP, :] = mem_grad[:, (start + index) * QUAD : (start + index + 1) * QUAD]

            @pl.when(meta[M_BLOCKS] > length)
            def _():
                place = pl.multiple_of(MEMP + SEG * length, MEMP)
                doc[index, pl.ds(place, SEG - MEMP), :] = jnp.zeros((SEG - MEMP, QUAD), BF16)

        wait_chain(meta, pieces, stat_from, stat_to, stat_sems)
        for spot in range(NBLK):
            span = slice(SEG * spot, SEG * (spot + 1))
            if spot == LONG:
                chain_stats[:, span] = jnp.zeros((STAT, SEG), F32)
                continue

            @pl.when(spot < length)
            def _():
                pair = stats[spot].astype(F32)
                chain_stats[:, span] = pair[0:STAT] + pair[STAT : 2 * STAT]

            @pl.when(spot >= length)
            def _():
                chain_stats[:, span] = jnp.zeros((STAT, SEG), F32)

        moved = pltpu.roll(chain_stats[...], MEMP, 1)
        column = lax.broadcasted_iota(jnp.int32, (STAT, CAP), 1)
        entry = lax.broadcasted_iota(jnp.int32, (STAT, CAP), 0)
        beyond = jnp.where(entry < H, -NEG, 0.0)
        chain_stats[...] = jnp.where(column < MEMP + SEG * length, moved, beyond)
        lane = lax.broadcasted_iota(jnp.int32, (STAT, PAIR), 1)
        at_front = pltpu.roll(mem_stats[...], MEMP, 1)
        chain_stats[:, 0:PAIR] = jnp.where(lane < MEMP, at_front, chain_stats[:, 0:PAIR])
        for index in range(count):
            wait_chain(meta, pieces, rows_from(index), rows_to(index), sems.at[index])

    place = pl.multiple_of(MEMP + SEG * meta[M_SPOT], MEMP)
    for own, chain in ((qown, qc), (kown, kc), (vown, vc), (down, doc.at[step])):
        own[0:SEG, :] = chain[pl.ds(place, SEG), :]
        own[SEG:OWN, :] = chain[0:MEMP, :]

    def head(index, carry):
        cols = pl.ds(pl.multiple_of((index // 2) * PAIR, PAIR), PAIR)
        number = quad * 4 + index
        lane = lax.broadcasted_iota(jnp.int32, (OWN, PAIR), 1)
        mine = (lane // HD) == (index % 2)
        masked = lambda ref: jnp.where(mine, ref[:, cols], jnp.zeros((OWN, PAIR), BF16))
        query, key, value, grad = masked(qown), masked(kown), masked(vown), masked(down)
        pick = lambda at: jnp.sum(jnp.where(lane == at, own_stats[...], 0.0), axis=1, keepdims=True)
        log_total, delta = pick(number), pick(H + number)
        for acc in (qacc, kacc, vacc):
            acc[...] = jnp.zeros_like(acc)

        def run(first, size):
            span = span_of(first, size)
            keys, values = kc[span, cols], vc[span, cols]
            scores = lax.dot_general(query, keys, LAST, preferred_element_type=F32)
            weights = jnp.exp(scores + bias[0:1, span] - log_total)
            weight_grad = lax.dot_general(grad, values, LAST, preferred_element_type=F32)
            score_grad = (weights * (weight_grad - delta)).astype(BF16)
            qacc[...] += jnp.dot(score_grad, keys, preferred_element_type=F32)

            queries, grads = qc[span, cols], doc[step, span, cols]
            scores = lax.dot_general(key, queries, LAST, preferred_element_type=F32)
            weights = jnp.exp(scores - chain_stats[pl.ds(number, 1), span])
            weight_grad = lax.dot_general(value, grads, LAST, preferred_element_type=F32)
            score_grad = (
                weights * (weight_grad - chain_stats[pl.ds(H + number, 1), span])
            ).astype(BF16)
            vacc[...] += jnp.dot(weights.astype(BF16), grads, preferred_element_type=F32)
            kacc[...] += jnp.dot(score_grad, queries, preferred_element_type=F32)

        by_chunks(meta[M_BLOCKS], run)
        row = lax.broadcasted_iota(jnp.int32, (OWN, PAIR), 0)
        alive = (row < meta[M_USED]) | ((row >= SEG) & (row < SEG + meta[M_MEM]))
        query_sum = qacc[...] * (HD**-0.5)
        key_sum = jnp.where(alive, kacc[...], 0.0)
        value_sum = jnp.where(alive, vacc[...], 0.0)
        for ref, sums in ((dq, query_sum), (dk, key_sum), (dv, value_sum)):
            ref[:, cols] = jnp.where(mine, sums.astype(BF16), ref[:, cols])
        return carry

    lax.fori_loop(0, 4, head, 0)


def attend_backward(meta, pieces, chain, mem_grad, mem_stats, own_stats, start, count):
    width = mem_grad.shape[1]
    whole = lambda shape: pl.BlockSpec(shape, lambda quad, meta: (0,) * len(shape))
    chain_column = pl.BlockSpec((CAP, QUAD), lambda step, meta: (0, start + step))
    own_column = pl.BlockSpec((OWN, QUAD), lambda step, meta: (0, step))
    return pl.pallas_call(
        functools.partial(backward_body, start, count),
        grid_spec=pltpu.PrefetchScalarGridSpec(
            num_scalar_prefetch=1,
            grid=(count,),
            in_specs=[pl.BlockSpec(memory_space=pl.ANY)] * len(pieces)
            + [chain_column] * 3
            + [whole((MEMP, width)), whole((STAT, PAIR)), whole((OWN, PAIR))],
            out_specs=[own_column] * 3,
            scratch_shapes=[
                pltpu.VMEM((count, CAP, QUAD), BF16),
                pltpu.VMEM((LONG, 2 * STAT, SEG), BF16),
                pltpu.VMEM((STAT, CAP), F32),
            ]
            + [pltpu.VMEM((OWN, QUAD), BF16)] * 4
            + [
                pltpu.VMEM((8, CAP), F32),
                pltpu.VMEM((OWN, PAIR), F32),
                pltpu.VMEM((OWN, PAIR), F32),
                pltpu.VMEM((OWN, PAIR), F32),
                pltpu.SemaphoreType.DMA((count, LONG)),
                pltpu.SemaphoreType.DMA((LONG,)),
            ],
        ),
        out_shape=[jax.ShapeDtypeStruct((OWN, count * QUAD), BF16)] * 3,
        compiler_params=pltpu.CompilerParams(vmem_limit_bytes=VMEM_LIMIT),
        cost_estimate=pl.CostEstimate(
            flops=BACK_COST, bytes_accessed=1_000_000, transcendentals=0
        ),
        name="attend_backward",
    )(meta, *pieces, *chain, mem_grad, mem_stats, own_stats)


def norm_stats(values):
    centered = values - jnp.mean(values, axis=-1, keepdims=True)
    scale = lax.rsqrt(jnp.mean(centered * centered, axis=-1, keepdims=True) + EPS)
    return centered * scale, scale


def norm_back(normed, scale, upstream):
    mean = jnp.mean(upstream, axis=-1, keepdims=True)
    along = jnp.mean(upstream * normed, axis=-1, keepdims=True)
    return scale * (upstream - mean - normed * along)


def turned(left, right):
    return lax.dot_general(left, right, LAST, preferred_element_type=F32)


def crossed(left, right):
    return lax.dot_general(left, right, (((0,), (0,)), ((), ())), preferred_element_type=F32)


def middle_body(
    meta, attended, lse, tokens, memory, token_cot, memory_cot,
    wo, bo, gain1, shift1, bi, b2, gain2, shift2, wi_from, w2_from,
    final, final_mem, payload, mem_grad, mem_stats, own_stats, res_grad, rows,
    attended_low, branch_out, first_low, inner_out, active, outer_out, sums, inner_sum,
    wi, w2, first, norm1, scale1, total, second_grad, outer_grad, slope, weight_sems,
):
    width, inner_width = wi.shape
    wi_copy = pltpu.make_async_copy(wi_from, wi, weight_sems.at[0])
    w2_copy = pltpu.make_async_copy(w2_from, w2, weight_sems.at[1])
    wi_copy.start()
    w2_copy.start()
    chain = meta[M_CHAIN]
    lead = jnp.where(meta[M_SPOT] == 0, 1.0, 0.0)
    rows[0:SEG, :] = tokens[...]
    rows[SEG:OWN, :] = memory[chain]
    attended_low[...] = attended[...].astype(BF16)
    total[...] = jnp.dot(attended_low[...], wo[...], preferred_element_type=F32)
    sums[...] = jnp.zeros_like(sums)
    inner_sum[...] = jnp.zeros_like(inner_sum)
    vector = lambda ref: ref[...].astype(F32)

    def by_rows(run):
        def step(index, carry):
            start = pl.multiple_of(index * ROWS, ROWS)
            row = start + lax.broadcasted_iota(jnp.int32, (ROWS, 1), 0)
            live = (row < meta[M_USED]) | ((row >= SEG) & (row < SEG + meta[M_MEM]))
            counted = jnp.where(row < SEG, 1.0, lead)
            run(pl.ds(start, ROWS), live, counted)
            return carry

        lax.fori_loop(0, OWN // ROWS, step, 0)

    def by_columns(run):
        def step(index, carry):
            run(pl.ds(pl.multiple_of(index * COLS, COLS), COLS))
            return carry

        lax.fori_loop(0, inner_width // COLS, step, 0)

    def add(place, value):
        sums[place : place + 1, :] += jnp.sum(value, axis=0, keepdims=True)

    def first_part(span, live, counted):
        value = rows[span, :].astype(F32) + total[span, :] + vector(bo)
        normed, scale = norm_stats(value)
        norm1[span, :] = normed
        scale1[span, :] = jnp.broadcast_to(scale, (ROWS, PAIR))
        value = normed * vector(gain1) + vector(shift1)
        first[span, :] = value
        first_low[span, :] = value.astype(BF16)

    by_rows(first_part)
    wi_copy.wait()
    w2_copy.wait()
    total[...] = jnp.zeros_like(total)

    def inner_part(cols):
        inner = jnp.dot(first_low[...], wi[:, cols], preferred_element_type=F32)
        inner = inner + bi[:, cols].astype(F32)
        cdf = 0.5 * (1.0 + lax.erf(inner * (2.0**-0.5)))
        density = jnp.exp(-0.5 * inner * inner) * 0.3989422804014327
        slope[:, cols] = cdf + inner * density
        low = (inner * cdf).astype(BF16)
        active[:, cols] = low
        total[...] += jnp.dot(low, w2[cols, :], preferred_element_type=F32)

    by_columns(inner_part)

    def final_part(span, live, counted):
        normed, scale = norm_stats(first[span, :] + total[span, :] + vector(b2))
        value = jnp.where(live, normed * vector(gain2) + vector(shift2), 0.0)
        rows_low = value.astype(BF16)
        outer_out[span, :] = rows_low
        start = span.start

        @pl.when(start < SEG)
        def _():
            cot = token_cot[span, :].astype(F32)
            first_back(span, live, counted, normed, scale, cot)

        @pl.when(start >= SEG)
        def _():
            cot = memory_cot[chain].astype(F32)
            first_back(span, live, counted, normed, scale, cot)

    def first_back(span, live, counted, normed, scale, cot):
        cot = jnp.where(live, cot, 0.0)
        weighted = cot * counted
        add(4, weighted * normed)
        add(5, weighted)
        grad = norm_back(normed, scale, cot * vector(gain2))
        second_grad[span, :] = grad
        outer_grad[span, :] = grad.astype(BF16)
        add(3, grad.astype(BF16).astype(F32) * counted)

    by_rows(final_part)
    final[...] = outer_out[0:SEG, :]
    final_mem[...] = outer_out[SEG:OWN, :]
    outer_out[0:SEG, :] = outer_grad[0:SEG, :]
    outer_out[SEG:OWN, :] = outer_grad[SEG:OWN, :] * lead.astype(BF16)
    total[...] = jnp.zeros_like(total)

    def inner_back(cols):
        grad = (turned(outer_grad[...], w2[cols, :]) * slope[:, cols]).astype(BF16)
        total[...] += turned(grad, wi[:, cols])
        tail = grad[SEG:OWN] * lead.astype(BF16)
        inner_out[0:SEG, cols] = grad[0:SEG]
        inner_out[SEG:OWN, cols] = tail
        inner_sum[:, cols] = jnp.sum(grad[0:SEG].astype(F32), axis=0, keepdims=True) + jnp.sum(
            tail.astype(F32), axis=0, keepdims=True
        )

    by_columns(inner_back)

    def last_part(span, live, counted):
        grad = second_grad[span, :] + total[span, :]
        normed = norm1[span, :]
        weighted = grad * counted
        add(1, weighted * normed)
        add(2, weighted)
        grad = norm_back(normed, scale1[span, 0:1], grad * vector(gain1))
        res_grad[span, :] = grad
        low = grad.astype(BF16)
        outer_grad[span, :] = low
        low = (low.astype(F32) * counted).astype(BF16)
        branch_out[span, :] = low
        add(0, low.astype(F32))

    by_rows(last_part)
    total[...] = turned(outer_grad[...], wo[...])
    feature = lax.broadcasted_iota(jnp.int32, (width, PAIR), 0)
    lane = lax.broadcasted_iota(jnp.int32, (width, PAIR), 1)
    head_of = jnp.where(feature // HD == lane - H, 1.0, 0.0).astype(BF16)

    def delta_part(span, live, counted):
        low = total[span, :].astype(BF16)
        outer_grad[span, :] = low
        product = low.astype(F32) * attended[span, :]
        high = product.astype(BF16)
        rest = (product - high.astype(F32)).astype(BF16)
        delta = jnp.dot(high, head_of, preferred_element_type=F32)
        delta = delta + jnp.dot(rest, head_of, preferred_element_type=F32)
        own_stats[span, :] = lse[span, :] + delta

    by_rows(delta_part)
    payload[0:SEG, :] = outer_grad[0:SEG, :]
    mem_grad[...] = outer_grad[SEG:OWN, :]
    stats = jnp.transpose(own_stats[0:SEG, :])[0:STAT]
    high = stats.astype(BF16)
    rest = (stats - high.astype(F32)).astype(BF16)
    both = jnp.concatenate([high.astype(F32), rest.astype(F32)], 0).astype(BF16)
    payload[SEG : SEG + 2 * STAT, 0:SEG] = both
    payload[SEG : SEG + 2 * STAT, SEG:width] = jnp.zeros((2 * STAT, width - SEG), BF16)
    mem_stats[...] = jnp.transpose(own_stats[OWN - PAIR : OWN, :])[0:STAT]


def middle(meta, attended, lse, tokens, memory, token_cot, memory_cot, weights):
    wo, bo, gain1, shift1, wi, bi, w2, b2, gain2, shift2 = weights
    width, inner_width = wi.shape
    vmem, line = pl.BlockSpec(memory_space=pltpu.VMEM), lambda value: value.reshape(1, -1)
    hbm = pl.BlockSpec(memory_space=pl.ANY)
    shape = jax.ShapeDtypeStruct
    return pl.pallas_call(
        middle_body,
        in_specs=[pl.BlockSpec(memory_space=pltpu.SMEM)] + [vmem] * 14 + [hbm] * 2,
        out_specs=[vmem] * 16,
        out_shape=[
            shape((SEG, width), BF16),
            shape((MEMP, width), BF16),
            shape((SEG + 2 * STAT, width), BF16),
            shape((MEMP, width), BF16),
            shape((STAT, PAIR), F32),
            shape((OWN, PAIR), F32),
            shape((OWN, width), F32),
            shape((OWN, width), BF16),
            shape((OWN, width), BF16),
            shape((OWN, width), BF16),
            shape((OWN, width), BF16),
            shape((OWN, inner_width), BF16),
            shape((OWN, inner_width), BF16),
            shape((OWN, width), BF16),
            shape((8, width), F32),
            shape((1, inner_width), F32),
        ],
        scratch_shapes=[
            pltpu.VMEM((width, inner_width), BF16),
            pltpu.VMEM((inner_width, width), BF16),
            pltpu.VMEM((OWN, width), F32),
            pltpu.VMEM((OWN, width), F32),
            pltpu.VMEM((OWN, PAIR), F32),
            pltpu.VMEM((OWN, width), F32),
            pltpu.VMEM((OWN, width), F32),
            pltpu.VMEM((OWN, width), BF16),
            pltpu.VMEM((OWN, inner_width), F32),
            pltpu.SemaphoreType.DMA((2,)),
        ],
        compiler_params=pltpu.CompilerParams(vmem_limit_bytes=VMEM_LIMIT),
        cost_estimate=pl.CostEstimate(
            flops=12_000_000_000, bytes_accessed=40_000_000, transcendentals=2_000_000
        ),
        name="middle",
    )(
        meta, attended, lse, tokens, memory, token_cot, memory_cot,
        wo, line(bo), line(gain1), line(shift1), line(bi), line(b2), line(gain2), line(shift2),
        wi, w2,
    )


def late_body(metas, group, *refs, batches, chains, parts):
    refs = list(refs)
    take = lambda count: [refs.pop(0) for _ in range(count)]
    rows, res_mem = take(batches), take(batches)
    grads = [[take(len(parts[b])) for _ in range(3)] for b in range(batches)]
    weights = take(3)
    out, masked = take(2)
    width = weights[0].shape[0]
    out[3 * width :, :] = jnp.zeros((out.shape[0] - 3 * width, width), BF16)
    for b in range(batches):
        lead = jnp.where(metas[b, M_SPOT] == 0, 1.0, 0.0)
        masked[b, 0:SEG, :] = rows[b][0:SEG, :]
        masked[b, SEG:OWN, :] = rows[b][SEG:OWN, :] * lead.astype(BF16)
        grad = res_mem[b][SEG:OWN, :]
        for k in range(3):
            first = 0
            for part, ref in zip(parts[b], grads[b][k]):
                grad = grad + turned(ref[SEG:OWN, :], weights[k][:, first : first + part])
                first += part
        place = ((group[0] * batches + b) * chains + metas[b, M_CHAIN]) * MEMP
        place = pl.multiple_of(3 * width + 16 + place, 16)
        out[pl.ds(place, MEMP), :] = (grad * lead).astype(BF16)
    cuts = sorted({sum(p[:i]) for p in parts for i in range(len(p) + 1)})
    for k in range(3):
        for low, high in zip(cuts[:-1], cuts[1:]):
            total, line = None, None
            for b in range(batches):
                lead = jnp.where(metas[b, M_SPOT] == 0, 1.0, 0.0)
                first = 0
                for part, ref in zip(parts[b], grads[b][k]):
                    if first <= low and high <= first + part:
                        grad = ref[:, low - first : high - first]
                    first += part
                value = crossed(masked[b], grad)
                total = value if total is None else total + value
                if k != 1:
                    grad = grad.astype(F32)
                    value = jnp.sum(grad[0:SEG], 0, keepdims=True)
                    value = value + jnp.sum(grad[SEG:OWN], 0, keepdims=True) * lead
                    line = value if line is None else line + value
            out[k * width : (k + 1) * width, low:high] = total.astype(BF16)
            if k != 1:
                row = lax.broadcasted_iota(jnp.int32, (16, high - low), 0)
                span = slice(3 * width, 3 * width + 16)
                old = out[span, low:high].astype(F32)
                out[span, low:high] = jnp.where(row == k // 2, line, old).astype(BF16)


def late_sums(metas, group, groups, chains, rows, res, grads, weights):
    batches, width = len(rows), weights[0].shape[0]
    parts = [[part.shape[1] for part in one[0]] for one in grads]
    count = 3 * width + 16 + groups * batches * chains * MEMP
    count += -count % LATE_ROWS
    vmem, smem = pl.BlockSpec(memory_space=pltpu.VMEM), pl.BlockSpec(memory_space=pltpu.SMEM)
    flat = [part for one in grads for name in one for part in name]
    return pl.pallas_call(
        functools.partial(late_body, batches=batches, chains=chains, parts=parts),
        in_specs=[smem] * 2 + [vmem] * (2 * batches + len(flat) + 3),
        out_specs=vmem,
        out_shape=jax.ShapeDtypeStruct((count, width), BF16),
        scratch_shapes=[pltpu.VMEM((batches, OWN, width), BF16)],
        compiler_params=pltpu.CompilerParams(vmem_limit_bytes=VMEM_LIMIT),
        name="late_sums",
    )(metas, group.reshape(1), *rows, *res, *flat, *weights)


def weight_grad(left, right):
    return lax.dot_general(left, right, (((0,), (0,)), ((), ())), preferred_element_type=F32)


def swap(value, mask):
    sizes = lax.axis_size("dp") * lax.axis_size("blk")
    return lax.ppermute(value, ("dp", "blk"), [(i, i ^ mask) for i in range(sizes)])


def sum_everywhere(value, beside):
    blk = lax.axis_size("blk")
    place = lax.axis_index("dp") * blk + lax.axis_index("blk")
    groups = [(1,), (2, blk), (4, 8)]
    bit = 2 * blk
    while bit < blk * lax.axis_size("dp"):
        groups.append((bit,))
        bit *= 2
    masks_of = lambda group: [
        sum(bit for i, bit in enumerate(group) if (k >> i) & 1) for k in range(1 << len(group))
    ]
    own_of = lambda group: sum(((place // bit) % 2) << i for i, bit in enumerate(group))
    for group in groups:
        masks, own = masks_of(group), own_of(group)
        size = value.shape[0] // len(masks)
        part = lambda k: lax.dynamic_slice_in_dim(value, (own ^ k) * size, size)
        got = [swap(part(k), mask) for k, mask in enumerate(masks) if k]
        value = sum((g.astype(F32) for g in got), part(0).astype(F32)).astype(BF16)
    for index, group in enumerate(reversed(groups)):
        if index + 1 == len(groups):
            value, beside = lax.optimization_barrier((value, beside))
        masks, own = masks_of(group), own_of(group)
        size = value.shape[0]
        got = [value] + [swap(value, mask) for mask in masks[1:]]
        value = jnp.zeros((size * len(masks), value.shape[1]), BF16)
        for k, part in enumerate(got):
            value = lax.dynamic_update_slice_in_dim(value, part, (own ^ k) * size, 0)
    return value, beside


def local(
    tokens, memory, chain_lengths, last_fill,
    query_proj, query_bias, key_proj, value_proj, value_bias, output_proj, output_bias,
    attn_gain, attn_shift, inner_proj, inner_bias, outer_proj, outer_bias,
    final_gain, final_shift, token_cotangent, memory_cotangent,
):
    own = lax.axis_index("blk").astype(jnp.int32)
    group = lax.axis_index("dp").astype(jnp.int32)
    groups = lax.axis_size("dp")
    batches, _, width = tokens.shape
    chains, mem_rows = memory.shape[1:3]
    pad_mem = ((0, 0), (0, 0), (0, MEMP - mem_rows), (0, 0))
    memory, memory_cotangent = jnp.pad(memory, pad_mem), jnp.pad(memory_cotangent, pad_mem)

    metas = metas_of(own, chain_lengths[:, 0], last_fill[:, 0], mem_rows)
    near = gather_near(tokens[0])
    later, near = lax.optimization_barrier(([tokens[b] for b in range(1, batches)], near))
    pieces = [near] + [gather_all(part) for part in later]
    meta_of = [metas[b] for b in range(batches)]

    states = []
    for b in range(batches):
        meta = meta_of[b]
        attended, lse, *chain_rows = attend_forward(
            meta, pieces[b], memory[b], (query_proj, query_bias, key_proj, value_proj, value_bias)
        )
        (
            final, final_mem, payload, mem_grad, mem_stats, own_stats, res_grad, rows,
            attended_low, branch, first_low, inner, active, outer, sums, inner_sum,
        ) = middle(
            meta, attended, lse, tokens[b], memory[b], token_cotangent[b], memory_cotangent[b],
            (
                output_proj, output_bias, attn_gain, attn_shift, inner_proj, inner_bias,
                outer_proj, outer_bias, final_gain, final_shift,
            ),
        )
        if b + 1 < batches:
            meta_of[b + 1], payload = lax.optimization_barrier((meta_of[b + 1], payload))
        states.append(
            dict(
                meta=meta, rows=rows, chain_rows=chain_rows, payload=payload, mem_grad=mem_grad,
                mem_stats=mem_stats, own_stats=own_stats, res_grad=res_grad, final=final,
                final_mem=final_mem, attended_low=attended_low, branch=branch,
                first_low=first_low, inner=inner, active=active, outer=outer, sums=sums,
                inner_sum=inner_sum,
            )
        )

    def over_batches(left, right):
        return weight_grad(
            jnp.concatenate([s[left] for s in states], 0),
            jnp.concatenate([s[right] for s in states], 0),
        ).astype(BF16)

    slots = (jnp.arange(groups)[:, None, None, None, None] == group) & (
        jnp.arange(chains)[:, None, None]
        == jnp.where(metas[:, M_SPOT] == 0, metas[:, M_CHAIN], -1)[:, None, None, None]
    )
    final_mem = jnp.stack([s["final_mem"] for s in states])[None, :, None]
    early = (
        over_batches("first_low", "inner"),
        over_batches("active", "outer"),
        over_batches("attended_low", "branch"),
        jnp.concatenate(
            [
                jnp.where(slots, final_mem, 0).astype(BF16).reshape(-1, width),
                sum(s["sums"] for s in states).astype(BF16),
                sum(s["inner_sum"] for s in states).astype(BF16).reshape(-1, width),
            ],
            0,
        ),
    )
    early, *held = lax.optimization_barrier((early, *[s["meta"] for s in states]))
    for s, meta in zip(states, held):
        s["meta"] = meta
    early = lax.psum(early, ("dp", "blk"))

    def backward(s, payload, *quads):
        return attend_backward(
            s["meta"], payload, s["chain_rows"], s["mem_grad"], s["mem_stats"], s["own_stats"],
            *quads,
        )

    def hold(stage, parts):
        got = [backward(s, s["gathered"], stage, 1) for s in states[:-1]]
        got, parts = lax.optimization_barrier((got, parts))
        for s, grads in zip(states, got):
            s["grads"] = [old + [new] for old, new in zip(s.get("grads", [[]] * 3), grads)]
        return parts

    for s in states[:-1]:
        s["gathered"] = gather_all(s["payload"])
    last = states[-1]
    near = gather_near(last["payload"], hold)
    last["grads"] = [[grad] for grad in backward(last, near, 0, NQUAD)]
    last["grads"], early = lax.optimization_barrier((last["grads"], early))
    grad_inner, grad_outer, grad_output, rest = early
    late = late_sums(
        metas, group, groups, chains, [s["rows"] for s in states],
        [s["res_grad"] for s in states], [s["grads"] for s in states],
        (query_proj, key_proj, value_proj),
    )

    def own_slots(rows):
        rows = rows.reshape(groups, batches, chains, MEMP, width)
        return lax.dynamic_index_in_dim(rows, group, keepdims=False)[:, :, :mem_rows]

    wide_early = [part.astype(F32) for part in (grad_inner, grad_outer, grad_output)]
    late, (grad_inner, grad_outer, grad_output) = sum_everywhere(late, wide_early)
    grad_query, grad_key, grad_value = (late[i * width : (i + 1) * width] for i in range(3))
    biases = late[3 * width : 3 * width + 2].astype(F32)
    count = groups * batches * chains * MEMP
    memory_grad = own_slots(late[3 * width + 16 : 3 * width + 16 + count])
    memory_out = own_slots(rest[:count])
    sums, inner_sum = rest[count : count + 8], rest[count + 8 :].reshape(1, -1)
    token_outs = [s["final"] for s in states]
    token_grads = []
    for s in states:
        grad = s["res_grad"][:SEG]
        for parts, weights in zip(s["grads"], (query_proj, key_proj, value_proj)):
            first = 0
            for part in parts:
                grad = grad + turned(part[:SEG], weights[:, first : first + part.shape[1]])
                first += part.shape[1]
        token_grads.append(grad.astype(BF16))

    wide = lambda value: value.astype(F32)
    return (
        jnp.stack(token_outs),
        memory_out,
        jnp.stack(token_grads),
        memory_grad,
        wide(grad_query),
        biases[0],
        wide(grad_key),
        wide(grad_value),
        biases[1],
        wide(grad_output),
        wide(sums[0]),
        wide(sums[1]),
        wide(sums[2]),
        wide(grad_inner),
        wide(inner_sum[0]),
        wide(grad_outer),
        wide(sums[3]),
        wide(sums[4]),
        wide(sums[5]),
    )


def solution(mesh):
    row_spec = P(None, ("dp", "blk"), None)
    mem_spec = P(None, "dp", None, None)
    int_spec = P(None, "dp", None)
    in_specs = (row_spec, mem_spec, int_spec, int_spec) + (P(),) * 15 + (row_spec, mem_spec)
    out_specs = (row_spec, mem_spec, row_spec, mem_spec) + (P(),) * 15
    return jax.shard_map(local, mesh=mesh, in_specs=in_specs, out_specs=out_specs, check_vma=False)
```

```python
import functools

import jax
import jax.numpy as jnp
from jax import lax
from jax.experimental import pallas as pl
from jax.experimental.pallas import tpu as pltpu
from jax.sharding import PartitionSpec as P

H = 12
HD = 64
QUAD = 256
NQUAD = 3
PAIR = 128
MEMP = 32
SEG = 512
LONG = 7
NBLK = LONG + 1
CAP = NBLK * SEG
OWN = SEG + MEMP
STAT = 24
BACK_COST = 10_000_000_000
LATE_ROWS = 256
NPIECE = 14
ROWS = 272
COLS = 1024
NEG = -1e30
SHIFT_FREE = 60.0
EPS = 1e-05
F32 = jnp.float32
BF16 = jnp.bfloat16
VMEM_LIMIT = 60 * 2**20
LAST = (((1,), (1,)), ((), ()))

M_LEN, M_ROWS, M_BLOCKS, M_SPOT, M_USED, M_MEM, M_CHAIN, M_START, M_PIECE = range(9)


def plane_moves(shift_of):
    pairs = []
    for plane in range(4):
        for place in range(4):
            target = plane + shift_of(place >> 1)
            if 0 <= target < 4:
                pairs.append((4 * plane + place, 4 * target + place))
    return pairs


UP = plane_moves(lambda side: 1)
DOWN = plane_moves(lambda side: -1)
OUTWARD = plane_moves(lambda side: 1 if side else -1)
SIDE = [(i, i ^ 2) for i in range(16)]
CORE = [(i, i ^ 1) for i in range(16)]


def move(value, pairs):
    return lax.ppermute(value, "blk", pairs)


def gather_near(value):
    side = (lax.axis_index("blk") >> 1) & 1
    below, above, beside = move(value, UP), move(value, DOWN), move(value, SIDE)
    far = move(jnp.where(side == 1, below, above), OUTWARD)
    moved = [move(beside, UP), move(beside, DOWN), move(far, SIDE)]
    here = [value, beside, below, above] + moved
    return here + [move(part, CORE) for part in here]


def gather_all(value):
    return [lax.all_gather(value, "blk")]


def piece_of(own, other):
    plane = (other >> 2) - (own >> 2)
    same_side = ((other >> 1) & 1) == ((own >> 1) & 1)
    on_side = jnp.where(plane == 0, 0, jnp.where(plane < 0, 2, 3))
    off_side = jnp.where(plane == 0, 1, jnp.where(plane == -1, 4, jnp.where(plane == 1, 5, 6)))
    index = jnp.where(same_side, on_side, off_side)
    return index + jnp.where((other & 1) == (own & 1), 0, LONG)


def meta_body(own_ref, lengths, fills, meta, *, batches, chains, mem_rows):
    own = own_ref[0]
    for b in range(batches):
        end = jnp.int32(0)
        length, start, fill, chain = (jnp.int32(0) for _ in range(4))
        for c in range(chains):
            begin = end
            end = end + lengths[b, c]
            inside = (begin <= own) & (own < end)
            length = jnp.where(inside, lengths[b, c], length)
            start = jnp.where(inside, begin, start)
            fill = jnp.where(inside, fills[b, c], fill)
            chain = jnp.where(inside, c, chain)
        rows = MEMP + SEG * (length - 1) + fill
        spot = own - start
        meta[b, M_LEN] = length
        meta[b, M_ROWS] = rows
        meta[b, M_BLOCKS] = (rows + SEG - 1) // SEG
        meta[b, M_SPOT] = spot
        meta[b, M_USED] = jnp.where(spot == length - 1, fill, SEG)
        meta[b, M_MEM] = jnp.int32(mem_rows)
        meta[b, M_CHAIN] = chain
        meta[b, M_START] = start
        for place in range(8):
            meta[b, M_PIECE + place] = piece_of(own, start + place)


def metas_of(own, lengths, fills, mem_rows):
    smem = pl.BlockSpec(memory_space=pltpu.SMEM)
    body = functools.partial(
        meta_body, batches=lengths.shape[0], chains=lengths.shape[1], mem_rows=mem_rows
    )
    return pl.pallas_call(
        body,
        in_specs=[smem] * 3,
        out_specs=smem,
        out_shape=jax.ShapeDtypeStruct((lengths.shape[0], 16), jnp.int32),
        name="find_chain",
    )(own.reshape(1), lengths, fills)


def load_chain(meta, pieces, view_from, view_to, sems):
    length = meta[M_LEN]
    for spot in range(LONG):
        def start(source):
            pltpu.make_async_copy(view_from(source), view_to(spot), sems.at[spot]).start()

        @pl.when(spot < length)
        def _():
            if len(pieces) == 1:
                start(pieces[0].at[meta[M_START] + spot])
                return
            for index in range(len(pieces)):
                @pl.when(meta[M_PIECE + spot] == index)
                def _():
                    start(pieces[index])


def wait_chain(meta, pieces, view_from, view_to, sems):
    length = meta[M_LEN]
    source = pieces[0].at[0] if len(pieces) == 1 else pieces[0]
    for spot in range(LONG):
        @pl.when(spot < length)
        def _():
            pltpu.make_async_copy(view_from(source), view_to(spot), sems.at[spot]).wait()


def key_bias(meta):
    column = lax.broadcasted_iota(jnp.int32, (8, CAP), 1)
    dead = (column >= meta[M_ROWS]) | ((column >= meta[M_MEM]) & (column < MEMP))
    return jnp.where(dead, NEG, 0.0).astype(F32)


def by_chunks(blocks, run):
    def four(index, carry):
        run(index * 4, 4)
        return carry

    lax.fori_loop(0, blocks // 4, four, 0)
    for count in (1, 2, 3):
        @pl.when(blocks % 4 == count)
        def _():
            run((blocks // 4) * 4, count)


def span_of(first, count):
    return pl.ds(pl.multiple_of(first * SEG, SEG), count * SEG)


def forward_body(meta, *refs):
    pieces, refs = refs[:-16], refs[-16:]
    mem, wq, wk, wv, bq, bv, out, lse, kc, vc, qc, rows, qown, extended, acc, sems = refs
    quad = pl.program_id(0)
    width = rows.shape[1]
    length, blocks = meta[M_LEN], meta[M_BLOCKS]
    here = lambda source: source
    there = lambda spot: rows.at[pl.ds(MEMP + SEG * spot, SEG)]

    @pl.when(quad == 0)
    def _():
        load_chain(meta, pieces, here, there, sems)
        rows[0:MEMP, :] = mem[meta[M_CHAIN]]
        lse[...] = jnp.zeros_like(lse)

        @pl.when(blocks > length)
        def _():
            place = pl.multiple_of(MEMP + SEG * length, MEMP)
            rows[pl.ds(place, SEG - MEMP), :] = jnp.zeros((SEG - MEMP, width), BF16)

        wait_chain(meta, pieces, here, there, sems)

    def longest(values):
        halves = [
            jnp.max(jnp.sum(jnp.square(values[:, p : p + PAIR]), axis=1, keepdims=True))
            for p in range(0, QUAD, PAIR)
        ]
        return jnp.maximum(*halves)

    def project(start, count):
        span = pl.ds(pl.multiple_of(start, MEMP), count)
        part = rows[span, :]
        row = start + lax.broadcasted_iota(jnp.int32, (count, QUAD), 0)
        alive = (row < meta[M_ROWS]) & ((row < meta[M_MEM]) | (row >= MEMP))
        lower = (lax.broadcasted_iota(jnp.int32, (count, QUAD), 1) % PAIR) < HD
        key = jnp.dot(part, wk[...], preferred_element_type=F32)
        kc[span, :] = key.astype(BF16)
        value = jnp.dot(part, wv[...], preferred_element_type=F32) + bv[...].astype(F32)
        vc[span, :] = value.astype(BF16)
        value = jnp.where(alive, value, 0.0)
        one = jnp.where(alive, 1.0, 0.0)
        extended[0, span, :] = jnp.where(lower, value, one).astype(BF16)
        extended[1, span, :] = jnp.where(lower, one, value).astype(BF16)
        query = jnp.dot(part, wq[...], preferred_element_type=F32) + bq[...].astype(F32)
        query = query.astype(BF16) * jnp.asarray(HD**-0.5, BF16)
        qc[span, :] = query
        return longest(key)

    def project_block(block, top):
        return jnp.maximum(top, project(block * SEG, SEG))

    key_top = lax.fori_loop(0, blocks, project_block, jnp.float32(0.0))

    @pl.when(blocks == length)
    def _():
        project(length * SEG, MEMP)

    place = pl.multiple_of(MEMP + SEG * meta[M_SPOT], MEMP)
    qown[0:SEG, :] = qc[pl.ds(place, SEG), :]
    qown[SEG:OWN, :] = qc[0:MEMP, :]
    near = longest(qown[...].astype(F32)) * key_top <= SHIFT_FREE**2

    def head(index, carry):
        cols = pl.ds(pl.multiple_of((index // 2) * PAIR, PAIR), PAIR)
        half = index % 2
        lane = lax.broadcasted_iota(jnp.int32, (OWN, PAIR), 1)
        mine = (lane // HD) == half
        query = qown[:, cols]
        query = jnp.where(mine, query, jnp.zeros_like(query))
        acc[...] = jnp.zeros_like(acc)
        number = lane == quad * 4 + index

        def score(span):
            return lax.dot_general(query, kc[span, cols], LAST, preferred_element_type=F32)

        def gather(span, terms):
            values = extended[half, span, cols]
            return jnp.dot(terms.astype(BF16), values, preferred_element_type=F32)

        @pl.when(near)
        def _():
            def run(first, count):
                span = span_of(first, count)
                acc[...] += gather(span, jnp.exp(score(span)))

            by_chunks(blocks, run)
            lse[...] = jnp.where(number, 0.0, lse[...])

        @pl.when(jnp.logical_not(near))
        def _():
            def run(block, top):
                span = span_of(block, 1)
                column = block * SEG + lax.broadcasted_iota(jnp.int32, (OWN, SEG), 1)
                dead = (column >= meta[M_ROWS]) | ((column >= meta[M_MEM]) & (column < MEMP))
                scores = jnp.where(dead, NEG, score(span))
                new = jnp.maximum(top, jnp.max(scores, axis=1, keepdims=True))
                acc[...] = acc[...] * jnp.exp(top - new) + gather(span, jnp.exp(scores - new))
                return new

            top = lax.fori_loop(0, blocks, run, jnp.full((OWN, 1), NEG, F32))
            lse[...] = jnp.where(number, top, lse[...])

        sums = acc[...]
        total = jnp.where(mine, pltpu.roll(sums, HD, 1), sums)
        out[:, cols] = jnp.where(mine, sums * (1.0 / total), out[:, cols])
        lse[...] += jnp.where(number, jnp.log(total), 0.0)
        return carry

    lax.fori_loop(0, 4, head, 0)


def attend_forward(meta, pieces, mem, weights):
    wq, bq, wk, wv, bv = weights
    width = wq.shape[0]
    whole = lambda shape: pl.BlockSpec(shape, lambda quad, meta: (0,) * len(shape))
    column = lambda count: pl.BlockSpec((count, QUAD), lambda quad, meta: (0, quad))
    return pl.pallas_call(
        forward_body,
        grid_spec=pltpu.PrefetchScalarGridSpec(
            num_scalar_prefetch=1,
            grid=(NQUAD,),
            in_specs=[pl.BlockSpec(memory_space=pl.ANY)] * len(pieces)
            + [whole((mem.shape[0], MEMP, width))]
            + [column(width)] * 3
            + [column(1)] * 2,
            out_specs=[column(OWN), whole((OWN, PAIR))] + [column(CAP)] * 3,
            scratch_shapes=[
                pltpu.VMEM((CAP, width), BF16),
                pltpu.VMEM((OWN, QUAD), BF16),
                pltpu.VMEM((2, CAP, QUAD), BF16),
                pltpu.VMEM((OWN, PAIR), F32),
                pltpu.SemaphoreType.DMA((LONG,)),
            ],
        ),
        out_shape=[
            jax.ShapeDtypeStruct((OWN, width), F32),
            jax.ShapeDtypeStruct((OWN, PAIR), F32),
        ]
        + [jax.ShapeDtypeStruct((CAP, width), BF16)] * 3,
        compiler_params=pltpu.CompilerParams(vmem_limit_bytes=VMEM_LIMIT),
        cost_estimate=pl.CostEstimate(
            flops=40_000_000_000, bytes_accessed=30_000_000, transcendentals=23_000_000
        ),
        name="attend_forward",
    )(meta, *pieces, mem, wq, wk, wv, bq.reshape(1, -1), bv.reshape(1, -1))


def backward_body(start, count, meta, *refs):
    pieces, refs = refs[:-22], refs[-22:]
    (
        kc, vc, qc, mem_grad, mem_stats, own_stats,
        dq, dk, dv,
        doc, stats, chain_stats, qown, kown, vown, down, bias, qacc, kacc, vacc, sems, stat_sems,
    ) = refs
    step = pl.program_id(0)
    quad = start + step
    length = meta[M_LEN]

    @pl.when(step == 0)
    def _():
        rows_from = lambda index: lambda ref: ref.at[0:SEG, pl.ds((start + index) * QUAD, QUAD)]
        rows_to = lambda index: lambda spot: doc.at[index, pl.ds(MEMP + SEG * spot, SEG)]
        stat_from = lambda ref: ref.at[SEG : SEG + 2 * STAT, 0:SEG]
        stat_to = lambda spot: stats.at[spot]
        load_chain(meta, pieces, stat_from, stat_to, stat_sems)
        for index in range(count):
            load_chain(meta, pieces, rows_from(index), rows_to(index), sems.at[index])
        bias[...] = key_bias(meta)
        for index in range(count):
            doc[index, 0:MEMP, :] = mem_grad[:, (start + index) * QUAD : (start + index + 1) * QUAD]

            @pl.when(meta[M_BLOCKS] > length)
            def _():
                place = pl.multiple_of(MEMP + SEG * length, MEMP)
                doc[index, pl.ds(place, SEG - MEMP), :] = jnp.zeros((SEG - MEMP, QUAD), BF16)

        wait_chain(meta, pieces, stat_from, stat_to, stat_sems)
        for spot in range(NBLK):
            span = slice(SEG * spot, SEG * (spot + 1))
            if spot == LONG:
                chain_stats[:, span] = jnp.zeros((STAT, SEG), F32)
                continue

            @pl.when(spot < length)
            def _():
                pair = stats[spot].astype(F32)
                chain_stats[:, span] = pair[0:STAT] + pair[STAT : 2 * STAT]

            @pl.when(spot >= length)
            def _():
                chain_stats[:, span] = jnp.zeros((STAT, SEG), F32)

        moved = pltpu.roll(chain_stats[...], MEMP, 1)
        column = lax.broadcasted_iota(jnp.int32, (STAT, CAP), 1)
        entry = lax.broadcasted_iota(jnp.int32, (STAT, CAP), 0)
        beyond = jnp.where(entry < H, -NEG, 0.0)
        chain_stats[...] = jnp.where(column < MEMP + SEG * length, moved, beyond)
        lane = lax.broadcasted_iota(jnp.int32, (STAT, PAIR), 1)
        at_front = pltpu.roll(mem_stats[...], MEMP, 1)
        chain_stats[:, 0:PAIR] = jnp.where(lane < MEMP, at_front, chain_stats[:, 0:PAIR])
        for index in range(count):
            wait_chain(meta, pieces, rows_from(index), rows_to(index), sems.at[index])

    place = pl.multiple_of(MEMP + SEG * meta[M_SPOT], MEMP)
    for own, chain in ((qown, qc), (kown, kc), (vown, vc), (down, doc.at[step])):
        own[0:SEG, :] = chain[pl.ds(place, SEG), :]
        own[SEG:OWN, :] = chain[0:MEMP, :]

    def head(index, carry):
        cols = pl.ds(pl.multiple_of((index // 2) * PAIR, PAIR), PAIR)
        number = quad * 4 + index
        lane = lax.broadcasted_iota(jnp.int32, (OWN, PAIR), 1)
        mine = (lane // HD) == (index % 2)
        masked = lambda ref: jnp.where(mine, ref[:, cols], jnp.zeros((OWN, PAIR), BF16))
        query, key, value, grad = masked(qown), masked(kown), masked(vown), masked(down)
        pick = lambda at: jnp.sum(jnp.where(lane == at, own_stats[...], 0.0), axis=1, keepdims=True)
        log_total, delta = pick(number), pick(H + number)
        for acc in (qacc, kacc, vacc):
            acc[...] = jnp.zeros_like(acc)

        def run(first, size):
            span = span_of(first, size)
            keys, values = kc[span, cols], vc[span, cols]
            scores = lax.dot_general(query, keys, LAST, preferred_element_type=F32)
            weights = jnp.exp(scores + bias[0:1, span] - log_total)
            weight_grad = lax.dot_general(grad, values, LAST, preferred_element_type=F32)
            score_grad = (weights * (weight_grad - delta)).astype(BF16)
            qacc[...] += jnp.dot(score_grad, keys, preferred_element_type=F32)

            queries, grads = qc[span, cols], doc[step, span, cols]
            scores = lax.dot_general(key, queries, LAST, preferred_element_type=F32)
            weights = jnp.exp(scores - chain_stats[pl.ds(number, 1), span])
            weight_grad = lax.dot_general(value, grads, LAST, preferred_element_type=F32)
            score_grad = (
                weights * (weight_grad - chain_stats[pl.ds(H + number, 1), span])
            ).astype(BF16)
            vacc[...] += jnp.dot(weights.astype(BF16), grads, preferred_element_type=F32)
            kacc[...] += jnp.dot(score_grad, queries, preferred_element_type=F32)

        by_chunks(meta[M_BLOCKS], run)
        row = lax.broadcasted_iota(jnp.int32, (OWN, PAIR), 0)
        alive = (row < meta[M_USED]) | ((row >= SEG) & (row < SEG + meta[M_MEM]))
        query_sum = qacc[...] * (HD**-0.5)
        key_sum = jnp.where(alive, kacc[...], 0.0)
        value_sum = jnp.where(alive, vacc[...], 0.0)
        for ref, sums in ((dq, query_sum), (dk, key_sum), (dv, value_sum)):
            ref[:, cols] = jnp.where(mine, sums.astype(BF16), ref[:, cols])
        return carry

    lax.fori_loop(0, 4, head, 0)


def attend_backward(meta, pieces, chain, mem_grad, mem_stats, own_stats, start, count):
    width = mem_grad.shape[1]
    whole = lambda shape: pl.BlockSpec(shape, lambda quad, meta: (0,) * len(shape))
    chain_column = pl.BlockSpec((CAP, QUAD), lambda step, meta: (0, start + step))
    own_column = pl.BlockSpec((OWN, QUAD), lambda step, meta: (0, step))
    return pl.pallas_call(
        functools.partial(backward_body, start, count),
        grid_spec=pltpu.PrefetchScalarGridSpec(
            num_scalar_prefetch=1,
            grid=(count,),
            in_specs=[pl.BlockSpec(memory_space=pl.ANY)] * len(pieces)
            + [chain_column] * 3
            + [whole((MEMP, width)), whole((STAT, PAIR)), whole((OWN, PAIR))],
            out_specs=[own_column] * 3,
            scratch_shapes=[
                pltpu.VMEM((count, CAP, QUAD), BF16),
                pltpu.VMEM((LONG, 2 * STAT, SEG), BF16),
                pltpu.VMEM((STAT, CAP), F32),
            ]
            + [pltpu.VMEM((OWN, QUAD), BF16)] * 4
            + [
                pltpu.VMEM((8, CAP), F32),
                pltpu.VMEM((OWN, PAIR), F32),
                pltpu.VMEM((OWN, PAIR), F32),
                pltpu.VMEM((OWN, PAIR), F32),
                pltpu.SemaphoreType.DMA((count, LONG)),
                pltpu.SemaphoreType.DMA((LONG,)),
            ],
        ),
        out_shape=[jax.ShapeDtypeStruct((OWN, count * QUAD), BF16)] * 3,
        compiler_params=pltpu.CompilerParams(vmem_limit_bytes=VMEM_LIMIT),
        cost_estimate=pl.CostEstimate(
            flops=BACK_COST, bytes_accessed=1_000_000, transcendentals=0
        ),
        name="attend_backward",
    )(meta, *pieces, *chain, mem_grad, mem_stats, own_stats)


def norm_stats(values):
    centered = values - jnp.mean(values, axis=-1, keepdims=True)
    scale = lax.rsqrt(jnp.mean(centered * centered, axis=-1, keepdims=True) + EPS)
    return centered * scale, scale


def norm_back(normed, scale, upstream):
    mean = jnp.mean(upstream, axis=-1, keepdims=True)
    along = jnp.mean(upstream * normed, axis=-1, keepdims=True)
    return scale * (upstream - mean - normed * along)


def turned(left, right):
    return lax.dot_general(left, right, LAST, preferred_element_type=F32)


def crossed(left, right):
    return lax.dot_general(left, right, (((0,), (0,)), ((), ())), preferred_element_type=F32)


def middle_body(
    meta, attended, lse, tokens, memory, token_cot, memory_cot,
    wo, bo, gain1, shift1, bi, b2, gain2, shift2, wi_from, w2_from,
    final, final_mem, payload, mem_grad, mem_stats, own_stats, res_grad, rows,
    attended_low, branch_out, first_low, inner_out, active, outer_out, sums, inner_sum,
    wi, w2, first, norm1, scale1, total, second_grad, outer_grad, slope, cots, weight_sems,
):
    width, inner_width = wi.shape
    wi_copy = pltpu.make_async_copy(wi_from, wi, weight_sems.at[0])
    w2_copy = pltpu.make_async_copy(w2_from, w2, weight_sems.at[1])
    wi_copy.start()
    w2_copy.start()
    chain = meta[M_CHAIN]
    lead = jnp.where(meta[M_SPOT] == 0, 1.0, 0.0)
    rows[0:SEG, :] = tokens[...]
    rows[SEG:OWN, :] = memory[chain]
    cots[0:SEG, :] = token_cot[...]
    cots[SEG:OWN, :] = memory_cot[chain]
    attended_low[...] = attended[...].astype(BF16)
    total[...] = jnp.dot(attended_low[...], wo[...], preferred_element_type=F32)
    sums[...] = jnp.zeros_like(sums)
    inner_sum[...] = jnp.zeros_like(inner_sum)
    vector = lambda ref: ref[...].astype(F32)

    def by_rows(run):
        def step(index, carry):
            start = pl.multiple_of(index * ROWS, ROWS)
            row = start + lax.broadcasted_iota(jnp.int32, (ROWS, 1), 0)
            live = (row < meta[M_USED]) | ((row >= SEG) & (row < SEG + meta[M_MEM]))
            counted = jnp.where(row < SEG, 1.0, lead)
            run(pl.ds(start, ROWS), live, counted)
            return carry

        lax.fori_loop(0, OWN // ROWS, step, 0)

    def by_columns(run):
        def step(index, carry):
            run(pl.ds(pl.multiple_of(index * COLS, COLS), COLS))
            return carry

        lax.fori_loop(0, inner_width // COLS, step, 0)

    def add(place, value):
        sums[place : place + 1, :] += jnp.sum(value, axis=0, keepdims=True)

    def first_part(span, live, counted):
        value = rows[span, :].astype(F32) + total[span, :] + vector(bo)
        normed, scale = norm_stats(value)
        norm1[span, :] = normed
        scale1[span, :] = jnp.broadcast_to(scale, (ROWS, PAIR))
        value = normed * vector(gain1) + vector(shift1)
        first[span, :] = value
        first_low[span, :] = value.astype(BF16)

    by_rows(first_part)
    wi_copy.wait()
    w2_copy.wait()
    total[...] = jnp.zeros_like(total)

    def inner_part(cols):
        inner = jnp.dot(first_low[...], wi[:, cols], preferred_element_type=F32)
        inner = inner + bi[:, cols].astype(F32)
        cdf = 0.5 * (1.0 + lax.erf(inner * (2.0**-0.5)))
        density = jnp.exp(-0.5 * inner * inner) * 0.3989422804014327
        slope[:, cols] = cdf + inner * density
        low = (inner * cdf).astype(BF16)
        active[:, cols] = low
        total[...] += jnp.dot(low, w2[cols, :], preferred_element_type=F32)

    by_columns(inner_part)

    def final_part(span, live, counted):
        normed, scale = norm_stats(first[span, :] + total[span, :] + vector(b2))
        value = jnp.where(live, normed * vector(gain2) + vector(shift2), 0.0)
        rows_low = value.astype(BF16)
        outer_out[span, :] = rows_low
        cot = cots[span, :].astype(F32)
        cot = jnp.where(live, cot, 0.0)
        weighted = cot * counted
        add(4, weighted * normed)
        add(5, weighted)
        grad = norm_back(normed, scale, cot * vector(gain2))
        second_grad[span, :] = grad
        outer_grad[span, :] = grad.astype(BF16)
        add(3, grad.astype(BF16).astype(F32) * counted)

    by_rows(final_part)
    final[...] = outer_out[0:SEG, :]
    final_mem[...] = outer_out[SEG:OWN, :]
    outer_out[0:SEG, :] = outer_grad[0:SEG, :]
    outer_out[SEG:OWN, :] = outer_grad[SEG:OWN, :] * lead.astype(BF16)
    total[...] = jnp.zeros_like(total)

    def inner_back(cols):
        grad = (turned(outer_grad[...], w2[cols, :]) * slope[:, cols]).astype(BF16)
        total[...] += turned(grad, wi[:, cols])
        tail = grad[SEG:OWN] * lead.astype(BF16)
        inner_out[0:SEG, cols] = grad[0:SEG]
        inner_out[SEG:OWN, cols] = tail
        inner_sum[:, cols] = jnp.sum(grad[0:SEG].astype(F32), axis=0, keepdims=True) + jnp.sum(
            tail.astype(F32), axis=0, keepdims=True
        )

    by_columns(inner_back)

    def last_part(span, live, counted):
        grad = second_grad[span, :] + total[span, :]
        normed = norm1[span, :]
        weighted = grad * counted
        add(1, weighted * normed)
        add(2, weighted)
        grad = norm_back(normed, scale1[span, 0:1], grad * vector(gain1))
        res_grad[span, :] = grad
        low = grad.astype(BF16)
        outer_grad[span, :] = low
        low = (low.astype(F32) * counted).astype(BF16)
        branch_out[span, :] = low
        add(0, low.astype(F32))

    by_rows(last_part)
    total[...] = turned(outer_grad[...], wo[...])
    feature = lax.broadcasted_iota(jnp.int32, (width, PAIR), 0)
    lane = lax.broadcasted_iota(jnp.int32, (width, PAIR), 1)
    head_of = jnp.where(feature // HD == lane - H, 1.0, 0.0).astype(BF16)

    def delta_part(span, live, counted):
        low = total[span, :].astype(BF16)
        outer_grad[span, :] = low
        product = low.astype(F32) * attended[span, :]
        high = product.astype(BF16)
        rest = (product - high.astype(F32)).astype(BF16)
        delta = jnp.dot(high, head_of, preferred_element_type=F32)
        delta = delta + jnp.dot(rest, head_of, preferred_element_type=F32)
        own_stats[span, :] = lse[span, :] + delta

    by_rows(delta_part)
    payload[0:SEG, :] = outer_grad[0:SEG, :]
    mem_grad[...] = outer_grad[SEG:OWN, :]
    stats = jnp.transpose(own_stats[0:SEG, :])[0:STAT]
    high = stats.astype(BF16)
    rest = (stats - high.astype(F32)).astype(BF16)
    both = jnp.concatenate([high.astype(F32), rest.astype(F32)], 0).astype(BF16)
    payload[SEG : SEG + 2 * STAT, 0:SEG] = both
    payload[SEG : SEG + 2 * STAT, SEG:width] = jnp.zeros((2 * STAT, width - SEG), BF16)
    mem_stats[...] = jnp.transpose(own_stats[OWN - PAIR : OWN, :])[0:STAT]


def middle(meta, attended, lse, tokens, memory, token_cot, memory_cot, weights):
    wo, bo, gain1, shift1, wi, bi, w2, b2, gain2, shift2 = weights
    width, inner_width = wi.shape
    vmem, line = pl.BlockSpec(memory_space=pltpu.VMEM), lambda value: value.reshape(1, -1)
    hbm = pl.BlockSpec(memory_space=pl.ANY)
    shape = jax.ShapeDtypeStruct
    return pl.pallas_call(
        middle_body,
        in_specs=[pl.BlockSpec(memory_space=pltpu.SMEM)] + [vmem] * 14 + [hbm] * 2,
        out_specs=[vmem] * 16,
        out_shape=[
            shape((SEG, width), BF16),
            shape((MEMP, width), BF16),
            shape((SEG + 2 * STAT, width), BF16),
            shape((MEMP, width), BF16),
            shape((STAT, PAIR), F32),
            shape((OWN, PAIR), F32),
            shape((OWN, width), F32),
            shape((OWN, width), BF16),
            shape((OWN, width), BF16),
            shape((OWN, width), BF16),
            shape((OWN, width), BF16),
            shape((OWN, inner_width), BF16),
            shape((OWN, inner_width), BF16),
            shape((OWN, width), BF16),
            shape((8, width), F32),
            shape((1, inner_width), F32),
        ],
        scratch_shapes=[
            pltpu.VMEM((width, inner_width), BF16),
            pltpu.VMEM((inner_width, width), BF16),
            pltpu.VMEM((OWN, width), F32),
            pltpu.VMEM((OWN, width), F32),
            pltpu.VMEM((OWN, PAIR), F32),
            pltpu.VMEM((OWN, width), F32),
            pltpu.VMEM((OWN, width), F32),
            pltpu.VMEM((OWN, width), BF16),
            pltpu.VMEM((OWN, inner_width), F32),
            pltpu.VMEM((OWN, width), BF16),
            pltpu.SemaphoreType.DMA((2,)),
        ],
        compiler_params=pltpu.CompilerParams(vmem_limit_bytes=VMEM_LIMIT),
        cost_estimate=pl.CostEstimate(
            flops=12_000_000_000, bytes_accessed=40_000_000, transcendentals=2_000_000
        ),
        name="middle",
    )(
        meta, attended, lse, tokens, memory, token_cot, memory_cot,
        wo, line(bo), line(gain1), line(shift1), line(bi), line(b2), line(gain2), line(shift2),
        wi, w2,
    )


def late_body(metas, group, *refs, batches, chains, parts):
    refs = list(refs)
    take = lambda count: [refs.pop(0) for _ in range(count)]
    rows, res_mem = take(batches), take(batches)
    grads = [[take(len(parts[b])) for _ in range(3)] for b in range(batches)]
    weights = take(3)
    out, masked = take(2)
    width = weights[0].shape[0]
    out[3 * width :, :] = jnp.zeros((out.shape[0] - 3 * width, width), BF16)
    for b in range(batches):
        lead = jnp.where(metas[b, M_SPOT] == 0, 1.0, 0.0)
        masked[b, 0:SEG, :] = rows[b][0:SEG, :]
        masked[b, SEG:OWN, :] = rows[b][SEG:OWN, :] * lead.astype(BF16)
        grad = res_mem[b][SEG:OWN, :]
        for k in range(3):
            first = 0
            for part, ref in zip(parts[b], grads[b][k]):
                grad = grad + turned(ref[SEG:OWN, :], weights[k][:, first : first + part])
                first += part
        place = ((group[0] * batches + b) * chains + metas[b, M_CHAIN]) * MEMP
        place = pl.multiple_of(3 * width + 16 + place, 16)
        out[pl.ds(place, MEMP), :] = (grad * lead).astype(BF16)
    cuts = sorted({sum(p[:i]) for p in parts for i in range(len(p) + 1)})
    for k in range(3):
        for low, high in zip(cuts[:-1], cuts[1:]):
            total, line = None, None
            for b in range(batches):
                lead = jnp.where(metas[b, M_SPOT] == 0, 1.0, 0.0)
                first = 0
                for part, ref in zip(parts[b], grads[b][k]):
                    if first <= low and high <= first + part:
                        grad = ref[:, low - first : high - first]
                    first += part
                value = crossed(masked[b], grad)
                total = value if total is None else total + value
                if k != 1:
                    grad = grad.astype(F32)
                    value = jnp.sum(grad[0:SEG], 0, keepdims=True)
                    value = value + jnp.sum(grad[SEG:OWN], 0, keepdims=True) * lead
                    line = value if line is None else line + value
            out[k * width : (k + 1) * width, low:high] = total.astype(BF16)
            if k != 1:
                row = lax.broadcasted_iota(jnp.int32, (16, high - low), 0)
                span = slice(3 * width, 3 * width + 16)
                old = out[span, low:high].astype(F32)
                out[span, low:high] = jnp.where(row == k // 2, line, old).astype(BF16)


def late_sums(metas, group, groups, chains, rows, res, grads, weights):
    batches, width = len(rows), weights[0].shape[0]
    parts = [[part.shape[1] for part in one[0]] for one in grads]
    count = 3 * width + 16 + groups * batches * chains * MEMP
    count += -count % LATE_ROWS
    vmem, smem = pl.BlockSpec(memory_space=pltpu.VMEM), pl.BlockSpec(memory_space=pltpu.SMEM)
    flat = [part for one in grads for name in one for part in name]
    return pl.pallas_call(
        functools.partial(late_body, batches=batches, chains=chains, parts=parts),
        in_specs=[smem] * 2 + [vmem] * (2 * batches + len(flat) + 3),
        out_specs=vmem,
        out_shape=jax.ShapeDtypeStruct((count, width), BF16),
        scratch_shapes=[pltpu.VMEM((batches, OWN, width), BF16)],
        compiler_params=pltpu.CompilerParams(vmem_limit_bytes=VMEM_LIMIT),
        name="late_sums",
    )(metas, group.reshape(1), *rows, *res, *flat, *weights)


def weight_grad(left, right):
    return lax.dot_general(left, right, (((0,), (0,)), ((), ())), preferred_element_type=F32)


def swap(value, mask):
    sizes = lax.axis_size("dp") * lax.axis_size("blk")
    return lax.ppermute(value, ("dp", "blk"), [(i, i ^ mask) for i in range(sizes)])


def sum_everywhere(value, beside):
    blk = lax.axis_size("blk")
    place = lax.axis_index("dp") * blk + lax.axis_index("blk")
    groups = [(1,), (2, blk), (4, 8)]
    bit = 2 * blk
    while bit < blk * lax.axis_size("dp"):
        groups.append((bit,))
        bit *= 2
    masks_of = lambda group: [
        sum(bit for i, bit in enumerate(group) if (k >> i) & 1) for k in range(1 << len(group))
    ]
    own_of = lambda group: sum(((place // bit) % 2) << i for i, bit in enumerate(group))
    for group in groups:
        masks, own = masks_of(group), own_of(group)
        size = value.shape[0] // len(masks)
        part = lambda k: lax.dynamic_slice_in_dim(value, (own ^ k) * size, size)
        got = [swap(part(k), mask) for k, mask in enumerate(masks) if k]
        value = sum((g.astype(F32) for g in got), part(0).astype(F32)).astype(BF16)
    for index, group in enumerate(reversed(groups)):
        if index == 1:
            value, beside = lax.optimization_barrier((value, beside))
        masks, own = masks_of(group), own_of(group)
        size = value.shape[0]
        got = [value] + [swap(value, mask) for mask in masks[1:]]
        value = jnp.zeros((size * len(masks), value.shape[1]), BF16)
        for k, part in enumerate(got):
            value = lax.dynamic_update_slice_in_dim(value, part, (own ^ k) * size, 0)
    return value, beside


def local(
    tokens, memory, chain_lengths, last_fill,
    query_proj, query_bias, key_proj, value_proj, value_bias, output_proj, output_bias,
    attn_gain, attn_shift, inner_proj, inner_bias, outer_proj, outer_bias,
    final_gain, final_shift, token_cotangent, memory_cotangent,
):
    own = lax.axis_index("blk").astype(jnp.int32)
    group = lax.axis_index("dp").astype(jnp.int32)
    groups = lax.axis_size("dp")
    batches, _, width = tokens.shape
    chains, mem_rows = memory.shape[1:3]
    pad_mem = ((0, 0), (0, 0), (0, MEMP - mem_rows), (0, 0))
    memory, memory_cotangent = jnp.pad(memory, pad_mem), jnp.pad(memory_cotangent, pad_mem)

    metas = metas_of(own, chain_lengths[:, 0], last_fill[:, 0], mem_rows)
    near = gather_near(tokens[0])
    later, near = lax.optimization_barrier(([tokens[b] for b in range(1, batches)], near))
    pieces = [near] + [gather_all(part) for part in later]
    meta_of = [metas[b] for b in range(batches)]

    states = []
    for b in range(batches):
        meta = meta_of[b]
        attended, lse, *chain_rows = attend_forward(
            meta, pieces[b], memory[b], (query_proj, query_bias, key_proj, value_proj, value_bias)
        )
        (
            final, final_mem, payload, mem_grad, mem_stats, own_stats, res_grad, rows,
            attended_low, branch, first_low, inner, active, outer, sums, inner_sum,
        ) = middle(
            meta, attended, lse, tokens[b], memory[b], token_cotangent[b], memory_cotangent[b],
            (
                output_proj, output_bias, attn_gain, attn_shift, inner_proj, inner_bias,
                outer_proj, outer_bias, final_gain, final_shift,
            ),
        )
        if b + 1 < batches:
            meta_of[b + 1], payload = lax.optimization_barrier((meta_of[b + 1], payload))
        states.append(
            dict(
                meta=meta, rows=rows, chain_rows=chain_rows, payload=payload, mem_grad=mem_grad,
                mem_stats=mem_stats, own_stats=own_stats, res_grad=res_grad, final=final,
                final_mem=final_mem, attended_low=attended_low, branch=branch,
                first_low=first_low, inner=inner, active=active, outer=outer, sums=sums,
                inner_sum=inner_sum,
            )
        )

    def over_batches(left, right):
        return weight_grad(
            jnp.concatenate([s[left] for s in states], 0),
            jnp.concatenate([s[right] for s in states], 0),
        ).astype(BF16)

    slots = (jnp.arange(groups)[:, None, None, None, None] == group) & (
        jnp.arange(chains)[:, None, None]
        == jnp.where(metas[:, M_SPOT] == 0, metas[:, M_CHAIN], -1)[:, None, None, None]
    )
    final_mem = jnp.stack([s["final_mem"] for s in states])[None, :, None]
    early = (
        over_batches("first_low", "inner"),
        over_batches("active", "outer"),
        over_batches("attended_low", "branch"),
        jnp.concatenate(
            [
                jnp.where(slots, final_mem, 0).astype(BF16).reshape(-1, width),
                sum(s["sums"] for s in states).astype(BF16),
                sum(s["inner_sum"] for s in states).astype(BF16).reshape(-1, width),
            ],
            0,
        ),
    )
    early, *held = lax.optimization_barrier((early, *[s["meta"] for s in states]))
    for s, meta in zip(states, held):
        s["meta"] = meta
        s["gathered"] = gather_all(s["payload"])
    for s in states:
        s["grads"] = attend_backward(
            s["meta"], s["gathered"], s["chain_rows"], s["mem_grad"], s["mem_stats"],
            s["own_stats"], 0, NQUAD,
        )
        if s is states[0]:
            s["grads"], states[-1]["gathered"], early = lax.optimization_barrier(
                (s["grads"], states[-1]["gathered"], early)
            )
            early = lax.psum(early, ("dp", "blk"))
        s["grads"] = [[grad] for grad in s["grads"]]
    grad_inner, grad_outer, grad_output, rest = early
    late = late_sums(
        metas, group, groups, chains, [s["rows"] for s in states],
        [s["res_grad"] for s in states], [s["grads"] for s in states],
        (query_proj, key_proj, value_proj),
    )

    def own_slots(rows):
        rows = rows.reshape(groups, batches, chains, MEMP, width)
        return lax.dynamic_index_in_dim(rows, group, keepdims=False)[:, :, :mem_rows]

    wide_early = [part.astype(F32) for part in (grad_inner, grad_outer, grad_output)]
    late, (grad_inner, grad_outer, grad_output) = sum_everywhere(late, wide_early)
    grad_query, grad_key, grad_value = (late[i * width : (i + 1) * width] for i in range(3))
    biases = late[3 * width : 3 * width + 2].astype(F32)
    count = groups * batches * chains * MEMP
    memory_grad = own_slots(late[3 * width + 16 : 3 * width + 16 + count])
    memory_out = own_slots(rest[:count])
    sums, inner_sum = rest[count : count + 8], rest[count + 8 :].reshape(1, -1)
    token_outs = [s["final"] for s in states]
    token_grads = []
    for s in states:
        grad = s["res_grad"][:SEG]
        for parts, weights in zip(s["grads"], (query_proj, key_proj, value_proj)):
            first = 0
            for part in parts:
                grad = grad + turned(part[:SEG], weights[:, first : first + part.shape[1]])
                first += part.shape[1]
        token_grads.append(grad.astype(BF16))

    wide = lambda value: value.astype(F32)
    return (
        jnp.stack(token_outs),
        memory_out,
        jnp.stack(token_grads),
        memory_grad,
        wide(grad_query),
        biases[0],
        wide(grad_key),
        wide(grad_value),
        biases[1],
        wide(grad_output),
        wide(sums[0]),
        wide(sums[1]),
        wide(sums[2]),
        wide(grad_inner),
        wide(inner_sum[0]),
        wide(grad_outer),
        wide(sums[3]),
        wide(sums[4]),
        wide(sums[5]),
    )


def solution(mesh):
    row_spec = P(None, ("dp", "blk"), None)
    mem_spec = P(None, "dp", None, None)
    int_spec = P(None, "dp", None)
    in_specs = (row_spec, mem_spec, int_spec, int_spec) + (P(),) * 15 + (row_spec, mem_spec)
    out_specs = (row_spec, mem_spec, row_spec, mem_spec) + (P(),) * 15
    return jax.shard_map(local, mesh=mesh, in_specs=in_specs, out_specs=out_specs, check_vma=False)
```

```python
import functools

import jax
import jax.numpy as jnp
from jax import lax
from jax.experimental import pallas as pl
from jax.experimental.pallas import tpu as pltpu
from jax.sharding import PartitionSpec as P

H = 12
HD = 64
QUAD = 256
NQUAD = 3
PAIR = 128
MEMP = 32
SEG = 512
LONG = 7
NBLK = LONG + 1
CAP = NBLK * SEG
OWN = SEG + MEMP
STAT = 24
BACK_COST = 10_000_000_000
LATE_ROWS = 256
NPIECE = 14
ROWS = 272
COLS = 1024
NEG = -1e30
SHIFT_FREE = 60.0
EPS = 1e-05
F32 = jnp.float32
BF16 = jnp.bfloat16
VMEM_LIMIT = 60 * 2**20
LAST = (((1,), (1,)), ((), ()))

M_LEN, M_ROWS, M_BLOCKS, M_SPOT, M_USED, M_MEM, M_CHAIN, M_START, M_PIECE = range(9)


def plane_moves(shift_of):
    pairs = []
    for plane in range(4):
        for place in range(4):
            target = plane + shift_of(place >> 1)
            if 0 <= target < 4:
                pairs.append((4 * plane + place, 4 * target + place))
    return pairs


UP = plane_moves(lambda side: 1)
DOWN = plane_moves(lambda side: -1)
OUTWARD = plane_moves(lambda side: 1 if side else -1)
SIDE = [(i, i ^ 2) for i in range(16)]
CORE = [(i, i ^ 1) for i in range(16)]


def move(value, pairs):
    return lax.ppermute(value, "blk", pairs)


def gather_near(value):
    steps = near_steps(value)
    parts = next(steps)
    while True:
        try:
            parts = steps.send(parts)
        except StopIteration as done:
            return done.value


def near_steps(value):
    side = (lax.axis_index("blk") >> 1) & 1
    below, above, beside = yield [move(value, pairs) for pairs in (UP, DOWN, SIDE)]
    far = move(jnp.where(side == 1, below, above), OUTWARD)
    moved = [far, move(beside, UP), move(beside, DOWN)]
    cores = [move(part, CORE) for part in (value, beside, below, above)]
    far, beside_below, beside_above, *cores = yield moved + cores
    far = move(far, SIDE)
    far, *more = yield [far] + [move(part, CORE) for part in (beside_below, beside_above)]
    here = [value, beside, below, above, beside_below, beside_above, far]
    return here + cores + more + [move(far, CORE)]


def gather_all(value):
    return [lax.all_gather(value, "blk")]


def piece_of(own, other):
    plane = (other >> 2) - (own >> 2)
    same_side = ((other >> 1) & 1) == ((own >> 1) & 1)
    on_side = jnp.where(plane == 0, 0, jnp.where(plane < 0, 2, 3))
    off_side = jnp.where(plane == 0, 1, jnp.where(plane == -1, 4, jnp.where(plane == 1, 5, 6)))
    index = jnp.where(same_side, on_side, off_side)
    return index + jnp.where((other & 1) == (own & 1), 0, LONG)


def meta_body(own_ref, lengths, fills, meta, *, batches, chains, mem_rows):
    own = own_ref[0]
    for b in range(batches):
        end = jnp.int32(0)
        length, start, fill, chain = (jnp.int32(0) for _ in range(4))
        for c in range(chains):
            begin = end
            end = end + lengths[b, c]
            inside = (begin <= own) & (own < end)
            length = jnp.where(inside, lengths[b, c], length)
            start = jnp.where(inside, begin, start)
            fill = jnp.where(inside, fills[b, c], fill)
            chain = jnp.where(inside, c, chain)
        rows = MEMP + SEG * (length - 1) + fill
        spot = own - start
        meta[b, M_LEN] = length
        meta[b, M_ROWS] = rows
        meta[b, M_BLOCKS] = (rows + SEG - 1) // SEG
        meta[b, M_SPOT] = spot
        meta[b, M_USED] = jnp.where(spot == length - 1, fill, SEG)
        meta[b, M_MEM] = jnp.int32(mem_rows)
        meta[b, M_CHAIN] = chain
        meta[b, M_START] = start
        for place in range(8):
            meta[b, M_PIECE + place] = piece_of(own, start + place)


def metas_of(own, lengths, fills, mem_rows):
    smem = pl.BlockSpec(memory_space=pltpu.SMEM)
    body = functools.partial(
        meta_body, batches=lengths.shape[0], chains=lengths.shape[1], mem_rows=mem_rows
    )
    return pl.pallas_call(
        body,
        in_specs=[smem] * 3,
        out_specs=smem,
        out_shape=jax.ShapeDtypeStruct((lengths.shape[0], 16), jnp.int32),
        name="find_chain",
    )(own.reshape(1), lengths, fills)


def load_chain(meta, pieces, view_from, view_to, sems):
    length = meta[M_LEN]
    for spot in range(LONG):
        def start(source):
            pltpu.make_async_copy(view_from(source), view_to(spot), sems.at[spot]).start()

        @pl.when(spot < length)
        def _():
            if len(pieces) == 1:
                start(pieces[0].at[meta[M_START] + spot])
                return
            for index in range(len(pieces)):
                @pl.when(meta[M_PIECE + spot] == index)
                def _():
                    start(pieces[index])


def wait_chain(meta, pieces, view_from, view_to, sems):
    length = meta[M_LEN]
    source = pieces[0].at[0] if len(pieces) == 1 else pieces[0]
    for spot in range(LONG):
        @pl.when(spot < length)
        def _():
            pltpu.make_async_copy(view_from(source), view_to(spot), sems.at[spot]).wait()


def key_bias(meta):
    column = lax.broadcasted_iota(jnp.int32, (8, CAP), 1)
    dead = (column >= meta[M_ROWS]) | ((column >= meta[M_MEM]) & (column < MEMP))
    return jnp.where(dead, NEG, 0.0).astype(F32)


def by_chunks(blocks, run):
    def four(index, carry):
        run(index * 4, 4)
        return carry

    lax.fori_loop(0, blocks // 4, four, 0)
    for count in (1, 2, 3):
        @pl.when(blocks % 4 == count)
        def _():
            run((blocks // 4) * 4, count)


def span_of(first, count):
    return pl.ds(pl.multiple_of(first * SEG, SEG), count * SEG)


def forward_body(meta, *refs):
    pieces, refs = refs[:-16], refs[-16:]
    mem, wq, wk, wv, bq, bv, out, lse, kc, vc, qc, rows, qown, extended, acc, sems = refs
    quad = pl.program_id(0)
    width = rows.shape[1]
    length, blocks = meta[M_LEN], meta[M_BLOCKS]
    here = lambda source: source
    there = lambda spot: rows.at[pl.ds(MEMP + SEG * spot, SEG)]

    @pl.when(quad == 0)
    def _():
        load_chain(meta, pieces, here, there, sems)
        rows[0:MEMP, :] = mem[meta[M_CHAIN]]
        lse[...] = jnp.zeros_like(lse)

        @pl.when(blocks > length)
        def _():
            place = pl.multiple_of(MEMP + SEG * length, MEMP)
            rows[pl.ds(place, SEG - MEMP), :] = jnp.zeros((SEG - MEMP, width), BF16)

        wait_chain(meta, pieces, here, there, sems)

    def longest(values):
        halves = [
            jnp.max(jnp.sum(jnp.square(values[:, p : p + PAIR]), axis=1, keepdims=True))
            for p in range(0, QUAD, PAIR)
        ]
        return jnp.maximum(*halves)

    def project(start, count):
        span = pl.ds(pl.multiple_of(start, MEMP), count)
        part = rows[span, :]
        row = start + lax.broadcasted_iota(jnp.int32, (count, QUAD), 0)
        alive = (row < meta[M_ROWS]) & ((row < meta[M_MEM]) | (row >= MEMP))
        lower = (lax.broadcasted_iota(jnp.int32, (count, QUAD), 1) % PAIR) < HD
        key = jnp.dot(part, wk[...], preferred_element_type=F32)
        kc[span, :] = key.astype(BF16)
        value = jnp.dot(part, wv[...], preferred_element_type=F32) + bv[...].astype(F32)
        vc[span, :] = value.astype(BF16)
        value = jnp.where(alive, value, 0.0)
        one = jnp.where(alive, 1.0, 0.0)
        extended[0, span, :] = jnp.where(lower, value, one).astype(BF16)
        extended[1, span, :] = jnp.where(lower, one, value).astype(BF16)
        query = jnp.dot(part, wq[...], preferred_element_type=F32) + bq[...].astype(F32)
        query = query.astype(BF16) * jnp.asarray(HD**-0.5, BF16)
        qc[span, :] = query
        return longest(key)

    def project_block(block, top):
        return jnp.maximum(top, project(block * SEG, SEG))

    key_top = lax.fori_loop(0, blocks, project_block, jnp.float32(0.0))

    @pl.when(blocks == length)
    def _():
        project(length * SEG, MEMP)

    place = pl.multiple_of(MEMP + SEG * meta[M_SPOT], MEMP)
    qown[0:SEG, :] = qc[pl.ds(place, SEG), :]
    qown[SEG:OWN, :] = qc[0:MEMP, :]
    near = longest(qown[...].astype(F32)) * key_top <= SHIFT_FREE**2

    def head(index, carry):
        cols = pl.ds(pl.multiple_of((index // 2) * PAIR, PAIR), PAIR)
        half = index % 2
        lane = lax.broadcasted_iota(jnp.int32, (OWN, PAIR), 1)
        mine = (lane // HD) == half
        query = qown[:, cols]
        query = jnp.where(mine, query, jnp.zeros_like(query))
        acc[...] = jnp.zeros_like(acc)
        number = lane == quad * 4 + index

        def score(span):
            return lax.dot_general(query, kc[span, cols], LAST, preferred_element_type=F32)

        def gather(span, terms):
            values = extended[half, span, cols]
            return jnp.dot(terms.astype(BF16), values, preferred_element_type=F32)

        @pl.when(near)
        def _():
            def run(first, count):
                span = span_of(first, count)
                acc[...] += gather(span, jnp.exp(score(span)))

            by_chunks(blocks, run)
            lse[...] = jnp.where(number, 0.0, lse[...])

        @pl.when(jnp.logical_not(near))
        def _():
            def run(block, top):
                span = span_of(block, 1)
                column = block * SEG + lax.broadcasted_iota(jnp.int32, (OWN, SEG), 1)
                dead = (column >= meta[M_ROWS]) | ((column >= meta[M_MEM]) & (column < MEMP))
                scores = jnp.where(dead, NEG, score(span))
                new = jnp.maximum(top, jnp.max(scores, axis=1, keepdims=True))
                acc[...] = acc[...] * jnp.exp(top - new) + gather(span, jnp.exp(scores - new))
                return new

            top = lax.fori_loop(0, blocks, run, jnp.full((OWN, 1), NEG, F32))
            lse[...] = jnp.where(number, top, lse[...])

        sums = acc[...]
        total = jnp.where(mine, pltpu.roll(sums, HD, 1), sums)
        out[:, cols] = jnp.where(mine, sums * (1.0 / total), out[:, cols])
        lse[...] += jnp.where(number, jnp.log(total), 0.0)
        return carry

    lax.fori_loop(0, 4, head, 0)


def attend_forward(meta, pieces, mem, weights):
    wq, bq, wk, wv, bv = weights
    width = wq.shape[0]
    whole = lambda shape: pl.BlockSpec(shape, lambda quad, meta: (0,) * len(shape))
    column = lambda count: pl.BlockSpec((count, QUAD), lambda quad, meta: (0, quad))
    return pl.pallas_call(
        forward_body,
        grid_spec=pltpu.PrefetchScalarGridSpec(
            num_scalar_prefetch=1,
            grid=(NQUAD,),
            in_specs=[pl.BlockSpec(memory_space=pl.ANY)] * len(pieces)
            + [whole((mem.shape[0], MEMP, width))]
            + [column(width)] * 3
            + [column(1)] * 2,
            out_specs=[column(OWN), whole((OWN, PAIR))] + [column(CAP)] * 3,
            scratch_shapes=[
                pltpu.VMEM((CAP, width), BF16),
                pltpu.VMEM((OWN, QUAD), BF16),
                pltpu.VMEM((2, CAP, QUAD), BF16),
                pltpu.VMEM((OWN, PAIR), F32),
                pltpu.SemaphoreType.DMA((LONG,)),
            ],
        ),
        out_shape=[
            jax.ShapeDtypeStruct((OWN, width), F32),
            jax.ShapeDtypeStruct((OWN, PAIR), F32),
        ]
        + [jax.ShapeDtypeStruct((CAP, width), BF16)] * 3,
        compiler_params=pltpu.CompilerParams(vmem_limit_bytes=VMEM_LIMIT),
        cost_estimate=pl.CostEstimate(
            flops=40_000_000_000, bytes_accessed=30_000_000, transcendentals=23_000_000
        ),
        name="attend_forward",
    )(meta, *pieces, mem, wq, wk, wv, bq.reshape(1, -1), bv.reshape(1, -1))


def backward_body(start, count, meta, *refs):
    pieces, refs = refs[:-22], refs[-22:]
    (
        kc, vc, qc, mem_grad, mem_stats, own_stats,
        dq, dk, dv,
        doc, stats, chain_stats, qown, kown, vown, down, bias, qacc, kacc, vacc, sems, stat_sems,
    ) = refs
    step = pl.program_id(0)
    quad = start + step
    length = meta[M_LEN]

    @pl.when(step == 0)
    def _():
        rows_from = lambda index: lambda ref: ref.at[0:SEG, pl.ds((start + index) * QUAD, QUAD)]
        rows_to = lambda index: lambda spot: doc.at[index, pl.ds(MEMP + SEG * spot, SEG)]
        stat_from = lambda ref: ref.at[SEG : SEG + 2 * STAT, 0:SEG]
        stat_to = lambda spot: stats.at[spot]
        load_chain(meta, pieces, stat_from, stat_to, stat_sems)
        for index in range(count):
            load_chain(meta, pieces, rows_from(index), rows_to(index), sems.at[index])
        bias[...] = key_bias(meta)
        for index in range(count):
            doc[index, 0:MEMP, :] = mem_grad[:, (start + index) * QUAD : (start + index + 1) * QUAD]

            @pl.when(meta[M_BLOCKS] > length)
            def _():
                place = pl.multiple_of(MEMP + SEG * length, MEMP)
                doc[index, pl.ds(place, SEG - MEMP), :] = jnp.zeros((SEG - MEMP, QUAD), BF16)

        wait_chain(meta, pieces, stat_from, stat_to, stat_sems)
        for spot in range(NBLK):
            span = slice(SEG * spot, SEG * (spot + 1))
            if spot == LONG:
                chain_stats[:, span] = jnp.zeros((STAT, SEG), F32)
                continue

            @pl.when(spot < length)
            def _():
                pair = stats[spot].astype(F32)
                chain_stats[:, span] = pair[0:STAT] + pair[STAT : 2 * STAT]

            @pl.when(spot >= length)
            def _():
                chain_stats[:, span] = jnp.zeros((STAT, SEG), F32)

        moved = pltpu.roll(chain_stats[...], MEMP, 1)
        column = lax.broadcasted_iota(jnp.int32, (STAT, CAP), 1)
        entry = lax.broadcasted_iota(jnp.int32, (STAT, CAP), 0)
        beyond = jnp.where(entry < H, -NEG, 0.0)
        chain_stats[...] = jnp.where(column < MEMP + SEG * length, moved, beyond)
        lane = lax.broadcasted_iota(jnp.int32, (STAT, PAIR), 1)
        at_front = pltpu.roll(mem_stats[...], MEMP, 1)
        chain_stats[:, 0:PAIR] = jnp.where(lane < MEMP, at_front, chain_stats[:, 0:PAIR])
        for index in range(count):
            wait_chain(meta, pieces, rows_from(index), rows_to(index), sems.at[index])

    place = pl.multiple_of(MEMP + SEG * meta[M_SPOT], MEMP)
    for own, chain in ((qown, qc), (kown, kc), (vown, vc), (down, doc.at[step])):
        own[0:SEG, :] = chain[pl.ds(place, SEG), :]
        own[SEG:OWN, :] = chain[0:MEMP, :]

    def head(index, carry):
        cols = pl.ds(pl.multiple_of((index // 2) * PAIR, PAIR), PAIR)
        number = quad * 4 + index
        lane = lax.broadcasted_iota(jnp.int32, (OWN, PAIR), 1)
        mine = (lane // HD) == (index % 2)
        masked = lambda ref: jnp.where(mine, ref[:, cols], jnp.zeros((OWN, PAIR), BF16))
        query, key, value, grad = masked(qown), masked(kown), masked(vown), masked(down)
        pick = lambda at: jnp.sum(jnp.where(lane == at, own_stats[...], 0.0), axis=1, keepdims=True)
        log_total, delta = pick(number), pick(H + number)
        for acc in (qacc, kacc, vacc):
            acc[...] = jnp.zeros_like(acc)

        def run(first, size):
            span = span_of(first, size)
            keys, values = kc[span, cols], vc[span, cols]
            scores = lax.dot_general(query, keys, LAST, preferred_element_type=F32)
            weights = jnp.exp(scores + bias[0:1, span] - log_total)
            weight_grad = lax.dot_general(grad, values, LAST, preferred_element_type=F32)
            score_grad = (weights * (weight_grad - delta)).astype(BF16)
            qacc[...] += jnp.dot(score_grad, keys, preferred_element_type=F32)

            queries, grads = qc[span, cols], doc[step, span, cols]
            scores = lax.dot_general(key, queries, LAST, preferred_element_type=F32)
            weights = jnp.exp(scores - chain_stats[pl.ds(number, 1), span])
            weight_grad = lax.dot_general(value, grads, LAST, preferred_element_type=F32)
            score_grad = (
                weights * (weight_grad - chain_stats[pl.ds(H + number, 1), span])
            ).astype(BF16)
            vacc[...] += jnp.dot(weights.astype(BF16), grads, preferred_element_type=F32)
            kacc[...] += jnp.dot(score_grad, queries, preferred_element_type=F32)

        by_chunks(meta[M_BLOCKS], run)
        row = lax.broadcasted_iota(jnp.int32, (OWN, PAIR), 0)
        alive = (row < meta[M_USED]) | ((row >= SEG) & (row < SEG + meta[M_MEM]))
        query_sum = qacc[...] * (HD**-0.5)
        key_sum = jnp.where(alive, kacc[...], 0.0)
        value_sum = jnp.where(alive, vacc[...], 0.0)
        for ref, sums in ((dq, query_sum), (dk, key_sum), (dv, value_sum)):
            ref[:, cols] = jnp.where(mine, sums.astype(BF16), ref[:, cols])
        return carry

    lax.fori_loop(0, 4, head, 0)


def attend_backward(meta, pieces, chain, mem_grad, mem_stats, own_stats, start, count):
    width = mem_grad.shape[1]
    whole = lambda shape: pl.BlockSpec(shape, lambda quad, meta: (0,) * len(shape))
    chain_column = pl.BlockSpec((CAP, QUAD), lambda step, meta: (0, start + step))
    own_column = pl.BlockSpec((OWN, QUAD), lambda step, meta: (0, step))
    return pl.pallas_call(
        functools.partial(backward_body, start, count),
        grid_spec=pltpu.PrefetchScalarGridSpec(
            num_scalar_prefetch=1,
            grid=(count,),
            in_specs=[pl.BlockSpec(memory_space=pl.ANY)] * len(pieces)
            + [chain_column] * 3
            + [whole((MEMP, width)), whole((STAT, PAIR)), whole((OWN, PAIR))],
            out_specs=[own_column] * 3,
            scratch_shapes=[
                pltpu.VMEM((count, CAP, QUAD), BF16),
                pltpu.VMEM((LONG, 2 * STAT, SEG), BF16),
                pltpu.VMEM((STAT, CAP), F32),
            ]
            + [pltpu.VMEM((OWN, QUAD), BF16)] * 4
            + [
                pltpu.VMEM((8, CAP), F32),
                pltpu.VMEM((OWN, PAIR), F32),
                pltpu.VMEM((OWN, PAIR), F32),
                pltpu.VMEM((OWN, PAIR), F32),
                pltpu.SemaphoreType.DMA((count, LONG)),
                pltpu.SemaphoreType.DMA((LONG,)),
            ],
        ),
        out_shape=[jax.ShapeDtypeStruct((OWN, count * QUAD), BF16)] * 3,
        compiler_params=pltpu.CompilerParams(vmem_limit_bytes=VMEM_LIMIT),
        cost_estimate=pl.CostEstimate(
            flops=BACK_COST, bytes_accessed=1_000_000, transcendentals=0
        ),
        name="attend_backward",
    )(meta, *pieces, *chain, mem_grad, mem_stats, own_stats)


def norm_stats(values):
    centered = values - jnp.mean(values, axis=-1, keepdims=True)
    scale = lax.rsqrt(jnp.mean(centered * centered, axis=-1, keepdims=True) + EPS)
    return centered * scale, scale


def norm_back(normed, scale, upstream):
    mean = jnp.mean(upstream, axis=-1, keepdims=True)
    along = jnp.mean(upstream * normed, axis=-1, keepdims=True)
    return scale * (upstream - mean - normed * along)


def turned(left, right):
    return lax.dot_general(left, right, LAST, preferred_element_type=F32)


def crossed(left, right):
    return lax.dot_general(left, right, (((0,), (0,)), ((), ())), preferred_element_type=F32)


def middle_body(
    meta, attended, lse, tokens, memory, token_cot, memory_cot,
    wo, bo, gain1, shift1, bi, b2, gain2, shift2, wi_from, w2_from,
    final, final_mem, payload, mem_grad, mem_stats, own_stats, res_grad, rows,
    attended_low, branch_out, first_low, inner_out, active, outer_out, sums, inner_sum,
    wi, w2, first, norm1, scale1, total, second_grad, outer_grad, slope, cots, weight_sems,
):
    width, inner_width = wi.shape
    wi_copy = pltpu.make_async_copy(wi_from, wi, weight_sems.at[0])
    w2_copy = pltpu.make_async_copy(w2_from, w2, weight_sems.at[1])
    wi_copy.start()
    w2_copy.start()
    chain = meta[M_CHAIN]
    lead = jnp.where(meta[M_SPOT] == 0, 1.0, 0.0)
    rows[0:SEG, :] = tokens[...]
    rows[SEG:OWN, :] = memory[chain]
    cots[0:SEG, :] = token_cot[...]
    cots[SEG:OWN, :] = memory_cot[chain]
    attended_low[...] = attended[...].astype(BF16)
    total[...] = jnp.dot(attended_low[...], wo[...], preferred_element_type=F32)
    sums[...] = jnp.zeros_like(sums)
    inner_sum[...] = jnp.zeros_like(inner_sum)
    vector = lambda ref: ref[...].astype(F32)

    def by_rows(run):
        def step(index, carry):
            start = pl.multiple_of(index * ROWS, ROWS)
            row = start + lax.broadcasted_iota(jnp.int32, (ROWS, 1), 0)
            live = (row < meta[M_USED]) | ((row >= SEG) & (row < SEG + meta[M_MEM]))
            counted = jnp.where(row < SEG, 1.0, lead)
            run(pl.ds(start, ROWS), live, counted)
            return carry

        lax.fori_loop(0, OWN // ROWS, step, 0)

    def by_columns(run):
        def step(index, carry):
            run(pl.ds(pl.multiple_of(index * COLS, COLS), COLS))
            return carry

        lax.fori_loop(0, inner_width // COLS, step, 0)

    def add(place, value):
        sums[place : place + 1, :] += jnp.sum(value, axis=0, keepdims=True)

    def first_part(span, live, counted):
        value = rows[span, :].astype(F32) + total[span, :] + vector(bo)
        normed, scale = norm_stats(value)
        norm1[span, :] = normed
        scale1[span, :] = jnp.broadcast_to(scale, (ROWS, PAIR))
        value = normed * vector(gain1) + vector(shift1)
        first[span, :] = value
        first_low[span, :] = value.astype(BF16)

    by_rows(first_part)
    wi_copy.wait()
    w2_copy.wait()
    total[...] = jnp.zeros_like(total)

    def inner_part(cols):
        inner = jnp.dot(first_low[...], wi[:, cols], preferred_element_type=F32)
        inner = inner + bi[:, cols].astype(F32)
        cdf = 0.5 * (1.0 + lax.erf(inner * (2.0**-0.5)))
        density = jnp.exp(-0.5 * inner * inner) * 0.3989422804014327
        slope[:, cols] = cdf + inner * density
        low = (inner * cdf).astype(BF16)
        active[:, cols] = low
        total[...] += jnp.dot(low, w2[cols, :], preferred_element_type=F32)

    by_columns(inner_part)

    def final_part(span, live, counted):
        normed, scale = norm_stats(first[span, :] + total[span, :] + vector(b2))
        value = jnp.where(live, normed * vector(gain2) + vector(shift2), 0.0)
        rows_low = value.astype(BF16)
        outer_out[span, :] = rows_low
        cot = cots[span, :].astype(F32)
        cot = jnp.where(live, cot, 0.0)
        weighted = cot * counted
        add(4, weighted * normed)
        add(5, weighted)
        grad = norm_back(normed, scale, cot * vector(gain2))
        second_grad[span, :] = grad
        outer_grad[span, :] = grad.astype(BF16)
        add(3, grad.astype(BF16).astype(F32) * counted)

    by_rows(final_part)
    final[...] = outer_out[0:SEG, :]
    final_mem[...] = outer_out[SEG:OWN, :]
    outer_out[0:SEG, :] = outer_grad[0:SEG, :]
    outer_out[SEG:OWN, :] = outer_grad[SEG:OWN, :] * lead.astype(BF16)
    total[...] = jnp.zeros_like(total)

    def inner_back(cols):
        grad = (turned(outer_grad[...], w2[cols, :]) * slope[:, cols]).astype(BF16)
        total[...] += turned(grad, wi[:, cols])
        tail = grad[SEG:OWN] * lead.astype(BF16)
        inner_out[0:SEG, cols] = grad[0:SEG]
        inner_out[SEG:OWN, cols] = tail
        inner_sum[:, cols] = jnp.sum(grad[0:SEG].astype(F32), axis=0, keepdims=True) + jnp.sum(
            tail.astype(F32), axis=0, keepdims=True
        )

    by_columns(inner_back)

    def last_part(span, live, counted):
        grad = second_grad[span, :] + total[span, :]
        normed = norm1[span, :]
        weighted = grad * counted
        add(1, weighted * normed)
        add(2, weighted)
        grad = norm_back(normed, scale1[span, 0:1], grad * vector(gain1))
        res_grad[span, :] = grad
        low = grad.astype(BF16)
        outer_grad[span, :] = low
        low = (low.astype(F32) * counted).astype(BF16)
        branch_out[span, :] = low
        add(0, low.astype(F32))

    by_rows(last_part)
    total[...] = turned(outer_grad[...], wo[...])
    feature = lax.broadcasted_iota(jnp.int32, (width, PAIR), 0)
    lane = lax.broadcasted_iota(jnp.int32, (width, PAIR), 1)
    head_of = jnp.where(feature // HD == lane - H, 1.0, 0.0).astype(BF16)

    def delta_part(span, live, counted):
        low = total[span, :].astype(BF16)
        outer_grad[span, :] = low
        product = low.astype(F32) * attended[span, :]
        high = product.astype(BF16)
        rest = (product - high.astype(F32)).astype(BF16)
        delta = jnp.dot(high, head_of, preferred_element_type=F32)
        delta = delta + jnp.dot(rest, head_of, preferred_element_type=F32)
        own_stats[span, :] = lse[span, :] + delta

    by_rows(delta_part)
    payload[0:SEG, :] = outer_grad[0:SEG, :]
    mem_grad[...] = outer_grad[SEG:OWN, :]
    stats = jnp.transpose(own_stats[0:SEG, :])[0:STAT]
    high = stats.astype(BF16)
    rest = (stats - high.astype(F32)).astype(BF16)
    both = jnp.concatenate([high.astype(F32), rest.astype(F32)], 0).astype(BF16)
    payload[SEG : SEG + 2 * STAT, 0:SEG] = both
    payload[SEG : SEG + 2 * STAT, SEG:width] = jnp.zeros((2 * STAT, width - SEG), BF16)
    mem_stats[...] = jnp.transpose(own_stats[OWN - PAIR : OWN, :])[0:STAT]


def middle(meta, attended, lse, tokens, memory, token_cot, memory_cot, weights):
    wo, bo, gain1, shift1, wi, bi, w2, b2, gain2, shift2 = weights
    width, inner_width = wi.shape
    vmem, line = pl.BlockSpec(memory_space=pltpu.VMEM), lambda value: value.reshape(1, -1)
    hbm = pl.BlockSpec(memory_space=pl.ANY)
    shape = jax.ShapeDtypeStruct
    return pl.pallas_call(
        middle_body,
        in_specs=[pl.BlockSpec(memory_space=pltpu.SMEM)] + [vmem] * 14 + [hbm] * 2,
        out_specs=[vmem] * 16,
        out_shape=[
            shape((SEG, width), BF16),
            shape((MEMP, width), BF16),
            shape((SEG + 2 * STAT, width), BF16),
            shape((MEMP, width), BF16),
            shape((STAT, PAIR), F32),
            shape((OWN, PAIR), F32),
            shape((OWN, width), F32),
            shape((OWN, width), BF16),
            shape((OWN, width), BF16),
            shape((OWN, width), BF16),
            shape((OWN, width), BF16),
            shape((OWN, inner_width), BF16),
            shape((OWN, inner_width), BF16),
            shape((OWN, width), BF16),
            shape((8, width), F32),
            shape((1, inner_width), F32),
        ],
        scratch_shapes=[
            pltpu.VMEM((width, inner_width), BF16),
            pltpu.VMEM((inner_width, width), BF16),
            pltpu.VMEM((OWN, width), F32),
            pltpu.VMEM((OWN, width), F32),
            pltpu.VMEM((OWN, PAIR), F32),
            pltpu.VMEM((OWN, width), F32),
            pltpu.VMEM((OWN, width), F32),
            pltpu.VMEM((OWN, width), BF16),
            pltpu.VMEM((OWN, inner_width), F32),
            pltpu.VMEM((OWN, width), BF16),
            pltpu.SemaphoreType.DMA((2,)),
        ],
        compiler_params=pltpu.CompilerParams(vmem_limit_bytes=VMEM_LIMIT),
        cost_estimate=pl.CostEstimate(
            flops=12_000_000_000, bytes_accessed=40_000_000, transcendentals=2_000_000
        ),
        name="middle",
    )(
        meta, attended, lse, tokens, memory, token_cot, memory_cot,
        wo, line(bo), line(gain1), line(shift1), line(bi), line(b2), line(gain2), line(shift2),
        wi, w2,
    )


def late_body(metas, group, *refs, batches, chains, parts):
    refs = list(refs)
    take = lambda count: [refs.pop(0) for _ in range(count)]
    rows, res_mem = take(batches), take(batches)
    grads = [[take(len(parts[b])) for _ in range(3)] for b in range(batches)]
    weights = take(3)
    out, masked = take(2)
    width = weights[0].shape[0]
    out[3 * width :, :] = jnp.zeros((out.shape[0] - 3 * width, width), BF16)
    for b in range(batches):
        lead = jnp.where(metas[b, M_SPOT] == 0, 1.0, 0.0)
        masked[b, 0:SEG, :] = rows[b][0:SEG, :]
        masked[b, SEG:OWN, :] = rows[b][SEG:OWN, :] * lead.astype(BF16)
        grad = res_mem[b][SEG:OWN, :]
        for k in range(3):
            first = 0
            for part, ref in zip(parts[b], grads[b][k]):
                grad = grad + turned(ref[SEG:OWN, :], weights[k][:, first : first + part])
                first += part
        place = ((group[0] * batches + b) * chains + metas[b, M_CHAIN]) * MEMP
        place = pl.multiple_of(3 * width + 16 + place, 16)
        out[pl.ds(place, MEMP), :] = (grad * lead).astype(BF16)
    cuts = sorted({sum(p[:i]) for p in parts for i in range(len(p) + 1)})
    for k in range(3):
        for low, high in zip(cuts[:-1], cuts[1:]):
            total, line = None, None
            for b in range(batches):
                lead = jnp.where(metas[b, M_SPOT] == 0, 1.0, 0.0)
                first = 0
                for part, ref in zip(parts[b], grads[b][k]):
                    if first <= low and high <= first + part:
                        grad = ref[:, low - first : high - first]
                    first += part
                value = crossed(masked[b], grad)
                total = value if total is None else total + value
                if k != 1:
                    grad = grad.astype(F32)
                    value = jnp.sum(grad[0:SEG], 0, keepdims=True)
                    value = value + jnp.sum(grad[SEG:OWN], 0, keepdims=True) * lead
                    line = value if line is None else line + value
            out[k * width : (k + 1) * width, low:high] = total.astype(BF16)
            if k != 1:
                row = lax.broadcasted_iota(jnp.int32, (16, high - low), 0)
                span = slice(3 * width, 3 * width + 16)
                old = out[span, low:high].astype(F32)
                out[span, low:high] = jnp.where(row == k // 2, line, old).astype(BF16)


def late_sums(metas, group, groups, chains, rows, res, grads, weights):
    batches, width = len(rows), weights[0].shape[0]
    parts = [[part.shape[1] for part in one[0]] for one in grads]
    count = 3 * width + 16 + groups * batches * chains * MEMP
    count += -count % LATE_ROWS
    vmem, smem = pl.BlockSpec(memory_space=pltpu.VMEM), pl.BlockSpec(memory_space=pltpu.SMEM)
    flat = [part for one in grads for name in one for part in name]
    return pl.pallas_call(
        functools.partial(late_body, batches=batches, chains=chains, parts=parts),
        in_specs=[smem] * 2 + [vmem] * (2 * batches + len(flat) + 3),
        out_specs=vmem,
        out_shape=jax.ShapeDtypeStruct((count, width), BF16),
        scratch_shapes=[pltpu.VMEM((batches, OWN, width), BF16)],
        compiler_params=pltpu.CompilerParams(vmem_limit_bytes=VMEM_LIMIT),
        name="late_sums",
    )(metas, group.reshape(1), *rows, *res, *flat, *weights)


def weight_grad(left, right):
    return lax.dot_general(left, right, (((0,), (0,)), ((), ())), preferred_element_type=F32)


def swap(value, mask):
    sizes = lax.axis_size("dp") * lax.axis_size("blk")
    return lax.ppermute(value, ("dp", "blk"), [(i, i ^ mask) for i in range(sizes)])


def sum_everywhere(value, beside):
    blk = lax.axis_size("blk")
    place = lax.axis_index("dp") * blk + lax.axis_index("blk")
    groups = [(1,), (2, blk), (4, 8)]
    bit = 2 * blk
    while bit < blk * lax.axis_size("dp"):
        groups.append((bit,))
        bit *= 2
    masks_of = lambda group: [
        sum(bit for i, bit in enumerate(group) if (k >> i) & 1) for k in range(1 << len(group))
    ]
    own_of = lambda group: sum(((place // bit) % 2) << i for i, bit in enumerate(group))
    for group in groups:
        masks, own = masks_of(group), own_of(group)
        size = value.shape[0] // len(masks)
        part = lambda k: lax.dynamic_slice_in_dim(value, (own ^ k) * size, size)
        got = [swap(part(k), mask) for k, mask in enumerate(masks) if k]
        value = sum((g.astype(F32) for g in got), part(0).astype(F32)).astype(BF16)
    for index, group in enumerate(reversed(groups)):
        if index == 1:
            value, beside = lax.optimization_barrier((value, beside))
        masks, own = masks_of(group), own_of(group)
        size = value.shape[0]
        got = [value] + [swap(value, mask) for mask in masks[1:]]
        value = jnp.zeros((size * len(masks), value.shape[1]), BF16)
        for k, part in enumerate(got):
            value = lax.dynamic_update_slice_in_dim(value, part, (own ^ k) * size, 0)
    return value, beside


def local(
    tokens, memory, chain_lengths, last_fill,
    query_proj, query_bias, key_proj, value_proj, value_bias, output_proj, output_bias,
    attn_gain, attn_shift, inner_proj, inner_bias, outer_proj, outer_bias,
    final_gain, final_shift, token_cotangent, memory_cotangent,
):
    own = lax.axis_index("blk").astype(jnp.int32)
    group = lax.axis_index("dp").astype(jnp.int32)
    groups = lax.axis_size("dp")
    batches, _, width = tokens.shape
    chains, mem_rows = memory.shape[1:3]
    pad_mem = ((0, 0), (0, 0), (0, MEMP - mem_rows), (0, 0))
    memory, memory_cotangent = jnp.pad(memory, pad_mem), jnp.pad(memory_cotangent, pad_mem)

    metas = metas_of(own, chain_lengths[:, 0], last_fill[:, 0], mem_rows)
    near = gather_near(tokens[0])
    later, near = lax.optimization_barrier(([tokens[b] for b in range(1, batches)], near))
    pieces = [near] + [gather_all(part) for part in later]
    meta_of = [metas[b] for b in range(batches)]

    states = []
    for b in range(batches):
        meta = meta_of[b]
        attended, lse, *chain_rows = attend_forward(
            meta, pieces[b], memory[b], (query_proj, query_bias, key_proj, value_proj, value_bias)
        )
        if b == 1:
            attended, parts = lax.optimization_barrier((attended, parts))
            parts = steps.send(parts)
        (
            final, final_mem, payload, mem_grad, mem_stats, own_stats, res_grad, rows,
            attended_low, branch, first_low, inner, active, outer, sums, inner_sum,
        ) = middle(
            meta, attended, lse, tokens[b], memory[b], token_cotangent[b], memory_cotangent[b],
            (
                output_proj, output_bias, attn_gain, attn_shift, inner_proj, inner_bias,
                outer_proj, outer_bias, final_gain, final_shift,
            ),
        )
        if b + 1 < batches:
            meta_of[b + 1], payload = lax.optimization_barrier((meta_of[b + 1], payload))
        if b == 0:
            steps = near_steps(payload)
            parts = next(steps)
        if b == 1:
            payload, parts = lax.optimization_barrier((payload, parts))
            parts = steps.send(parts)
        states.append(
            dict(
                meta=meta, rows=rows, chain_rows=chain_rows, payload=payload, mem_grad=mem_grad,
                mem_stats=mem_stats, own_stats=own_stats, res_grad=res_grad, final=final,
                final_mem=final_mem, attended_low=attended_low, branch=branch,
                first_low=first_low, inner=inner, active=active, outer=outer, sums=sums,
                inner_sum=inner_sum,
            )
        )

    def over_batches(left, right):
        return weight_grad(
            jnp.concatenate([s[left] for s in states], 0),
            jnp.concatenate([s[right] for s in states], 0),
        ).astype(BF16)

    slots = (jnp.arange(groups)[:, None, None, None, None] == group) & (
        jnp.arange(chains)[:, None, None]
        == jnp.where(metas[:, M_SPOT] == 0, metas[:, M_CHAIN], -1)[:, None, None, None]
    )
    final_mem = jnp.stack([s["final_mem"] for s in states])[None, :, None]
    early = (
        over_batches("first_low", "inner"),
        over_batches("active", "outer"),
        over_batches("attended_low", "branch"),
        jnp.concatenate(
            [
                jnp.where(slots, final_mem, 0).astype(BF16).reshape(-1, width),
                sum(s["sums"] for s in states).astype(BF16),
                sum(s["inner_sum"] for s in states).astype(BF16).reshape(-1, width),
            ],
            0,
        ),
    )
    early, parts, *held = lax.optimization_barrier((early, parts, *[s["meta"] for s in states]))
    for s, meta in zip(states, held):
        s["meta"] = meta
        if s is not states[0]:
            s["gathered"] = gather_all(s["payload"])
    try:
        steps.send(parts)
    except StopIteration as done:
        states[0]["gathered"] = done.value
    for s in states:
        s["grads"] = attend_backward(
            s["meta"], s["gathered"], s["chain_rows"], s["mem_grad"], s["mem_stats"],
            s["own_stats"], 0, NQUAD,
        )
        if s is states[0]:
            s["grads"], states[-1]["gathered"], early = lax.optimization_barrier(
                (s["grads"], states[-1]["gathered"], early)
            )
            early = lax.psum(early, ("dp", "blk"))
        s["grads"] = [[grad] for grad in s["grads"]]
    grad_inner, grad_outer, grad_output, rest = early
    late = late_sums(
        metas, group, groups, chains, [s["rows"] for s in states],
        [s["res_grad"] for s in states], [s["grads"] for s in states],
        (query_proj, key_proj, value_proj),
    )

    def own_slots(rows):
        rows = rows.reshape(groups, batches, chains, MEMP, width)
        return lax.dynamic_index_in_dim(rows, group, keepdims=False)[:, :, :mem_rows]

    wide_early = [part.astype(F32) for part in (grad_inner, grad_outer, grad_output)]
    late, (grad_inner, grad_outer, grad_output) = sum_everywhere(late, wide_early)
    grad_query, grad_key, grad_value = (late[i * width : (i + 1) * width] for i in range(3))
    biases = late[3 * width : 3 * width + 2].astype(F32)
    count = groups * batches * chains * MEMP
    memory_grad = own_slots(late[3 * width + 16 : 3 * width + 16 + count])
    memory_out = own_slots(rest[:count])
    sums, inner_sum = rest[count : count + 8], rest[count + 8 :].reshape(1, -1)
    token_outs = [s["final"] for s in states]
    token_grads = []
    for s in states:
        grad = s["res_grad"][:SEG]
        for parts, weights in zip(s["grads"], (query_proj, key_proj, value_proj)):
            first = 0
            for part in parts:
                grad = grad + turned(part[:SEG], weights[:, first : first + part.shape[1]])
                first += part.shape[1]
        token_grads.append(grad.astype(BF16))

    wide = lambda value: value.astype(F32)
    return (
        jnp.stack(token_outs),
        memory_out,
        jnp.stack(token_grads),
        memory_grad,
        wide(grad_query),
        biases[0],
        wide(grad_key),
        wide(grad_value),
        biases[1],
        wide(grad_output),
        wide(sums[0]),
        wide(sums[1]),
        wide(sums[2]),
        wide(grad_inner),
        wide(inner_sum[0]),
        wide(grad_outer),
        wide(sums[3]),
        wide(sums[4]),
        wide(sums[5]),
    )


def solution(mesh):
    row_spec = P(None, ("dp", "blk"), None)
    mem_spec = P(None, "dp", None, None)
    int_spec = P(None, "dp", None)
    in_specs = (row_spec, mem_spec, int_spec, int_spec) + (P(),) * 15 + (row_spec, mem_spec)
    out_specs = (row_spec, mem_spec, row_spec, mem_spec) + (P(),) * 15
    return jax.shard_map(local, mesh=mesh, in_specs=in_specs, out_specs=out_specs, check_vma=False)
```

```python
import functools

import jax
import jax.numpy as jnp
from jax import lax
from jax.experimental import pallas as pl
from jax.experimental.pallas import tpu as pltpu
from jax.sharding import PartitionSpec as P

H = 12
HD = 64
QUAD = 256
NQUAD = 3
PAIR = 128
MEMP = 32
SEG = 512
LONG = 7
NBLK = LONG + 1
CAP = NBLK * SEG
OWN = SEG + MEMP
STAT = 24
BACK_COST = 10_000_000_000
LATE_ROWS = 256
NPIECE = 14
ROWS = 272
COLS = 1024
NEG = -1e30
SHIFT_FREE = 60.0
EPS = 1e-05
F32 = jnp.float32
BF16 = jnp.bfloat16
VMEM_LIMIT = 60 * 2**20
LAST = (((1,), (1,)), ((), ()))

M_LEN, M_ROWS, M_BLOCKS, M_SPOT, M_USED, M_MEM, M_CHAIN, M_START, M_PIECE = range(9)


def plane_moves(shift_of):
    pairs = []
    for plane in range(4):
        for place in range(4):
            target = plane + shift_of(place >> 1)
            if 0 <= target < 4:
                pairs.append((4 * plane + place, 4 * target + place))
    return pairs


UP = plane_moves(lambda side: 1)
DOWN = plane_moves(lambda side: -1)
OUTWARD = plane_moves(lambda side: 1 if side else -1)
SIDE = [(i, i ^ 2) for i in range(16)]
CORE = [(i, i ^ 1) for i in range(16)]


def move(value, pairs):
    return lax.ppermute(value, "blk", pairs)


def gather_near(value):
    side = (lax.axis_index("blk") >> 1) & 1
    below, above, beside = move(value, UP), move(value, DOWN), move(value, SIDE)
    far = move(jnp.where(side == 1, below, above), OUTWARD)
    moved = [move(beside, UP), move(beside, DOWN), move(far, SIDE)]
    here = [value, beside, below, above] + moved
    return here + [move(part, CORE) for part in here]


def gather_all(value):
    return [lax.all_gather(value, "blk")]


def piece_of(own, other):
    plane = (other >> 2) - (own >> 2)
    same_side = ((other >> 1) & 1) == ((own >> 1) & 1)
    on_side = jnp.where(plane == 0, 0, jnp.where(plane < 0, 2, 3))
    off_side = jnp.where(plane == 0, 1, jnp.where(plane == -1, 4, jnp.where(plane == 1, 5, 6)))
    index = jnp.where(same_side, on_side, off_side)
    return index + jnp.where((other & 1) == (own & 1), 0, LONG)


def meta_body(own_ref, lengths, fills, meta, *, batches, chains, mem_rows):
    own = own_ref[0]
    for b in range(batches):
        end = jnp.int32(0)
        length, start, fill, chain = (jnp.int32(0) for _ in range(4))
        for c in range(chains):
            begin = end
            end = end + lengths[b, c]
            inside = (begin <= own) & (own < end)
            length = jnp.where(inside, lengths[b, c], length)
            start = jnp.where(inside, begin, start)
            fill = jnp.where(inside, fills[b, c], fill)
            chain = jnp.where(inside, c, chain)
        rows = MEMP + SEG * (length - 1) + fill
        spot = own - start
        meta[b, M_LEN] = length
        meta[b, M_ROWS] = rows
        meta[b, M_BLOCKS] = (rows + SEG - 1) // SEG
        meta[b, M_SPOT] = spot
        meta[b, M_USED] = jnp.where(spot == length - 1, fill, SEG)
        meta[b, M_MEM] = jnp.int32(mem_rows)
        meta[b, M_CHAIN] = chain
        meta[b, M_START] = start
        for place in range(8):
            meta[b, M_PIECE + place] = piece_of(own, start + place)


def metas_of(own, lengths, fills, mem_rows):
    smem = pl.BlockSpec(memory_space=pltpu.SMEM)
    body = functools.partial(
        meta_body, batches=lengths.shape[0], chains=lengths.shape[1], mem_rows=mem_rows
    )
    return pl.pallas_call(
        body,
        in_specs=[smem] * 3,
        out_specs=smem,
        out_shape=jax.ShapeDtypeStruct((lengths.shape[0], 16), jnp.int32),
        name="find_chain",
    )(own.reshape(1), lengths, fills)


def load_chain(meta, pieces, view_from, view_to, sems):
    length = meta[M_LEN]
    for spot in range(LONG):
        def start(source):
            pltpu.make_async_copy(view_from(source), view_to(spot), sems.at[spot]).start()

        @pl.when(spot < length)
        def _():
            if len(pieces) == 1:
                start(pieces[0].at[meta[M_START] + spot])
                return
            for index in range(len(pieces)):
                @pl.when(meta[M_PIECE + spot] == index)
                def _():
                    start(pieces[index])


def wait_chain(meta, pieces, view_from, view_to, sems):
    length = meta[M_LEN]
    source = pieces[0].at[0] if len(pieces) == 1 else pieces[0]
    for spot in range(LONG):
        @pl.when(spot < length)
        def _():
            pltpu.make_async_copy(view_from(source), view_to(spot), sems.at[spot]).wait()


def key_bias(meta):
    column = lax.broadcasted_iota(jnp.int32, (8, CAP), 1)
    dead = (column >= meta[M_ROWS]) | ((column >= meta[M_MEM]) & (column < MEMP))
    return jnp.where(dead, NEG, 0.0).astype(F32)


def by_chunks(blocks, run):
    def four(index, carry):
        run(index * 4, 4)
        return carry

    lax.fori_loop(0, blocks // 4, four, 0)
    for count in (1, 2, 3):
        @pl.when(blocks % 4 == count)
        def _():
            run((blocks // 4) * 4, count)


def span_of(first, count):
    return pl.ds(pl.multiple_of(first * SEG, SEG), count * SEG)


def forward_body(meta, *refs):
    pieces, refs = refs[:-16], refs[-16:]
    mem, wq, wk, wv, bq, bv, out, lse, kc, vc, qc, rows, qown, extended, acc, sems = refs
    quad = pl.program_id(0)
    width = rows.shape[1]
    length, blocks = meta[M_LEN], meta[M_BLOCKS]
    here = lambda source: source
    there = lambda spot: rows.at[pl.ds(MEMP + SEG * spot, SEG)]

    @pl.when(quad == 0)
    def _():
        load_chain(meta, pieces, here, there, sems)
        rows[0:MEMP, :] = mem[meta[M_CHAIN]]
        lse[...] = jnp.zeros_like(lse)

        @pl.when(blocks > length)
        def _():
            place = pl.multiple_of(MEMP + SEG * length, MEMP)
            rows[pl.ds(place, SEG - MEMP), :] = jnp.zeros((SEG - MEMP, width), BF16)

        wait_chain(meta, pieces, here, there, sems)

    def longest(values):
        halves = [
            jnp.max(jnp.sum(jnp.square(values[:, p : p + PAIR]), axis=1, keepdims=True))
            for p in range(0, QUAD, PAIR)
        ]
        return jnp.maximum(*halves)

    def project(start, count):
        span = pl.ds(pl.multiple_of(start, MEMP), count)
        part = rows[span, :]
        row = start + lax.broadcasted_iota(jnp.int32, (count, QUAD), 0)
        alive = (row < meta[M_ROWS]) & ((row < meta[M_MEM]) | (row >= MEMP))
        lower = (lax.broadcasted_iota(jnp.int32, (count, QUAD), 1) % PAIR) < HD
        key = jnp.dot(part, wk[...], preferred_element_type=F32)
        kc[span, :] = key.astype(BF16)
        value = jnp.dot(part, wv[...], preferred_element_type=F32) + bv[...].astype(F32)
        vc[span, :] = value.astype(BF16)
        value = jnp.where(alive, value, 0.0)
        one = jnp.where(alive, 1.0, 0.0)
        extended[0, span, :] = jnp.where(lower, value, one).astype(BF16)
        extended[1, span, :] = jnp.where(lower, one, value).astype(BF16)
        query = jnp.dot(part, wq[...], preferred_element_type=F32) + bq[...].astype(F32)
        query = query.astype(BF16) * jnp.asarray(HD**-0.5, BF16)
        qc[span, :] = query
        return longest(key)

    def project_block(block, top):
        return jnp.maximum(top, project(block * SEG, SEG))

    key_top = lax.fori_loop(0, blocks, project_block, jnp.float32(0.0))

    @pl.when(blocks == length)
    def _():
        project(length * SEG, MEMP)

    place = pl.multiple_of(MEMP + SEG * meta[M_SPOT], MEMP)
    qown[0:SEG, :] = qc[pl.ds(place, SEG), :]
    qown[SEG:OWN, :] = qc[0:MEMP, :]
    near = longest(qown[...].astype(F32)) * key_top <= SHIFT_FREE**2

    def pair(index, carry):
        cols = pl.ds(pl.multiple_of(index * PAIR, PAIR), PAIR)
        lane = lax.broadcasted_iota(jnp.int32, (OWN, PAIR), 1)
        halves = (0, 1)
        mine = [(lane // HD) == half for half in halves]
        numbers = [lane == quad * 4 + index * 2 + half for half in halves]
        both = qown[:, cols]
        queries = [jnp.where(mine[half], both, jnp.zeros_like(both)) for half in halves]
        acc[...] = jnp.zeros_like(acc)

        def score(half, span):
            return lax.dot_general(queries[half], kc[span, cols], LAST, preferred_element_type=F32)

        def gather(half, span, terms):
            values = extended[half, span, cols]
            return jnp.dot(terms.astype(BF16), values, preferred_element_type=F32)

        @pl.when(near)
        def _():
            def run(first, count):
                span = span_of(first, count)
                for half in halves:
                    acc[half] += gather(half, span, jnp.exp(score(half, span)))

            by_chunks(blocks, run)

        @pl.when(jnp.logical_not(near))
        def _():
            for half in halves:
                def run(block, top):
                    span = span_of(block, 1)
                    column = block * SEG + lax.broadcasted_iota(jnp.int32, (OWN, SEG), 1)
                    dead = (column >= meta[M_ROWS]) | ((column >= meta[M_MEM]) & (column < MEMP))
                    scores = jnp.where(dead, NEG, score(half, span))
                    new = jnp.maximum(top, jnp.max(scores, axis=1, keepdims=True))
                    terms = gather(half, span, jnp.exp(scores - new))
                    acc[half] = acc[half] * jnp.exp(top - new) + terms
                    return new

                top = lax.fori_loop(0, blocks, run, jnp.full((OWN, 1), NEG, F32))
                lse[...] = jnp.where(numbers[half], top, lse[...])

        sums = [acc[half] for half in halves]
        value = jnp.where(mine[0], sums[0], sums[1])
        total = pltpu.roll(jnp.where(mine[0], sums[1], sums[0]), HD, 1)
        out[:, cols] = value * (1.0 / total)
        turned_total = pltpu.roll(total, HD, 1)
        for half in halves:
            spread = jnp.where(mine[half], total, turned_total)
            lse[...] += jnp.where(numbers[half], jnp.log(spread), 0.0)
        return carry

    lax.fori_loop(0, 2, pair, 0)


def attend_forward(meta, pieces, mem, weights):
    wq, bq, wk, wv, bv = weights
    width = wq.shape[0]
    whole = lambda shape: pl.BlockSpec(shape, lambda quad, meta: (0,) * len(shape))
    column = lambda count: pl.BlockSpec((count, QUAD), lambda quad, meta: (0, quad))
    return pl.pallas_call(
        forward_body,
        grid_spec=pltpu.PrefetchScalarGridSpec(
            num_scalar_prefetch=1,
            grid=(NQUAD,),
            in_specs=[pl.BlockSpec(memory_space=pl.ANY)] * len(pieces)
            + [whole((mem.shape[0], MEMP, width))]
            + [column(width)] * 3
            + [column(1)] * 2,
            out_specs=[column(OWN), whole((OWN, PAIR))] + [column(CAP)] * 3,
            scratch_shapes=[
                pltpu.VMEM((CAP, width), BF16),
                pltpu.VMEM((OWN, QUAD), BF16),
                pltpu.VMEM((2, CAP, QUAD), BF16),
                pltpu.VMEM((2, OWN, PAIR), F32),
                pltpu.SemaphoreType.DMA((LONG,)),
            ],
        ),
        out_shape=[
            jax.ShapeDtypeStruct((OWN, width), F32),
            jax.ShapeDtypeStruct((OWN, PAIR), F32),
        ]
        + [jax.ShapeDtypeStruct((CAP, width), BF16)] * 3,
        compiler_params=pltpu.CompilerParams(vmem_limit_bytes=VMEM_LIMIT),
        cost_estimate=pl.CostEstimate(
            flops=40_000_000_000, bytes_accessed=30_000_000, transcendentals=23_000_000
        ),
        name="attend_forward",
    )(meta, *pieces, mem, wq, wk, wv, bq.reshape(1, -1), bv.reshape(1, -1))


def backward_body(start, count, meta, *refs):
    pieces, refs = refs[:-22], refs[-22:]
    (
        kc, vc, qc, mem_grad, mem_stats, own_stats,
        dq, dk, dv,
        doc, stats, chain_stats, qown, kown, vown, down, bias, qacc, kacc, vacc, sems, stat_sems,
    ) = refs
    step = pl.program_id(0)
    quad = start + step
    length = meta[M_LEN]

    @pl.when(step == 0)
    def _():
        rows_from = lambda index: lambda ref: ref.at[0:SEG, pl.ds((start + index) * QUAD, QUAD)]
        rows_to = lambda index: lambda spot: doc.at[index, pl.ds(MEMP + SEG * spot, SEG)]
        stat_from = lambda ref: ref.at[SEG : SEG + 2 * STAT, 0:SEG]
        stat_to = lambda spot: stats.at[spot]
        load_chain(meta, pieces, stat_from, stat_to, stat_sems)
        for index in range(count):
            load_chain(meta, pieces, rows_from(index), rows_to(index), sems.at[index])
        bias[...] = key_bias(meta)
        for index in range(count):
            doc[index, 0:MEMP, :] = mem_grad[:, (start + index) * QUAD : (start + index + 1) * QUAD]

            @pl.when(meta[M_BLOCKS] > length)
            def _():
                place = pl.multiple_of(MEMP + SEG * length, MEMP)
                doc[index, pl.ds(place, SEG - MEMP), :] = jnp.zeros((SEG - MEMP, QUAD), BF16)

        wait_chain(meta, pieces, stat_from, stat_to, stat_sems)
        for spot in range(NBLK):
            span = slice(SEG * spot, SEG * (spot + 1))
            if spot == LONG:
                chain_stats[:, span] = jnp.zeros((STAT, SEG), F32)
                continue

            @pl.when(spot < length)
            def _():
                pair = stats[spot].astype(F32)
                chain_stats[:, span] = pair[0:STAT] + pair[STAT : 2 * STAT]

            @pl.when(spot >= length)
            def _():
                chain_stats[:, span] = jnp.zeros((STAT, SEG), F32)

        moved = pltpu.roll(chain_stats[...], MEMP, 1)
        column = lax.broadcasted_iota(jnp.int32, (STAT, CAP), 1)
        entry = lax.broadcasted_iota(jnp.int32, (STAT, CAP), 0)
        beyond = jnp.where(entry < H, -NEG, 0.0)
        chain_stats[...] = jnp.where(column < MEMP + SEG * length, moved, beyond)
        lane = lax.broadcasted_iota(jnp.int32, (STAT, PAIR), 1)
        at_front = pltpu.roll(mem_stats[...], MEMP, 1)
        chain_stats[:, 0:PAIR] = jnp.where(lane < MEMP, at_front, chain_stats[:, 0:PAIR])
        for index in range(count):
            wait_chain(meta, pieces, rows_from(index), rows_to(index), sems.at[index])

    place = pl.multiple_of(MEMP + SEG * meta[M_SPOT], MEMP)
    for own, chain in ((qown, qc), (kown, kc), (vown, vc), (down, doc.at[step])):
        own[0:SEG, :] = chain[pl.ds(place, SEG), :]
        own[SEG:OWN, :] = chain[0:MEMP, :]

    def head(index, carry):
        cols = pl.ds(pl.multiple_of((index // 2) * PAIR, PAIR), PAIR)
        number = quad * 4 + index
        lane = lax.broadcasted_iota(jnp.int32, (OWN, PAIR), 1)
        mine = (lane // HD) == (index % 2)
        masked = lambda ref: jnp.where(mine, ref[:, cols], jnp.zeros((OWN, PAIR), BF16))
        query, key, value, grad = masked(qown), masked(kown), masked(vown), masked(down)
        pick = lambda at: jnp.sum(jnp.where(lane == at, own_stats[...], 0.0), axis=1, keepdims=True)
        log_total, delta = pick(number), pick(H + number)
        for acc in (qacc, kacc, vacc):
            acc[...] = jnp.zeros_like(acc)

        def run(first, size):
            span = span_of(first, size)
            keys, values = kc[span, cols], vc[span, cols]
            scores = lax.dot_general(query, keys, LAST, preferred_element_type=F32)
            weights = jnp.exp(scores + bias[0:1, span] - log_total)
            weight_grad = lax.dot_general(grad, values, LAST, preferred_element_type=F32)
            score_grad = (weights * (weight_grad - delta)).astype(BF16)
            qacc[...] += jnp.dot(score_grad, keys, preferred_element_type=F32)

            queries, grads = qc[span, cols], doc[step, span, cols]
            scores = lax.dot_general(key, queries, LAST, preferred_element_type=F32)
            weights = jnp.exp(scores - chain_stats[pl.ds(number, 1), span])
            weight_grad = lax.dot_general(value, grads, LAST, preferred_element_type=F32)
            score_grad = (
                weights * (weight_grad - chain_stats[pl.ds(H + number, 1), span])
            ).astype(BF16)
            vacc[...] += jnp.dot(weights.astype(BF16), grads, preferred_element_type=F32)
            kacc[...] += jnp.dot(score_grad, queries, preferred_element_type=F32)

        by_chunks(meta[M_BLOCKS], run)
        row = lax.broadcasted_iota(jnp.int32, (OWN, PAIR), 0)
        alive = (row < meta[M_USED]) | ((row >= SEG) & (row < SEG + meta[M_MEM]))
        query_sum = qacc[...] * (HD**-0.5)
        key_sum = jnp.where(alive, kacc[...], 0.0)
        value_sum = jnp.where(alive, vacc[...], 0.0)
        for ref, sums in ((dq, query_sum), (dk, key_sum), (dv, value_sum)):
            ref[:, cols] = jnp.where(mine, sums.astype(BF16), ref[:, cols])
        return carry

    lax.fori_loop(0, 4, head, 0)


def attend_backward(meta, pieces, chain, mem_grad, mem_stats, own_stats, start, count):
    width = mem_grad.shape[1]
    whole = lambda shape: pl.BlockSpec(shape, lambda quad, meta: (0,) * len(shape))
    chain_column = pl.BlockSpec((CAP, QUAD), lambda step, meta: (0, start + step))
    own_column = pl.BlockSpec((OWN, QUAD), lambda step, meta: (0, step))
    return pl.pallas_call(
        functools.partial(backward_body, start, count),
        grid_spec=pltpu.PrefetchScalarGridSpec(
            num_scalar_prefetch=1,
            grid=(count,),
            in_specs=[pl.BlockSpec(memory_space=pl.ANY)] * len(pieces)
            + [chain_column] * 3
            + [whole((MEMP, width)), whole((STAT, PAIR)), whole((OWN, PAIR))],
            out_specs=[own_column] * 3,
            scratch_shapes=[
                pltpu.VMEM((count, CAP, QUAD), BF16),
                pltpu.VMEM((LONG, 2 * STAT, SEG), BF16),
                pltpu.VMEM((STAT, CAP), F32),
            ]
            + [pltpu.VMEM((OWN, QUAD), BF16)] * 4
            + [
                pltpu.VMEM((8, CAP), F32),
                pltpu.VMEM((OWN, PAIR), F32),
                pltpu.VMEM((OWN, PAIR), F32),
                pltpu.VMEM((OWN, PAIR), F32),
                pltpu.SemaphoreType.DMA((count, LONG)),
                pltpu.SemaphoreType.DMA((LONG,)),
            ],
        ),
        out_shape=[jax.ShapeDtypeStruct((OWN, count * QUAD), BF16)] * 3,
        compiler_params=pltpu.CompilerParams(vmem_limit_bytes=VMEM_LIMIT),
        cost_estimate=pl.CostEstimate(
            flops=BACK_COST, bytes_accessed=1_000_000, transcendentals=0
        ),
        name="attend_backward",
    )(meta, *pieces, *chain, mem_grad, mem_stats, own_stats)


def norm_stats(values):
    centered = values - jnp.mean(values, axis=-1, keepdims=True)
    scale = lax.rsqrt(jnp.mean(centered * centered, axis=-1, keepdims=True) + EPS)
    return centered * scale, scale


def norm_back(normed, scale, upstream):
    mean = jnp.mean(upstream, axis=-1, keepdims=True)
    along = jnp.mean(upstream * normed, axis=-1, keepdims=True)
    return scale * (upstream - mean - normed * along)


def turned(left, right):
    return lax.dot_general(left, right, LAST, preferred_element_type=F32)


def crossed(left, right):
    return lax.dot_general(left, right, (((0,), (0,)), ((), ())), preferred_element_type=F32)


def middle_body(
    meta, attended, lse, tokens, memory, token_cot, memory_cot,
    wo, bo, gain1, shift1, bi, b2, gain2, shift2, wi_from, w2_from,
    final, final_mem, payload, mem_grad, mem_stats, own_stats, res_grad, rows,
    attended_low, branch_out, first_low, inner_out, active, outer_out, sums, inner_sum,
    wi, w2, first, norm1, scale1, total, second_grad, outer_grad, slope, cots, weight_sems,
):
    width, inner_width = wi.shape
    wi_copy = pltpu.make_async_copy(wi_from, wi, weight_sems.at[0])
    w2_copy = pltpu.make_async_copy(w2_from, w2, weight_sems.at[1])
    wi_copy.start()
    w2_copy.start()
    chain = meta[M_CHAIN]
    lead = jnp.where(meta[M_SPOT] == 0, 1.0, 0.0)
    rows[0:SEG, :] = tokens[...]
    rows[SEG:OWN, :] = memory[chain]
    cots[0:SEG, :] = token_cot[...]
    cots[SEG:OWN, :] = memory_cot[chain]
    attended_low[...] = attended[...].astype(BF16)
    total[...] = jnp.dot(attended_low[...], wo[...], preferred_element_type=F32)
    sums[...] = jnp.zeros_like(sums)
    inner_sum[...] = jnp.zeros_like(inner_sum)
    vector = lambda ref: ref[...].astype(F32)

    def by_rows(run):
        def step(index, carry):
            start = pl.multiple_of(index * ROWS, ROWS)
            row = start + lax.broadcasted_iota(jnp.int32, (ROWS, 1), 0)
            live = (row < meta[M_USED]) | ((row >= SEG) & (row < SEG + meta[M_MEM]))
            counted = jnp.where(row < SEG, 1.0, lead)
            run(pl.ds(start, ROWS), live, counted)
            return carry

        lax.fori_loop(0, OWN // ROWS, step, 0)

    def by_columns(run):
        def step(index, carry):
            run(pl.ds(pl.multiple_of(index * COLS, COLS), COLS))
            return carry

        lax.fori_loop(0, inner_width // COLS, step, 0)

    def add(place, value):
        sums[place : place + 1, :] += jnp.sum(value, axis=0, keepdims=True)

    def first_part(span, live, counted):
        value = rows[span, :].astype(F32) + total[span, :] + vector(bo)
        normed, scale = norm_stats(value)
        norm1[span, :] = normed
        scale1[span, :] = jnp.broadcast_to(scale, (ROWS, PAIR))
        value = normed * vector(gain1) + vector(shift1)
        first[span, :] = value
        first_low[span, :] = value.astype(BF16)

    by_rows(first_part)
    wi_copy.wait()
    w2_copy.wait()
    total[...] = jnp.zeros_like(total)

    def inner_part(cols):
        inner = jnp.dot(first_low[...], wi[:, cols], preferred_element_type=F32)
        inner = inner + bi[:, cols].astype(F32)
        cdf = 0.5 * (1.0 + lax.erf(inner * (2.0**-0.5)))
        density = jnp.exp(-0.5 * inner * inner) * 0.3989422804014327
        slope[:, cols] = cdf + inner * density
        low = (inner * cdf).astype(BF16)
        active[:, cols] = low
        total[...] += jnp.dot(low, w2[cols, :], preferred_element_type=F32)

    by_columns(inner_part)

    def final_part(span, live, counted):
        normed, scale = norm_stats(first[span, :] + total[span, :] + vector(b2))
        value = jnp.where(live, normed * vector(gain2) + vector(shift2), 0.0)
        rows_low = value.astype(BF16)
        outer_out[span, :] = rows_low
        cot = cots[span, :].astype(F32)
        cot = jnp.where(live, cot, 0.0)
        weighted = cot * counted
        add(4, weighted * normed)
        add(5, weighted)
        grad = norm_back(normed, scale, cot * vector(gain2))
        second_grad[span, :] = grad
        outer_grad[span, :] = grad.astype(BF16)
        add(3, grad.astype(BF16).astype(F32) * counted)

    by_rows(final_part)
    final[...] = outer_out[0:SEG, :]
    final_mem[...] = outer_out[SEG:OWN, :]
    outer_out[0:SEG, :] = outer_grad[0:SEG, :]
    outer_out[SEG:OWN, :] = outer_grad[SEG:OWN, :] * lead.astype(BF16)
    total[...] = jnp.zeros_like(total)

    def inner_back(cols):
        grad = (turned(outer_grad[...], w2[cols, :]) * slope[:, cols]).astype(BF16)
        total[...] += turned(grad, wi[:, cols])
        tail = grad[SEG:OWN] * lead.astype(BF16)
        inner_out[0:SEG, cols] = grad[0:SEG]
        inner_out[SEG:OWN, cols] = tail
        inner_sum[:, cols] = jnp.sum(grad[0:SEG].astype(F32), axis=0, keepdims=True) + jnp.sum(
            tail.astype(F32), axis=0, keepdims=True
        )

    by_columns(inner_back)

    def last_part(span, live, counted):
        grad = second_grad[span, :] + total[span, :]
        normed = norm1[span, :]
        weighted = grad * counted
        add(1, weighted * normed)
        add(2, weighted)
        grad = norm_back(normed, scale1[span, 0:1], grad * vector(gain1))
        res_grad[span, :] = grad
        low = grad.astype(BF16)
        outer_grad[span, :] = low
        low = (low.astype(F32) * counted).astype(BF16)
        branch_out[span, :] = low
        add(0, low.astype(F32))

    by_rows(last_part)
    total[...] = turned(outer_grad[...], wo[...])
    feature = lax.broadcasted_iota(jnp.int32, (width, PAIR), 0)
    lane = lax.broadcasted_iota(jnp.int32, (width, PAIR), 1)
    head_of = jnp.where(feature // HD == lane - H, 1.0, 0.0).astype(BF16)

    def delta_part(span, live, counted):
        low = total[span, :].astype(BF16)
        outer_grad[span, :] = low
        product = low.astype(F32) * attended[span, :]
        high = product.astype(BF16)
        rest = (product - high.astype(F32)).astype(BF16)
        delta = jnp.dot(high, head_of, preferred_element_type=F32)
        delta = delta + jnp.dot(rest, head_of, preferred_element_type=F32)
        own_stats[span, :] = lse[span, :] + delta

    by_rows(delta_part)
    payload[0:SEG, :] = outer_grad[0:SEG, :]
    mem_grad[...] = outer_grad[SEG:OWN, :]
    stats = jnp.transpose(own_stats[0:SEG, :])[0:STAT]
    high = stats.astype(BF16)
    rest = (stats - high.astype(F32)).astype(BF16)
    both = jnp.concatenate([high.astype(F32), rest.astype(F32)], 0).astype(BF16)
    payload[SEG : SEG + 2 * STAT, 0:SEG] = both
    payload[SEG : SEG + 2 * STAT, SEG:width] = jnp.zeros((2 * STAT, width - SEG), BF16)
    mem_stats[...] = jnp.transpose(own_stats[OWN - PAIR : OWN, :])[0:STAT]


def middle(meta, attended, lse, tokens, memory, token_cot, memory_cot, weights):
    wo, bo, gain1, shift1, wi, bi, w2, b2, gain2, shift2 = weights
    width, inner_width = wi.shape
    vmem, line = pl.BlockSpec(memory_space=pltpu.VMEM), lambda value: value.reshape(1, -1)
    hbm = pl.BlockSpec(memory_space=pl.ANY)
    shape = jax.ShapeDtypeStruct
    return pl.pallas_call(
        middle_body,
        in_specs=[pl.BlockSpec(memory_space=pltpu.SMEM)] + [vmem] * 14 + [hbm] * 2,
        out_specs=[vmem] * 16,
        out_shape=[
            shape((SEG, width), BF16),
            shape((MEMP, width), BF16),
            shape((SEG + 2 * STAT, width), BF16),
            shape((MEMP, width), BF16),
            shape((STAT, PAIR), F32),
            shape((OWN, PAIR), F32),
            shape((OWN, width), F32),
            shape((OWN, width), BF16),
            shape((OWN, width), BF16),
            shape((OWN, width), BF16),
            shape((OWN, width), BF16),
            shape((OWN, inner_width), BF16),
            shape((OWN, inner_width), BF16),
            shape((OWN, width), BF16),
            shape((8, width), F32),
            shape((1, inner_width), F32),
        ],
        scratch_shapes=[
            pltpu.VMEM((width, inner_width), BF16),
            pltpu.VMEM((inner_width, width), BF16),
            pltpu.VMEM((OWN, width), F32),
            pltpu.VMEM((OWN, width), F32),
            pltpu.VMEM((OWN, PAIR), F32),
            pltpu.VMEM((OWN, width), F32),
            pltpu.VMEM((OWN, width), F32),
            pltpu.VMEM((OWN, width), BF16),
            pltpu.VMEM((OWN, inner_width), F32),
            pltpu.VMEM((OWN, width), BF16),
            pltpu.SemaphoreType.DMA((2,)),
        ],
        compiler_params=pltpu.CompilerParams(vmem_limit_bytes=VMEM_LIMIT),
        cost_estimate=pl.CostEstimate(
            flops=12_000_000_000, bytes_accessed=40_000_000, transcendentals=2_000_000
        ),
        name="middle",
    )(
        meta, attended, lse, tokens, memory, token_cot, memory_cot,
        wo, line(bo), line(gain1), line(shift1), line(bi), line(b2), line(gain2), line(shift2),
        wi, w2,
    )


def late_body(metas, group, *refs, batches, chains, parts):
    refs = list(refs)
    take = lambda count: [refs.pop(0) for _ in range(count)]
    rows, res_mem = take(batches), take(batches)
    grads = [[take(len(parts[b])) for _ in range(3)] for b in range(batches)]
    weights = take(3)
    out, masked = take(2)
    width = weights[0].shape[0]
    out[3 * width :, :] = jnp.zeros((out.shape[0] - 3 * width, width), BF16)
    for b in range(batches):
        lead = jnp.where(metas[b, M_SPOT] == 0, 1.0, 0.0)
        masked[b, 0:SEG, :] = rows[b][0:SEG, :]
        masked[b, SEG:OWN, :] = rows[b][SEG:OWN, :] * lead.astype(BF16)
        grad = res_mem[b][SEG:OWN, :]
        for k in range(3):
            first = 0
            for part, ref in zip(parts[b], grads[b][k]):
                grad = grad + turned(ref[SEG:OWN, :], weights[k][:, first : first + part])
                first += part
        place = ((group[0] * batches + b) * chains + metas[b, M_CHAIN]) * MEMP
        place = pl.multiple_of(3 * width + 16 + place, 16)
        out[pl.ds(place, MEMP), :] = (grad * lead).astype(BF16)
    cuts = sorted({sum(p[:i]) for p in parts for i in range(len(p) + 1)})
    for k in range(3):
        for low, high in zip(cuts[:-1], cuts[1:]):
            total, line = None, None
            for b in range(batches):
                lead = jnp.where(metas[b, M_SPOT] == 0, 1.0, 0.0)
                first = 0
                for part, ref in zip(parts[b], grads[b][k]):
                    if first <= low and high <= first + part:
                        grad = ref[:, low - first : high - first]
                    first += part
                value = crossed(masked[b], grad)
                total = value if total is None else total + value
                if k != 1:
                    grad = grad.astype(F32)
                    value = jnp.sum(grad[0:SEG], 0, keepdims=True)
                    value = value + jnp.sum(grad[SEG:OWN], 0, keepdims=True) * lead
                    line = value if line is None else line + value
            out[k * width : (k + 1) * width, low:high] = total.astype(BF16)
            if k != 1:
                row = lax.broadcasted_iota(jnp.int32, (16, high - low), 0)
                span = slice(3 * width, 3 * width + 16)
                old = out[span, low:high].astype(F32)
                out[span, low:high] = jnp.where(row == k // 2, line, old).astype(BF16)


def late_sums(metas, group, groups, chains, rows, res, grads, weights):
    batches, width = len(rows), weights[0].shape[0]
    parts = [[part.shape[1] for part in one[0]] for one in grads]
    count = 3 * width + 16 + groups * batches * chains * MEMP
    count += -count % LATE_ROWS
    vmem, smem = pl.BlockSpec(memory_space=pltpu.VMEM), pl.BlockSpec(memory_space=pltpu.SMEM)
    flat = [part for one in grads for name in one for part in name]
    return pl.pallas_call(
        functools.partial(late_body, batches=batches, chains=chains, parts=parts),
        in_specs=[smem] * 2 + [vmem] * (2 * batches + len(flat) + 3),
        out_specs=vmem,
        out_shape=jax.ShapeDtypeStruct((count, width), BF16),
        scratch_shapes=[pltpu.VMEM((batches, OWN, width), BF16)],
        compiler_params=pltpu.CompilerParams(vmem_limit_bytes=VMEM_LIMIT),
        name="late_sums",
    )(metas, group.reshape(1), *rows, *res, *flat, *weights)


def weight_grad(left, right):
    return lax.dot_general(left, right, (((0,), (0,)), ((), ())), preferred_element_type=F32)


def swap(value, mask):
    sizes = lax.axis_size("dp") * lax.axis_size("blk")
    return lax.ppermute(value, ("dp", "blk"), [(i, i ^ mask) for i in range(sizes)])


def sum_everywhere(value, beside):
    blk = lax.axis_size("blk")
    place = lax.axis_index("dp") * blk + lax.axis_index("blk")
    groups = [(1,), (2, blk), (4, 8)]
    bit = 2 * blk
    while bit < blk * lax.axis_size("dp"):
        groups.append((bit,))
        bit *= 2
    masks_of = lambda group: [
        sum(bit for i, bit in enumerate(group) if (k >> i) & 1) for k in range(1 << len(group))
    ]
    own_of = lambda group: sum(((place // bit) % 2) << i for i, bit in enumerate(group))
    for group in groups:
        masks, own = masks_of(group), own_of(group)
        size = value.shape[0] // len(masks)
        part = lambda k: lax.dynamic_slice_in_dim(value, (own ^ k) * size, size)
        got = [swap(part(k), mask) for k, mask in enumerate(masks) if k]
        value = sum((g.astype(F32) for g in got), part(0).astype(F32)).astype(BF16)
    for index, group in enumerate(reversed(groups)):
        masks, own = masks_of(group), own_of(group)
        size = value.shape[0]
        if index == len(groups) - 2:
            value, beside = lax.optimization_barrier((value, beside))
        got = [value] + [swap(value, mask) for mask in masks[1:]]
        if index == len(groups) - 2:
            beside = [part.astype(F32) for part in beside]
            got[-1], beside = lax.optimization_barrier((got[-1], beside))
        value = jnp.zeros((size * len(masks), value.shape[1]), BF16)
        for k, part in enumerate(got):
            value = lax.dynamic_update_slice_in_dim(value, part, (own ^ k) * size, 0)
    return value, beside


def local(
    tokens, memory, chain_lengths, last_fill,
    query_proj, query_bias, key_proj, value_proj, value_bias, output_proj, output_bias,
    attn_gain, attn_shift, inner_proj, inner_bias, outer_proj, outer_bias,
    final_gain, final_shift, token_cotangent, memory_cotangent,
):
    own = lax.axis_index("blk").astype(jnp.int32)
    group = lax.axis_index("dp").astype(jnp.int32)
    groups = lax.axis_size("dp")
    batches, _, width = tokens.shape
    chains, mem_rows = memory.shape[1:3]
    pad_mem = ((0, 0), (0, 0), (0, MEMP - mem_rows), (0, 0))
    memory, memory_cotangent = jnp.pad(memory, pad_mem), jnp.pad(memory_cotangent, pad_mem)

    metas = metas_of(own, chain_lengths[:, 0], last_fill[:, 0], mem_rows)
    near = gather_near(tokens[0])
    later, near = lax.optimization_barrier(([tokens[b] for b in range(1, batches)], near))
    pieces = [near] + [gather_all(part) for part in later]
    meta_of = [metas[b] for b in range(batches)]

    states = []
    for b in range(batches):
        meta = meta_of[b]
        attended, lse, *chain_rows = attend_forward(
            meta, pieces[b], memory[b], (query_proj, query_bias, key_proj, value_proj, value_bias)
        )
        (
            final, final_mem, payload, mem_grad, mem_stats, own_stats, res_grad, rows,
            attended_low, branch, first_low, inner, active, outer, sums, inner_sum,
        ) = middle(
            meta, attended, lse, tokens[b], memory[b], token_cotangent[b], memory_cotangent[b],
            (
                output_proj, output_bias, attn_gain, attn_shift, inner_proj, inner_bias,
                outer_proj, outer_bias, final_gain, final_shift,
            ),
        )
        if b + 1 < batches:
            meta_of[b + 1], payload = lax.optimization_barrier((meta_of[b + 1], payload))
        states.append(
            dict(
                meta=meta, rows=rows, chain_rows=chain_rows, payload=payload, mem_grad=mem_grad,
                mem_stats=mem_stats, own_stats=own_stats, res_grad=res_grad, final=final,
                final_mem=final_mem, attended_low=attended_low, branch=branch,
                first_low=first_low, inner=inner, active=active, outer=outer, sums=sums,
                inner_sum=inner_sum,
            )
        )

    def over_batches(left, right):
        return weight_grad(
            jnp.concatenate([s[left] for s in states], 0),
            jnp.concatenate([s[right] for s in states], 0),
        ).astype(BF16)

    slots = (jnp.arange(groups)[:, None, None, None, None] == group) & (
        jnp.arange(chains)[:, None, None]
        == jnp.where(metas[:, M_SPOT] == 0, metas[:, M_CHAIN], -1)[:, None, None, None]
    )
    final_mem = jnp.stack([s["final_mem"] for s in states])[None, :, None]
    early = (
        over_batches("first_low", "inner"),
        over_batches("active", "outer"),
        over_batches("attended_low", "branch"),
        jnp.concatenate(
            [
                jnp.where(slots, final_mem, 0).astype(BF16).reshape(-1, width),
                sum(s["sums"] for s in states).astype(BF16),
                sum(s["inner_sum"] for s in states).astype(BF16).reshape(-1, width),
            ],
            0,
        ),
    )
    early, *held = lax.optimization_barrier((early, *[s["meta"] for s in states]))
    for s, meta in zip(states, held):
        s["meta"] = meta
        s["gathered"] = gather_all(s["payload"])
    for s in states:
        s["grads"] = attend_backward(
            s["meta"], s["gathered"], s["chain_rows"], s["mem_grad"], s["mem_stats"],
            s["own_stats"], 0, NQUAD,
        )
        if s is states[0]:
            s["grads"], states[-1]["gathered"], early = lax.optimization_barrier(
                (s["grads"], states[-1]["gathered"], early)
            )
            early = lax.psum(early, ("dp", "blk"))
        s["grads"] = [[grad] for grad in s["grads"]]
    grad_inner, grad_outer, grad_output, rest = early
    late = late_sums(
        metas, group, groups, chains, [s["rows"] for s in states],
        [s["res_grad"] for s in states], [s["grads"] for s in states],
        (query_proj, key_proj, value_proj),
    )

    def own_slots(rows):
        rows = rows.reshape(groups, batches, chains, MEMP, width)
        return lax.dynamic_index_in_dim(rows, group, keepdims=False)[:, :, :mem_rows]

    late, (grad_inner, grad_outer, grad_output) = sum_everywhere(
        late, [grad_inner, grad_outer, grad_output]
    )
    grad_query, grad_key, grad_value = (late[i * width : (i + 1) * width] for i in range(3))
    biases = late[3 * width : 3 * width + 2].astype(F32)
    count = groups * batches * chains * MEMP
    memory_grad = own_slots(late[3 * width + 16 : 3 * width + 16 + count])
    memory_out = own_slots(rest[:count])
    sums, inner_sum = rest[count : count + 8], rest[count + 8 :].reshape(1, -1)
    token_outs = [s["final"] for s in states]
    token_grads = []
    for s in states:
        grad = s["res_grad"][:SEG]
        for parts, weights in zip(s["grads"], (query_proj, key_proj, value_proj)):
            first = 0
            for part in parts:
                grad = grad + turned(part[:SEG], weights[:, first : first + part.shape[1]])
                first += part.shape[1]
        token_grads.append(grad.astype(BF16))

    wide = lambda value: value.astype(F32)
    return (
        jnp.stack(token_outs),
        memory_out,
        jnp.stack(token_grads),
        memory_grad,
        wide(grad_query),
        biases[0],
        wide(grad_key),
        wide(grad_value),
        biases[1],
        wide(grad_output),
        wide(sums[0]),
        wide(sums[1]),
        wide(sums[2]),
        wide(grad_inner),
        wide(inner_sum[0]),
        wide(grad_outer),
        wide(sums[3]),
        wide(sums[4]),
        wide(sums[5]),
    )


def solution(mesh):
    row_spec = P(None, ("dp", "blk"), None)
    mem_spec = P(None, "dp", None, None)
    int_spec = P(None, "dp", None)
    in_specs = (row_spec, mem_spec, int_spec, int_spec) + (P(),) * 15 + (row_spec, mem_spec)
    out_specs = (row_spec, mem_spec, row_spec, mem_spec) + (P(),) * 15
    return jax.shard_map(local, mesh=mesh, in_specs=in_specs, out_specs=out_specs, check_vma=False)
```

```python
import functools

import jax
import jax.numpy as jnp
from jax import lax
from jax.experimental import pallas as pl
from jax.experimental.pallas import tpu as pltpu
from jax.sharding import PartitionSpec as P

H = 12
HD = 64
QUAD = 256
NQUAD = 3
PAIR = 128
MEMP = 32
SEG = 512
LONG = 7
NBLK = LONG + 1
CAP = NBLK * SEG
OWN = SEG + MEMP
STAT = 24
BACK_COST = 10_000_000_000
LATE_ROWS = 256
NPIECE = 14
ROWS = 272
COLS = 1024
NEG = -1e30
SHIFT_FREE = 60.0
EPS = 1e-05
F32 = jnp.float32
BF16 = jnp.bfloat16
VMEM_LIMIT = 60 * 2**20
LAST = (((1,), (1,)), ((), ()))

M_LEN, M_ROWS, M_BLOCKS, M_SPOT, M_USED, M_MEM, M_CHAIN, M_START, M_PIECE = range(9)


def plane_moves(shift_of):
    pairs = []
    for plane in range(4):
        for place in range(4):
            target = plane + shift_of(place >> 1)
            if 0 <= target < 4:
                pairs.append((4 * plane + place, 4 * target + place))
    return pairs


UP = plane_moves(lambda side: 1)
DOWN = plane_moves(lambda side: -1)
OUTWARD = plane_moves(lambda side: 1 if side else -1)
SIDE = [(i, i ^ 2) for i in range(16)]
CORE = [(i, i ^ 1) for i in range(16)]


def move(value, pairs):
    return lax.ppermute(value, "blk", pairs)


def gather_near(value):
    side = (lax.axis_index("blk") >> 1) & 1
    below, above, beside = move(value, UP), move(value, DOWN), move(value, SIDE)
    far = move(jnp.where(side == 1, below, above), OUTWARD)
    moved = [move(beside, UP), move(beside, DOWN), move(far, SIDE)]
    here = [value, beside, below, above] + moved
    return here + [move(part, CORE) for part in here]


def gather_all(value):
    return [lax.all_gather(value, "blk")]


def piece_of(own, other):
    plane = (other >> 2) - (own >> 2)
    same_side = ((other >> 1) & 1) == ((own >> 1) & 1)
    on_side = jnp.where(plane == 0, 0, jnp.where(plane < 0, 2, 3))
    off_side = jnp.where(plane == 0, 1, jnp.where(plane == -1, 4, jnp.where(plane == 1, 5, 6)))
    index = jnp.where(same_side, on_side, off_side)
    return index + jnp.where((other & 1) == (own & 1), 0, LONG)


def meta_body(own_ref, lengths, fills, meta, *, batches, chains, mem_rows):
    own = own_ref[0]
    for b in range(batches):
        end = jnp.int32(0)
        length, start, fill, chain = (jnp.int32(0) for _ in range(4))
        for c in range(chains):
            begin = end
            end = end + lengths[b, c]
            inside = (begin <= own) & (own < end)
            length = jnp.where(inside, lengths[b, c], length)
            start = jnp.where(inside, begin, start)
            fill = jnp.where(inside, fills[b, c], fill)
            chain = jnp.where(inside, c, chain)
        rows = MEMP + SEG * (length - 1) + fill
        spot = own - start
        meta[b, M_LEN] = length
        meta[b, M_ROWS] = rows
        meta[b, M_BLOCKS] = (rows + SEG - 1) // SEG
        meta[b, M_SPOT] = spot
        meta[b, M_USED] = jnp.where(spot == length - 1, fill, SEG)
        meta[b, M_MEM] = jnp.int32(mem_rows)
        meta[b, M_CHAIN] = chain
        meta[b, M_START] = start
        for place in range(8):
            meta[b, M_PIECE + place] = piece_of(own, start + place)


def metas_of(own, lengths, fills, mem_rows):
    smem = pl.BlockSpec(memory_space=pltpu.SMEM)
    body = functools.partial(
        meta_body, batches=lengths.shape[0], chains=lengths.shape[1], mem_rows=mem_rows
    )
    return pl.pallas_call(
        body,
        in_specs=[smem] * 3,
        out_specs=smem,
        out_shape=jax.ShapeDtypeStruct((lengths.shape[0], 16), jnp.int32),
        name="find_chain",
    )(own.reshape(1), lengths, fills)


def load_chain(meta, pieces, view_from, view_to, sems):
    length = meta[M_LEN]
    for spot in range(LONG):
        def start(source):
            pltpu.make_async_copy(view_from(source), view_to(spot), sems.at[spot]).start()

        @pl.when(spot < length)
        def _():
            if len(pieces) == 1:
                start(pieces[0].at[meta[M_START] + spot])
                return
            for index in range(len(pieces)):
                @pl.when(meta[M_PIECE + spot] == index)
                def _():
                    start(pieces[index])


def wait_chain(meta, pieces, view_from, view_to, sems):
    length = meta[M_LEN]
    source = pieces[0].at[0] if len(pieces) == 1 else pieces[0]
    for spot in range(LONG):
        @pl.when(spot < length)
        def _():
            pltpu.make_async_copy(view_from(source), view_to(spot), sems.at[spot]).wait()


def key_bias(meta):
    column = lax.broadcasted_iota(jnp.int32, (8, CAP), 1)
    dead = (column >= meta[M_ROWS]) | ((column >= meta[M_MEM]) & (column < MEMP))
    return jnp.where(dead, NEG, 0.0).astype(F32)


def by_chunks(blocks, run):
    def four(index, carry):
        run(index * 4, 4)
        return carry

    lax.fori_loop(0, blocks // 4, four, 0)
    for count in (1, 2, 3):
        @pl.when(blocks % 4 == count)
        def _():
            run((blocks // 4) * 4, count)


def span_of(first, count):
    return pl.ds(pl.multiple_of(first * SEG, SEG), count * SEG)


def forward_body(meta, *refs):
    pieces, refs = refs[:-16], refs[-16:]
    mem, wq, wk, wv, bq, bv, out, lse, kc, vc, qc, rows, qown, extended, acc, sems = refs
    quad = pl.program_id(0)
    width = rows.shape[1]
    length, blocks = meta[M_LEN], meta[M_BLOCKS]
    here = lambda source: source
    there = lambda spot: rows.at[pl.ds(MEMP + SEG * spot, SEG)]

    @pl.when(quad == 0)
    def _():
        load_chain(meta, pieces, here, there, sems)
        rows[0:MEMP, :] = mem[meta[M_CHAIN]]
        lse[...] = jnp.zeros_like(lse)

        @pl.when(blocks > length)
        def _():
            place = pl.multiple_of(MEMP + SEG * length, MEMP)
            rows[pl.ds(place, SEG - MEMP), :] = jnp.zeros((SEG - MEMP, width), BF16)

        wait_chain(meta, pieces, here, there, sems)

    def longest(values):
        halves = [
            jnp.max(jnp.sum(jnp.square(values[:, p : p + PAIR]), axis=1, keepdims=True))
            for p in range(0, QUAD, PAIR)
        ]
        return jnp.maximum(*halves)

    def project(start, count):
        span = pl.ds(pl.multiple_of(start, MEMP), count)
        part = rows[span, :]
        row = start + lax.broadcasted_iota(jnp.int32, (count, QUAD), 0)
        alive = (row < meta[M_ROWS]) & ((row < meta[M_MEM]) | (row >= MEMP))
        lower = (lax.broadcasted_iota(jnp.int32, (count, QUAD), 1) % PAIR) < HD
        key = jnp.dot(part, wk[...], preferred_element_type=F32)
        kc[span, :] = key.astype(BF16)
        value = jnp.dot(part, wv[...], preferred_element_type=F32) + bv[...].astype(F32)
        vc[span, :] = value.astype(BF16)
        value = jnp.where(alive, value, 0.0)
        one = jnp.where(alive, 1.0, 0.0)
        extended[0, span, :] = jnp.where(lower, value, one).astype(BF16)
        extended[1, span, :] = jnp.where(lower, one, value).astype(BF16)
        query = jnp.dot(part, wq[...], preferred_element_type=F32) + bq[...].astype(F32)
        query = query.astype(BF16) * jnp.asarray(HD**-0.5, BF16)
        qc[span, :] = query
        return longest(key)

    def project_block(block, top):
        return jnp.maximum(top, project(block * SEG, SEG))

    key_top = lax.fori_loop(0, blocks, project_block, jnp.float32(0.0))

    @pl.when(blocks == length)
    def _():
        project(length * SEG, MEMP)

    place = pl.multiple_of(MEMP + SEG * meta[M_SPOT], MEMP)
    qown[0:SEG, :] = qc[pl.ds(place, SEG), :]
    qown[SEG:OWN, :] = qc[0:MEMP, :]
    near = longest(qown[...].astype(F32)) * key_top <= SHIFT_FREE**2

    def pair(index, carry):
        cols = pl.ds(pl.multiple_of(index * PAIR, PAIR), PAIR)
        lane = lax.broadcasted_iota(jnp.int32, (OWN, PAIR), 1)
        halves = (0, 1)
        mine = [(lane // HD) == half for half in halves]
        numbers = [lane == quad * 4 + index * 2 + half for half in halves]
        both = qown[:, cols]
        queries = [jnp.where(mine[half], both, jnp.zeros_like(both)) for half in halves]
        acc[...] = jnp.zeros_like(acc)

        def score(half, span):
            return lax.dot_general(queries[half], kc[span, cols], LAST, preferred_element_type=F32)

        def gather(half, span, terms):
            values = extended[half, span, cols]
            return jnp.dot(terms.astype(BF16), values, preferred_element_type=F32)

        @pl.when(near)
        def _():
            def run(first, count):
                span = span_of(first, count)
                for half in halves:
                    acc[half] += gather(half, span, jnp.exp(score(half, span)))

            by_chunks(blocks, run)

        @pl.when(jnp.logical_not(near))
        def _():
            for half in halves:
                def run(block, top):
                    span = span_of(block, 1)
                    column = block * SEG + lax.broadcasted_iota(jnp.int32, (OWN, SEG), 1)
                    dead = (column >= meta[M_ROWS]) | ((column >= meta[M_MEM]) & (column < MEMP))
                    scores = jnp.where(dead, NEG, score(half, span))
                    new = jnp.maximum(top, jnp.max(scores, axis=1, keepdims=True))
                    terms = gather(half, span, jnp.exp(scores - new))
                    acc[half] = acc[half] * jnp.exp(top - new) + terms
                    return new

                top = lax.fori_loop(0, blocks, run, jnp.full((OWN, 1), NEG, F32))
                lse[...] = jnp.where(numbers[half], top, lse[...])

        sums = [acc[half] for half in halves]
        value = jnp.where(mine[0], sums[0], sums[1])
        total = pltpu.roll(jnp.where(mine[0], sums[1], sums[0]), HD, 1)
        out[:, cols] = value * (1.0 / total)
        turned_total = pltpu.roll(total, HD, 1)
        for half in halves:
            spread = jnp.where(mine[half], total, turned_total)
            lse[...] += jnp.where(numbers[half], jnp.log(spread), 0.0)
        return carry

    lax.fori_loop(0, 2, pair, 0)


def attend_forward(meta, pieces, mem, weights):
    wq, bq, wk, wv, bv = weights
    width = wq.shape[0]
    whole = lambda shape: pl.BlockSpec(shape, lambda quad, meta: (0,) * len(shape))
    column = lambda count: pl.BlockSpec((count, QUAD), lambda quad, meta: (0, quad))
    return pl.pallas_call(
        forward_body,
        grid_spec=pltpu.PrefetchScalarGridSpec(
            num_scalar_prefetch=1,
            grid=(NQUAD,),
            in_specs=[pl.BlockSpec(memory_space=pl.ANY)] * len(pieces)
            + [whole((mem.shape[0], MEMP, width))]
            + [column(width)] * 3
            + [column(1)] * 2,
            out_specs=[column(OWN), whole((OWN, PAIR))] + [column(CAP)] * 3,
            scratch_shapes=[
                pltpu.VMEM((CAP, width), BF16),
                pltpu.VMEM((OWN, QUAD), BF16),
                pltpu.VMEM((2, CAP, QUAD), BF16),
                pltpu.VMEM((2, OWN, PAIR), F32),
                pltpu.SemaphoreType.DMA((LONG,)),
            ],
        ),
        out_shape=[
            jax.ShapeDtypeStruct((OWN, width), F32),
            jax.ShapeDtypeStruct((OWN, PAIR), F32),
        ]
        + [jax.ShapeDtypeStruct((CAP, width), BF16)] * 3,
        compiler_params=pltpu.CompilerParams(vmem_limit_bytes=VMEM_LIMIT),
        cost_estimate=pl.CostEstimate(
            flops=40_000_000_000, bytes_accessed=30_000_000, transcendentals=23_000_000
        ),
        name="attend_forward",
    )(meta, *pieces, mem, wq, wk, wv, bq.reshape(1, -1), bv.reshape(1, -1))


def backward_body(start, count, meta, *refs):
    pieces, refs = refs[:-22], refs[-22:]
    (
        kc, vc, qc, mem_grad, mem_stats, own_stats,
        dq, dk, dv,
        doc, stats, chain_stats, qown, kown, vown, down, bias, qacc, kacc, vacc, sems, stat_sems,
    ) = refs
    step = pl.program_id(0)
    quad = start + step
    length = meta[M_LEN]

    @pl.when(step == 0)
    def _():
        rows_from = lambda index: lambda ref: ref.at[0:SEG, pl.ds((start + index) * QUAD, QUAD)]
        rows_to = lambda index: lambda spot: doc.at[index, pl.ds(MEMP + SEG * spot, SEG)]
        stat_from = lambda ref: ref.at[SEG : SEG + 2 * STAT, 0:SEG]
        stat_to = lambda spot: stats.at[spot]
        load_chain(meta, pieces, stat_from, stat_to, stat_sems)
        for index in range(count):
            load_chain(meta, pieces, rows_from(index), rows_to(index), sems.at[index])
        bias[...] = key_bias(meta)
        for index in range(count):
            doc[index, 0:MEMP, :] = mem_grad[:, (start + index) * QUAD : (start + index + 1) * QUAD]

            @pl.when(meta[M_BLOCKS] > length)
            def _():
                place = pl.multiple_of(MEMP + SEG * length, MEMP)
                doc[index, pl.ds(place, SEG - MEMP), :] = jnp.zeros((SEG - MEMP, QUAD), BF16)

        wait_chain(meta, pieces, stat_from, stat_to, stat_sems)
        for spot in range(NBLK):
            span = slice(SEG * spot, SEG * (spot + 1))
            if spot == LONG:
                chain_stats[:, span] = jnp.zeros((STAT, SEG), F32)
                continue

            @pl.when(spot < length)
            def _():
                pair = stats[spot].astype(F32)
                chain_stats[:, span] = pair[0:STAT] + pair[STAT : 2 * STAT]

            @pl.when(spot >= length)
            def _():
                chain_stats[:, span] = jnp.zeros((STAT, SEG), F32)

        moved = pltpu.roll(chain_stats[...], MEMP, 1)
        column = lax.broadcasted_iota(jnp.int32, (STAT, CAP), 1)
        entry = lax.broadcasted_iota(jnp.int32, (STAT, CAP), 0)
        beyond = jnp.where(entry < H, -NEG, 0.0)
        chain_stats[...] = jnp.where(column < MEMP + SEG * length, moved, beyond)
        lane = lax.broadcasted_iota(jnp.int32, (STAT, PAIR), 1)
        at_front = pltpu.roll(mem_stats[...], MEMP, 1)
        chain_stats[:, 0:PAIR] = jnp.where(lane < MEMP, at_front, chain_stats[:, 0:PAIR])
        for index in range(count):
            wait_chain(meta, pieces, rows_from(index), rows_to(index), sems.at[index])

    place = pl.multiple_of(MEMP + SEG * meta[M_SPOT], MEMP)
    for own, chain in ((qown, qc), (kown, kc), (vown, vc), (down, doc.at[step])):
        own[0:SEG, :] = chain[pl.ds(place, SEG), :]
        own[SEG:OWN, :] = chain[0:MEMP, :]

    def head(index, carry):
        cols = pl.ds(pl.multiple_of((index // 2) * PAIR, PAIR), PAIR)
        number = quad * 4 + index
        lane = lax.broadcasted_iota(jnp.int32, (OWN, PAIR), 1)
        mine = (lane // HD) == (index % 2)
        masked = lambda ref: jnp.where(mine, ref[:, cols], jnp.zeros((OWN, PAIR), BF16))
        query, key, value, grad = masked(qown), masked(kown), masked(vown), masked(down)
        pick = lambda at: jnp.sum(jnp.where(lane == at, own_stats[...], 0.0), axis=1, keepdims=True)
        log_total, delta = pick(number), pick(H + number)
        for acc in (qacc, kacc, vacc):
            acc[...] = jnp.zeros_like(acc)

        def run(first, size):
            span = span_of(first, size)
            keys, values = kc[span, cols], vc[span, cols]
            scores = lax.dot_general(query, keys, LAST, preferred_element_type=F32)
            weights = jnp.exp(scores + bias[0:1, span] - log_total)
            weight_grad = lax.dot_general(grad, values, LAST, preferred_element_type=F32)
            score_grad = (weights * (weight_grad - delta)).astype(BF16)
            qacc[...] += jnp.dot(score_grad, keys, preferred_element_type=F32)

            queries, grads = qc[span, cols], doc[step, span, cols]
            scores = lax.dot_general(key, queries, LAST, preferred_element_type=F32)
            weights = jnp.exp(scores - chain_stats[pl.ds(number, 1), span])
            weight_grad = lax.dot_general(value, grads, LAST, preferred_element_type=F32)
            score_grad = (
                weights * (weight_grad - chain_stats[pl.ds(H + number, 1), span])
            ).astype(BF16)
            vacc[...] += jnp.dot(weights.astype(BF16), grads, preferred_element_type=F32)
            kacc[...] += jnp.dot(score_grad, queries, preferred_element_type=F32)

        by_chunks(meta[M_BLOCKS], run)
        row = lax.broadcasted_iota(jnp.int32, (OWN, PAIR), 0)
        alive = (row < meta[M_USED]) | ((row >= SEG) & (row < SEG + meta[M_MEM]))
        query_sum = qacc[...] * (HD**-0.5)
        key_sum = jnp.where(alive, kacc[...], 0.0)
        value_sum = jnp.where(alive, vacc[...], 0.0)
        for ref, sums in ((dq, query_sum), (dk, key_sum), (dv, value_sum)):
            ref[:, cols] = jnp.where(mine, sums.astype(BF16), ref[:, cols])
        return carry

    lax.fori_loop(0, 4, head, 0)


def attend_backward(meta, pieces, chain, mem_grad, mem_stats, own_stats, start, count):
    width = mem_grad.shape[1]
    whole = lambda shape: pl.BlockSpec(shape, lambda quad, meta: (0,) * len(shape))
    chain_column = pl.BlockSpec((CAP, QUAD), lambda step, meta: (0, start + step))
    own_column = pl.BlockSpec((OWN, QUAD), lambda step, meta: (0, step))
    return pl.pallas_call(
        functools.partial(backward_body, start, count),
        grid_spec=pltpu.PrefetchScalarGridSpec(
            num_scalar_prefetch=1,
            grid=(count,),
            in_specs=[pl.BlockSpec(memory_space=pl.ANY)] * len(pieces)
            + [chain_column] * 3
            + [whole((MEMP, width)), whole((STAT, PAIR)), whole((OWN, PAIR))],
            out_specs=[own_column] * 3,
            scratch_shapes=[
                pltpu.VMEM((count, CAP, QUAD), BF16),
                pltpu.VMEM((LONG, 2 * STAT, SEG), BF16),
                pltpu.VMEM((STAT, CAP), F32),
            ]
            + [pltpu.VMEM((OWN, QUAD), BF16)] * 4
            + [
                pltpu.VMEM((8, CAP), F32),
                pltpu.VMEM((OWN, PAIR), F32),
                pltpu.VMEM((OWN, PAIR), F32),
                pltpu.VMEM((OWN, PAIR), F32),
                pltpu.SemaphoreType.DMA((count, LONG)),
                pltpu.SemaphoreType.DMA((LONG,)),
            ],
        ),
        out_shape=[jax.ShapeDtypeStruct((OWN, count * QUAD), BF16)] * 3,
        compiler_params=pltpu.CompilerParams(vmem_limit_bytes=VMEM_LIMIT),
        cost_estimate=pl.CostEstimate(
            flops=BACK_COST, bytes_accessed=1_000_000, transcendentals=0
        ),
        name="attend_backward",
    )(meta, *pieces, *chain, mem_grad, mem_stats, own_stats)


def norm_stats(values):
    centered = values - jnp.mean(values, axis=-1, keepdims=True)
    scale = lax.rsqrt(jnp.mean(centered * centered, axis=-1, keepdims=True) + EPS)
    return centered * scale, scale


def norm_back(normed, scale, upstream):
    mean = jnp.mean(upstream, axis=-1, keepdims=True)
    along = jnp.mean(upstream * normed, axis=-1, keepdims=True)
    return scale * (upstream - mean - normed * along)


def turned(left, right):
    return lax.dot_general(left, right, LAST, preferred_element_type=F32)


def crossed(left, right):
    return lax.dot_general(left, right, (((0,), (0,)), ((), ())), preferred_element_type=F32)


def middle_body(
    meta, attended, lse, tokens, memory, token_cot, memory_cot,
    wo, bo, gain1, shift1, bi, b2, gain2, shift2, wi_from, w2_from,
    final, final_mem, payload, mem_grad, mem_stats, own_stats, res_grad, rows,
    attended_low, branch_out, first_low, inner_out, active, outer_out, sums, inner_sum,
    wi, w2, first, norm1, scale1, total, second_grad, outer_grad, slope, cots, weight_sems,
):
    width, inner_width = wi.shape
    wi_copy = pltpu.make_async_copy(wi_from, wi, weight_sems.at[0])
    w2_copy = pltpu.make_async_copy(w2_from, w2, weight_sems.at[1])
    wi_copy.start()
    w2_copy.start()
    chain = meta[M_CHAIN]
    lead = jnp.where(meta[M_SPOT] == 0, 1.0, 0.0)
    rows[0:SEG, :] = tokens[...]
    rows[SEG:OWN, :] = memory[chain]
    cots[0:SEG, :] = token_cot[...]
    cots[SEG:OWN, :] = memory_cot[chain]
    attended_low[...] = attended[...].astype(BF16)
    total[...] = jnp.dot(attended_low[...], wo[...], preferred_element_type=F32)
    sums[...] = jnp.zeros_like(sums)
    inner_sum[...] = jnp.zeros_like(inner_sum)
    vector = lambda ref: ref[...].astype(F32)

    def by_rows(run):
        def step(index, carry):
            start = pl.multiple_of(index * ROWS, ROWS)
            row = start + lax.broadcasted_iota(jnp.int32, (ROWS, 1), 0)
            live = (row < meta[M_USED]) | ((row >= SEG) & (row < SEG + meta[M_MEM]))
            counted = jnp.where(row < SEG, 1.0, lead)
            run(pl.ds(start, ROWS), live, counted)
            return carry

        lax.fori_loop(0, OWN // ROWS, step, 0)

    def by_columns(run):
        def step(index, carry):
            run(pl.ds(pl.multiple_of(index * COLS, COLS), COLS))
            return carry

        lax.fori_loop(0, inner_width // COLS, step, 0)

    def add(place, value):
        sums[place : place + 1, :] += jnp.sum(value, axis=0, keepdims=True)

    def first_part(span, live, counted):
        value = rows[span, :].astype(F32) + total[span, :] + vector(bo)
        normed, scale = norm_stats(value)
        norm1[span, :] = normed
        scale1[span, :] = jnp.broadcast_to(scale, (ROWS, PAIR))
        value = normed * vector(gain1) + vector(shift1)
        first[span, :] = value
        first_low[span, :] = value.astype(BF16)

    by_rows(first_part)
    wi_copy.wait()
    w2_copy.wait()
    total[...] = jnp.zeros_like(total)

    def inner_part(cols):
        inner = jnp.dot(first_low[...], wi[:, cols], preferred_element_type=F32)
        inner = inner + bi[:, cols].astype(F32)
        cdf = 0.5 * (1.0 + lax.erf(inner * (2.0**-0.5)))
        density = jnp.exp(-0.5 * inner * inner) * 0.3989422804014327
        slope[:, cols] = cdf + inner * density
        low = (inner * cdf).astype(BF16)
        active[:, cols] = low
        total[...] += jnp.dot(low, w2[cols, :], preferred_element_type=F32)

    by_columns(inner_part)

    def final_part(span, live, counted):
        normed, scale = norm_stats(first[span, :] + total[span, :] + vector(b2))
        value = jnp.where(live, normed * vector(gain2) + vector(shift2), 0.0)
        rows_low = value.astype(BF16)
        outer_out[span, :] = rows_low
        cot = cots[span, :].astype(F32)
        cot = jnp.where(live, cot, 0.0)
        weighted = cot * counted
        add(4, weighted * normed)
        add(5, weighted)
        grad = norm_back(normed, scale, cot * vector(gain2))
        second_grad[span, :] = grad
        outer_grad[span, :] = grad.astype(BF16)
        add(3, grad.astype(BF16).astype(F32) * counted)

    by_rows(final_part)
    final[...] = outer_out[0:SEG, :]
    final_mem[...] = outer_out[SEG:OWN, :]
    outer_out[0:SEG, :] = outer_grad[0:SEG, :]
    outer_out[SEG:OWN, :] = outer_grad[SEG:OWN, :] * lead.astype(BF16)
    total[...] = jnp.zeros_like(total)

    def inner_back(cols):
        grad = (turned(outer_grad[...], w2[cols, :]) * slope[:, cols]).astype(BF16)
        total[...] += turned(grad, wi[:, cols])
        tail = grad[SEG:OWN] * lead.astype(BF16)
        inner_out[0:SEG, cols] = grad[0:SEG]
        inner_out[SEG:OWN, cols] = tail
        inner_sum[:, cols] = jnp.sum(grad[0:SEG].astype(F32), axis=0, keepdims=True) + jnp.sum(
            tail.astype(F32), axis=0, keepdims=True
        )

    by_columns(inner_back)

    def last_part(span, live, counted):
        grad = second_grad[span, :] + total[span, :]
        normed = norm1[span, :]
        weighted = grad * counted
        add(1, weighted * normed)
        add(2, weighted)
        grad = norm_back(normed, scale1[span, 0:1], grad * vector(gain1))
        res_grad[span, :] = grad
        low = grad.astype(BF16)
        outer_grad[span, :] = low
        low = (low.astype(F32) * counted).astype(BF16)
        branch_out[span, :] = low
        add(0, low.astype(F32))

    by_rows(last_part)
    total[...] = turned(outer_grad[...], wo[...])
    feature = lax.broadcasted_iota(jnp.int32, (width, PAIR), 0)
    lane = lax.broadcasted_iota(jnp.int32, (width, PAIR), 1)
    head_of = jnp.where(feature // HD == lane - H, 1.0, 0.0).astype(BF16)

    def delta_part(span, live, counted):
        low = total[span, :].astype(BF16)
        outer_grad[span, :] = low
        product = low.astype(F32) * attended[span, :]
        high = product.astype(BF16)
        rest = (product - high.astype(F32)).astype(BF16)
        delta = jnp.dot(high, head_of, preferred_element_type=F32)
        delta = delta + jnp.dot(rest, head_of, preferred_element_type=F32)
        own_stats[span, :] = lse[span, :] + delta

    by_rows(delta_part)
    payload[0:SEG, :] = outer_grad[0:SEG, :]
    mem_grad[...] = outer_grad[SEG:OWN, :]
    stats = jnp.transpose(own_stats[0:SEG, :])[0:STAT]
    high = stats.astype(BF16)
    rest = (stats - high.astype(F32)).astype(BF16)
    both = jnp.concatenate([high.astype(F32), rest.astype(F32)], 0).astype(BF16)
    payload[SEG : SEG + 2 * STAT, 0:SEG] = both
    payload[SEG : SEG + 2 * STAT, SEG:width] = jnp.zeros((2 * STAT, width - SEG), BF16)
    mem_stats[...] = jnp.transpose(own_stats[OWN - PAIR : OWN, :])[0:STAT]


def middle(meta, attended, lse, tokens, memory, token_cot, memory_cot, weights):
    wo, bo, gain1, shift1, wi, bi, w2, b2, gain2, shift2 = weights
    width, inner_width = wi.shape
    vmem, line = pl.BlockSpec(memory_space=pltpu.VMEM), lambda value: value.reshape(1, -1)
    hbm = pl.BlockSpec(memory_space=pl.ANY)
    shape = jax.ShapeDtypeStruct
    return pl.pallas_call(
        middle_body,
        in_specs=[pl.BlockSpec(memory_space=pltpu.SMEM)] + [vmem] * 14 + [hbm] * 2,
        out_specs=[vmem] * 16,
        out_shape=[
            shape((SEG, width), BF16),
            shape((MEMP, width), BF16),
            shape((SEG + 2 * STAT, width), BF16),
            shape((MEMP, width), BF16),
            shape((STAT, PAIR), F32),
            shape((OWN, PAIR), F32),
            shape((OWN, width), F32),
            shape((OWN, width), BF16),
            shape((OWN, width), BF16),
            shape((OWN, width), BF16),
            shape((OWN, width), BF16),
            shape((OWN, inner_width), BF16),
            shape((OWN, inner_width), BF16),
            shape((OWN, width), BF16),
            shape((8, width), F32),
            shape((1, inner_width), F32),
        ],
        scratch_shapes=[
            pltpu.VMEM((width, inner_width), BF16),
            pltpu.VMEM((inner_width, width), BF16),
            pltpu.VMEM((OWN, width), F32),
            pltpu.VMEM((OWN, width), F32),
            pltpu.VMEM((OWN, PAIR), F32),
            pltpu.VMEM((OWN, width), F32),
            pltpu.VMEM((OWN, width), F32),
            pltpu.VMEM((OWN, width), BF16),
            pltpu.VMEM((OWN, inner_width), F32),
            pltpu.VMEM((OWN, width), BF16),
            pltpu.SemaphoreType.DMA((2,)),
        ],
        compiler_params=pltpu.CompilerParams(vmem_limit_bytes=VMEM_LIMIT),
        cost_estimate=pl.CostEstimate(
            flops=12_000_000_000, bytes_accessed=40_000_000, transcendentals=2_000_000
        ),
        name="middle",
    )(
        meta, attended, lse, tokens, memory, token_cot, memory_cot,
        wo, line(bo), line(gain1), line(shift1), line(bi), line(b2), line(gain2), line(shift2),
        wi, w2,
    )


def late_body(metas, group, *refs, batches, chains, parts):
    refs = list(refs)
    take = lambda count: [refs.pop(0) for _ in range(count)]
    rows, res_mem = take(batches), take(batches)
    grads = [[take(len(parts[b])) for _ in range(3)] for b in range(batches)]
    weights = take(3)
    out, masked = take(2)
    width = weights[0].shape[0]
    out[3 * width :, :] = jnp.zeros((out.shape[0] - 3 * width, width), BF16)
    for b in range(batches):
        lead = jnp.where(metas[b, M_SPOT] == 0, 1.0, 0.0)
        masked[b, 0:SEG, :] = rows[b][0:SEG, :]
        masked[b, SEG:OWN, :] = rows[b][SEG:OWN, :] * lead.astype(BF16)
        grad = res_mem[b][SEG:OWN, :]
        for k in range(3):
            first = 0
            for part, ref in zip(parts[b], grads[b][k]):
                grad = grad + turned(ref[SEG:OWN, :], weights[k][:, first : first + part])
                first += part
        place = ((group[0] * batches + b) * chains + metas[b, M_CHAIN]) * MEMP
        place = pl.multiple_of(3 * width + 16 + place, 16)
        out[pl.ds(place, MEMP), :] = (grad * lead).astype(BF16)
    cuts = sorted({sum(p[:i]) for p in parts for i in range(len(p) + 1)})
    for k in range(3):
        for low, high in zip(cuts[:-1], cuts[1:]):
            total, line = None, None
            for b in range(batches):
                lead = jnp.where(metas[b, M_SPOT] == 0, 1.0, 0.0)
                first = 0
                for part, ref in zip(parts[b], grads[b][k]):
                    if first <= low and high <= first + part:
                        grad = ref[:, low - first : high - first]
                    first += part
                value = crossed(masked[b], grad)
                total = value if total is None else total + value
                if k != 1:
                    grad = grad.astype(F32)
                    value = jnp.sum(grad[0:SEG], 0, keepdims=True)
                    value = value + jnp.sum(grad[SEG:OWN], 0, keepdims=True) * lead
                    line = value if line is None else line + value
            out[k * width : (k + 1) * width, low:high] = total.astype(BF16)
            if k != 1:
                row = lax.broadcasted_iota(jnp.int32, (16, high - low), 0)
                span = slice(3 * width, 3 * width + 16)
                old = out[span, low:high].astype(F32)
                out[span, low:high] = jnp.where(row == k // 2, line, old).astype(BF16)


def late_sums(metas, group, groups, chains, rows, res, grads, weights):
    batches, width = len(rows), weights[0].shape[0]
    parts = [[part.shape[1] for part in one[0]] for one in grads]
    count = 3 * width + 16 + groups * batches * chains * MEMP
    count += -count % LATE_ROWS
    vmem, smem = pl.BlockSpec(memory_space=pltpu.VMEM), pl.BlockSpec(memory_space=pltpu.SMEM)
    flat = [part for one in grads for name in one for part in name]
    return pl.pallas_call(
        functools.partial(late_body, batches=batches, chains=chains, parts=parts),
        in_specs=[smem] * 2 + [vmem] * (2 * batches + len(flat) + 3),
        out_specs=vmem,
        out_shape=jax.ShapeDtypeStruct((count, width), BF16),
        scratch_shapes=[pltpu.VMEM((batches, OWN, width), BF16)],
        compiler_params=pltpu.CompilerParams(vmem_limit_bytes=VMEM_LIMIT),
        name="late_sums",
    )(metas, group.reshape(1), *rows, *res, *flat, *weights)


def weight_grad(left, right):
    return lax.dot_general(left, right, (((0,), (0,)), ((), ())), preferred_element_type=F32)


def swap(value, mask):
    sizes = lax.axis_size("dp") * lax.axis_size("blk")
    return lax.ppermute(value, ("dp", "blk"), [(i, i ^ mask) for i in range(sizes)])


def sum_everywhere(value):
    blk = lax.axis_size("blk")
    place = lax.axis_index("dp") * blk + lax.axis_index("blk")
    groups = [(1,), (2, blk), (4, 8)]
    bit = 2 * blk
    while bit < blk * lax.axis_size("dp"):
        groups.append((bit,))
        bit *= 2
    masks_of = lambda group: [
        sum(bit for i, bit in enumerate(group) if (k >> i) & 1) for k in range(1 << len(group))
    ]
    own_of = lambda group: sum(((place // bit) % 2) << i for i, bit in enumerate(group))
    for group in groups:
        masks, own = masks_of(group), own_of(group)
        size = value.shape[0] // len(masks)
        part = lambda k: lax.dynamic_slice_in_dim(value, (own ^ k) * size, size)
        got = [swap(part(k), mask) for k, mask in enumerate(masks) if k]
        value = sum((g.astype(F32) for g in got), part(0).astype(F32)).astype(BF16)
    for group in reversed(groups):
        masks, own = masks_of(group), own_of(group)
        size = value.shape[0]
        got = [value] + [swap(value, mask) for mask in masks[1:]]
        value = jnp.zeros((size * len(masks), value.shape[1]), BF16)
        for k, part in enumerate(got):
            value = lax.dynamic_update_slice_in_dim(value, part, (own ^ k) * size, 0)
    return value


def local(
    tokens, memory, chain_lengths, last_fill,
    query_proj, query_bias, key_proj, value_proj, value_bias, output_proj, output_bias,
    attn_gain, attn_shift, inner_proj, inner_bias, outer_proj, outer_bias,
    final_gain, final_shift, token_cotangent, memory_cotangent,
):
    own = lax.axis_index("blk").astype(jnp.int32)
    group = lax.axis_index("dp").astype(jnp.int32)
    groups = lax.axis_size("dp")
    batches, _, width = tokens.shape
    chains, mem_rows = memory.shape[1:3]
    pad_mem = ((0, 0), (0, 0), (0, MEMP - mem_rows), (0, 0))
    memory, memory_cotangent = jnp.pad(memory, pad_mem), jnp.pad(memory_cotangent, pad_mem)

    metas = metas_of(own, chain_lengths[:, 0], last_fill[:, 0], mem_rows)
    near = gather_near(tokens[0])
    later, near = lax.optimization_barrier(([tokens[b] for b in range(1, batches)], near))
    pieces = [near] + [gather_all(part) for part in later]
    meta_of = [metas[b] for b in range(batches)]

    states = []
    for b in range(batches):
        meta = meta_of[b]
        attended, lse, *chain_rows = attend_forward(
            meta, pieces[b], memory[b], (query_proj, query_bias, key_proj, value_proj, value_bias)
        )
        (
            final, final_mem, payload, mem_grad, mem_stats, own_stats, res_grad, rows,
            attended_low, branch, first_low, inner, active, outer, sums, inner_sum,
        ) = middle(
            meta, attended, lse, tokens[b], memory[b], token_cotangent[b], memory_cotangent[b],
            (
                output_proj, output_bias, attn_gain, attn_shift, inner_proj, inner_bias,
                outer_proj, outer_bias, final_gain, final_shift,
            ),
        )
        if b + 1 < batches:
            meta_of[b + 1], payload = lax.optimization_barrier((meta_of[b + 1], payload))
        states.append(
            dict(
                meta=meta, rows=rows, chain_rows=chain_rows, payload=payload, mem_grad=mem_grad,
                mem_stats=mem_stats, own_stats=own_stats, res_grad=res_grad, final=final,
                final_mem=final_mem, attended_low=attended_low, branch=branch,
                first_low=first_low, inner=inner, active=active, outer=outer, sums=sums,
                inner_sum=inner_sum,
            )
        )

    def over_batches(left, right):
        return weight_grad(
            jnp.concatenate([s[left] for s in states], 0),
            jnp.concatenate([s[right] for s in states], 0),
        ).astype(BF16)

    slots = (jnp.arange(groups)[:, None, None, None, None] == group) & (
        jnp.arange(chains)[:, None, None]
        == jnp.where(metas[:, M_SPOT] == 0, metas[:, M_CHAIN], -1)[:, None, None, None]
    )
    final_mem = jnp.stack([s["final_mem"] for s in states])[None, :, None]
    early = (
        over_batches("first_low", "inner"),
        over_batches("active", "outer"),
        over_batches("attended_low", "branch"),
        jnp.concatenate(
            [
                jnp.where(slots, final_mem, 0).astype(BF16).reshape(-1, width),
                sum(s["sums"] for s in states).astype(BF16),
                sum(s["inner_sum"] for s in states).astype(BF16).reshape(-1, width),
            ],
            0,
        ),
    )
    early, *held = lax.optimization_barrier((early, *[s["meta"] for s in states]))
    for s, meta in zip(states, held):
        s["meta"] = meta
        s["gathered"] = gather_all(s["payload"])
    def backward(s, meta):
        return attend_backward(
            meta, s["gathered"], s["chain_rows"], s["mem_grad"], s["mem_stats"],
            s["own_stats"], 0, NQUAD,
        )

    *others, last = states
    for s in others:
        s["grads"] = backward(s, s["meta"])
    got, last["gathered"], early = lax.optimization_barrier(
        ([s["grads"] for s in others], last["gathered"], early)
    )
    for s, grads in zip(others, got):
        s["grads"] = grads
    early = lax.psum(early, ("dp", "blk"))

    def late_part(turn, carry):
        grads = backward(last, last["meta"] + turn)
        every = [s["grads"] for s in others] + [grads]
        late = late_sums(
            metas, group, groups, chains, [s["rows"] for s in states],
            [s["res_grad"] for s in states], [[[part] for part in one] for one in every],
            (query_proj, key_proj, value_proj),
        )
        return sum_everywhere(late), grads

    once = jnp.minimum(metas[0, M_LEN], 1)
    start = jax.tree.map(
        lambda like: jnp.zeros(like.shape, like.dtype), jax.eval_shape(late_part, once, None)
    )
    late, last["grads"] = lax.fori_loop(0, once, late_part, start)
    late, early = lax.optimization_barrier((late, early))
    grad_inner, grad_outer, grad_output, rest = early

    def own_slots(rows):
        rows = rows.reshape(groups, batches, chains, MEMP, width)
        return lax.dynamic_index_in_dim(rows, group, keepdims=False)[:, :, :mem_rows]

    grad_query, grad_key, grad_value = (late[i * width : (i + 1) * width] for i in range(3))
    biases = late[3 * width : 3 * width + 2].astype(F32)
    count = groups * batches * chains * MEMP
    memory_grad = own_slots(late[3 * width + 16 : 3 * width + 16 + count])
    memory_out = own_slots(rest[:count])
    sums, inner_sum = rest[count : count + 8], rest[count + 8 :].reshape(1, -1)
    token_outs = [s["final"] for s in states]
    token_grads = []
    for s in states:
        grad = s["res_grad"][:SEG]
        for part, weights in zip(s["grads"], (query_proj, key_proj, value_proj)):
            grad = grad + turned(part[:SEG], weights)
        token_grads.append(grad.astype(BF16))

    wide = lambda value: value.astype(F32)
    return (
        jnp.stack(token_outs),
        memory_out,
        jnp.stack(token_grads),
        memory_grad,
        wide(grad_query),
        biases[0],
        wide(grad_key),
        wide(grad_value),
        biases[1],
        wide(grad_output),
        wide(sums[0]),
        wide(sums[1]),
        wide(sums[2]),
        wide(grad_inner),
        wide(inner_sum[0]),
        wide(grad_outer),
        wide(sums[3]),
        wide(sums[4]),
        wide(sums[5]),
    )


def solution(mesh):
    row_spec = P(None, ("dp", "blk"), None)
    mem_spec = P(None, "dp", None, None)
    int_spec = P(None, "dp", None)
    in_specs = (row_spec, mem_spec, int_spec, int_spec) + (P(),) * 15 + (row_spec, mem_spec)
    out_specs = (row_spec, mem_spec, row_spec, mem_spec) + (P(),) * 15
    return jax.shard_map(local, mesh=mesh, in_specs=in_specs, out_specs=out_specs, check_vma=False)
```

```python
import functools

import jax
import jax.numpy as jnp
from jax import lax
from jax.experimental import pallas as pl
from jax.experimental.pallas import tpu as pltpu
from jax.sharding import PartitionSpec as P

H = 12
HD = 64
QUAD = 256
NQUAD = 3
PAIR = 128
MEMP = 32
SEG = 512
LONG = 7
NBLK = LONG + 1
CAP = NBLK * SEG
OWN = SEG + MEMP
STAT = 24
BACK_COST = 10_000_000_000
LATE_ROWS = 256
NPIECE = 14
ROWS = 272
COLS = 1024
NEG = -1e30
SHIFT_FREE = 60.0
EPS = 1e-05
F32 = jnp.float32
BF16 = jnp.bfloat16
VMEM_LIMIT = 60 * 2**20
LAST = (((1,), (1,)), ((), ()))

M_LEN, M_ROWS, M_BLOCKS, M_SPOT, M_USED, M_MEM, M_CHAIN, M_START, M_PIECE = range(9)


def plane_moves(shift_of):
    pairs = []
    for plane in range(4):
        for place in range(4):
            target = plane + shift_of(place >> 1)
            if 0 <= target < 4:
                pairs.append((4 * plane + place, 4 * target + place))
    return pairs


UP = plane_moves(lambda side: 1)
DOWN = plane_moves(lambda side: -1)
OUTWARD = plane_moves(lambda side: 1 if side else -1)
SIDE = [(i, i ^ 2) for i in range(16)]
CORE = [(i, i ^ 1) for i in range(16)]


def move(value, pairs):
    return lax.ppermute(value, "blk", pairs)


def gather_near(value, others):
    side = (lax.axis_index("blk") >> 1) & 1
    below, above, beside = move(value, UP), move(value, DOWN), move(value, SIDE)
    below, others = lax.optimization_barrier((below, others))
    far = move(jnp.where(side == 1, below, above), OUTWARD)
    moved = [move(beside, UP), move(beside, DOWN), move(far, SIDE)]
    here = [value, beside, below, above] + moved
    return here + [move(part, CORE) for part in here], others


def gather_all(value):
    return [lax.all_gather(value, "blk")]


def piece_of(own, other):
    plane = (other >> 2) - (own >> 2)
    same_side = ((other >> 1) & 1) == ((own >> 1) & 1)
    on_side = jnp.where(plane == 0, 0, jnp.where(plane < 0, 2, 3))
    off_side = jnp.where(plane == 0, 1, jnp.where(plane == -1, 4, jnp.where(plane == 1, 5, 6)))
    index = jnp.where(same_side, on_side, off_side)
    return index + jnp.where((other & 1) == (own & 1), 0, LONG)


def meta_body(own_ref, lengths, fills, meta, *, batches, chains, mem_rows):
    own = own_ref[0]
    for b in range(batches):
        end = jnp.int32(0)
        length, start, fill, chain = (jnp.int32(0) for _ in range(4))
        for c in range(chains):
            begin = end
            end = end + lengths[b, c]
            inside = (begin <= own) & (own < end)
            length = jnp.where(inside, lengths[b, c], length)
            start = jnp.where(inside, begin, start)
            fill = jnp.where(inside, fills[b, c], fill)
            chain = jnp.where(inside, c, chain)
        rows = MEMP + SEG * (length - 1) + fill
        spot = own - start
        meta[b, M_LEN] = length
        meta[b, M_ROWS] = rows
        meta[b, M_BLOCKS] = (rows + SEG - 1) // SEG
        meta[b, M_SPOT] = spot
        meta[b, M_USED] = jnp.where(spot == length - 1, fill, SEG)
        meta[b, M_MEM] = jnp.int32(mem_rows)
        meta[b, M_CHAIN] = chain
        meta[b, M_START] = start
        for place in range(8):
            meta[b, M_PIECE + place] = piece_of(own, start + place)


def metas_of(own, lengths, fills, mem_rows):
    smem = pl.BlockSpec(memory_space=pltpu.SMEM)
    body = functools.partial(
        meta_body, batches=lengths.shape[0], chains=lengths.shape[1], mem_rows=mem_rows
    )
    return pl.pallas_call(
        body,
        in_specs=[smem] * 3,
        out_specs=smem,
        out_shape=jax.ShapeDtypeStruct((lengths.shape[0], 16), jnp.int32),
        name="find_chain",
    )(own.reshape(1), lengths, fills)


def load_chain(meta, pieces, view_from, view_to, sems):
    length = meta[M_LEN]
    for spot in range(LONG):
        def start(source):
            pltpu.make_async_copy(view_from(source), view_to(spot), sems.at[spot]).start()

        @pl.when(spot < length)
        def _():
            if len(pieces) == 1:
                start(pieces[0].at[meta[M_START] + spot])
                return
            for index in range(len(pieces)):
                @pl.when(meta[M_PIECE + spot] == index)
                def _():
                    start(pieces[index])


def wait_chain(meta, pieces, view_from, view_to, sems):
    length = meta[M_LEN]
    source = pieces[0].at[0] if len(pieces) == 1 else pieces[0]
    for spot in range(LONG):
        @pl.when(spot < length)
        def _():
            pltpu.make_async_copy(view_from(source), view_to(spot), sems.at[spot]).wait()


def key_bias(meta):
    column = lax.broadcasted_iota(jnp.int32, (8, CAP), 1)
    dead = (column >= meta[M_ROWS]) | ((column >= meta[M_MEM]) & (column < MEMP))
    return jnp.where(dead, NEG, 0.0).astype(F32)


def by_chunks(blocks, run):
    def four(index, carry):
        run(index * 4, 4)
        return carry

    lax.fori_loop(0, blocks // 4, four, 0)
    for count in (1, 2, 3):
        @pl.when(blocks % 4 == count)
        def _():
            run((blocks // 4) * 4, count)


def span_of(first, count):
    return pl.ds(pl.multiple_of(first * SEG, SEG), count * SEG)


def forward_body(meta, *refs):
    pieces, refs = refs[:-16], refs[-16:]
    mem, wq, wk, wv, bq, bv, out, lse, kc, vc, qc, rows, qown, extended, acc, sems = refs
    quad = pl.program_id(0)
    width = rows.shape[1]
    length, blocks = meta[M_LEN], meta[M_BLOCKS]
    here = lambda source: source
    there = lambda spot: rows.at[pl.ds(MEMP + SEG * spot, SEG)]

    @pl.when(quad == 0)
    def _():
        load_chain(meta, pieces, here, there, sems)
        rows[0:MEMP, :] = mem[meta[M_CHAIN]]
        lse[...] = jnp.zeros_like(lse)

        @pl.when(blocks > length)
        def _():
            place = pl.multiple_of(MEMP + SEG * length, MEMP)
            rows[pl.ds(place, SEG - MEMP), :] = jnp.zeros((SEG - MEMP, width), BF16)

        wait_chain(meta, pieces, here, there, sems)

    def longest(values):
        halves = [
            jnp.max(jnp.sum(jnp.square(values[:, p : p + PAIR]), axis=1, keepdims=True))
            for p in range(0, QUAD, PAIR)
        ]
        return jnp.maximum(*halves)

    def project(start, count):
        span = pl.ds(pl.multiple_of(start, MEMP), count)
        part = rows[span, :]
        row = start + lax.broadcasted_iota(jnp.int32, (count, QUAD), 0)
        alive = (row < meta[M_ROWS]) & ((row < meta[M_MEM]) | (row >= MEMP))
        lower = (lax.broadcasted_iota(jnp.int32, (count, QUAD), 1) % PAIR) < HD
        key = jnp.dot(part, wk[...], preferred_element_type=F32)
        kc[span, :] = key.astype(BF16)
        value = jnp.dot(part, wv[...], preferred_element_type=F32) + bv[...].astype(F32)
        vc[span, :] = value.astype(BF16)
        value = jnp.where(alive, value, 0.0)
        one = jnp.where(alive, 1.0, 0.0)
        extended[0, span, :] = jnp.where(lower, value, one).astype(BF16)
        extended[1, span, :] = jnp.where(lower, one, value).astype(BF16)
        query = jnp.dot(part, wq[...], preferred_element_type=F32) + bq[...].astype(F32)
        query = query.astype(BF16) * jnp.asarray(HD**-0.5, BF16)
        qc[span, :] = query
        return longest(key)

    def project_block(block, top):
        return jnp.maximum(top, project(block * SEG, SEG))

    key_top = lax.fori_loop(0, blocks, project_block, jnp.float32(0.0))

    @pl.when(blocks == length)
    def _():
        project(length * SEG, MEMP)

    place = pl.multiple_of(MEMP + SEG * meta[M_SPOT], MEMP)
    qown[0:SEG, :] = qc[pl.ds(place, SEG), :]
    qown[SEG:OWN, :] = qc[0:MEMP, :]
    near = longest(qown[...].astype(F32)) * key_top <= SHIFT_FREE**2

    def pair(index, carry):
        cols = pl.ds(pl.multiple_of(index * PAIR, PAIR), PAIR)
        lane = lax.broadcasted_iota(jnp.int32, (OWN, PAIR), 1)
        halves = (0, 1)
        mine = [(lane // HD) == half for half in halves]
        numbers = [lane == quad * 4 + index * 2 + half for half in halves]
        both = qown[:, cols]
        queries = [jnp.where(mine[half], both, jnp.zeros_like(both)) for half in halves]
        acc[...] = jnp.zeros_like(acc)

        def score(half, span):
            return lax.dot_general(queries[half], kc[span, cols], LAST, preferred_element_type=F32)

        def gather(half, span, terms):
            values = extended[half, span, cols]
            return jnp.dot(terms.astype(BF16), values, preferred_element_type=F32)

        @pl.when(near)
        def _():
            def run(first, count):
                span = span_of(first, count)
                for half in halves:
                    acc[half] += gather(half, span, jnp.exp(score(half, span)))

            by_chunks(blocks, run)

        @pl.when(jnp.logical_not(near))
        def _():
            for half in halves:
                def run(block, top):
                    span = span_of(block, 1)
                    column = block * SEG + lax.broadcasted_iota(jnp.int32, (OWN, SEG), 1)
                    dead = (column >= meta[M_ROWS]) | ((column >= meta[M_MEM]) & (column < MEMP))
                    scores = jnp.where(dead, NEG, score(half, span))
                    new = jnp.maximum(top, jnp.max(scores, axis=1, keepdims=True))
                    terms = gather(half, span, jnp.exp(scores - new))
                    acc[half] = acc[half] * jnp.exp(top - new) + terms
                    return new

                top = lax.fori_loop(0, blocks, run, jnp.full((OWN, 1), NEG, F32))
                lse[...] = jnp.where(numbers[half], top, lse[...])

        sums = [acc[half] for half in halves]
        value = jnp.where(mine[0], sums[0], sums[1])
        total = pltpu.roll(jnp.where(mine[0], sums[1], sums[0]), HD, 1)
        out[:, cols] = value * (1.0 / total)
        turned_total = pltpu.roll(total, HD, 1)
        for half in halves:
            spread = jnp.where(mine[half], total, turned_total)
            lse[...] += jnp.where(numbers[half], jnp.log(spread), 0.0)
        return carry

    lax.fori_loop(0, 2, pair, 0)


def attend_forward(meta, pieces, mem, weights):
    wq, bq, wk, wv, bv = weights
    width = wq.shape[0]
    whole = lambda shape: pl.BlockSpec(shape, lambda quad, meta: (0,) * len(shape))
    column = lambda count: pl.BlockSpec((count, QUAD), lambda quad, meta: (0, quad))
    return pl.pallas_call(
        forward_body,
        grid_spec=pltpu.PrefetchScalarGridSpec(
            num_scalar_prefetch=1,
            grid=(NQUAD,),
            in_specs=[pl.BlockSpec(memory_space=pl.ANY)] * len(pieces)
            + [whole((mem.shape[0], MEMP, width))]
            + [column(width)] * 3
            + [column(1)] * 2,
            out_specs=[column(OWN), whole((OWN, PAIR))] + [column(CAP)] * 3,
            scratch_shapes=[
                pltpu.VMEM((CAP, width), BF16),
                pltpu.VMEM((OWN, QUAD), BF16),
                pltpu.VMEM((2, CAP, QUAD), BF16),
                pltpu.VMEM((2, OWN, PAIR), F32),
                pltpu.SemaphoreType.DMA((LONG,)),
            ],
        ),
        out_shape=[
            jax.ShapeDtypeStruct((OWN, width), F32),
            jax.ShapeDtypeStruct((OWN, PAIR), F32),
        ]
        + [jax.ShapeDtypeStruct((CAP, width), BF16)] * 3,
        compiler_params=pltpu.CompilerParams(vmem_limit_bytes=VMEM_LIMIT),
        cost_estimate=pl.CostEstimate(
            flops=40_000_000_000, bytes_accessed=30_000_000, transcendentals=23_000_000
        ),
        name="attend_forward",
    )(meta, *pieces, mem, wq, wk, wv, bq.reshape(1, -1), bv.reshape(1, -1))


def backward_body(start, count, meta, *refs):
    pieces, refs = refs[:-22], refs[-22:]
    (
        kc, vc, qc, mem_grad, mem_stats, own_stats,
        dq, dk, dv,
        doc, stats, chain_stats, qown, kown, vown, down, bias, qacc, kacc, vacc, sems, stat_sems,
    ) = refs
    step = pl.program_id(0)
    quad = start + step
    length = meta[M_LEN]

    @pl.when(step == 0)
    def _():
        rows_from = lambda index: lambda ref: ref.at[0:SEG, pl.ds((start + index) * QUAD, QUAD)]
        rows_to = lambda index: lambda spot: doc.at[index, pl.ds(MEMP + SEG * spot, SEG)]
        stat_from = lambda ref: ref.at[SEG : SEG + 2 * STAT, 0:SEG]
        stat_to = lambda spot: stats.at[spot]
        load_chain(meta, pieces, stat_from, stat_to, stat_sems)
        for index in range(count):
            load_chain(meta, pieces, rows_from(index), rows_to(index), sems.at[index])
        bias[...] = key_bias(meta)
        for index in range(count):
            doc[index, 0:MEMP, :] = mem_grad[:, (start + index) * QUAD : (start + index + 1) * QUAD]

            @pl.when(meta[M_BLOCKS] > length)
            def _():
                place = pl.multiple_of(MEMP + SEG * length, MEMP)
                doc[index, pl.ds(place, SEG - MEMP), :] = jnp.zeros((SEG - MEMP, QUAD), BF16)

        wait_chain(meta, pieces, stat_from, stat_to, stat_sems)
        for spot in range(NBLK):
            span = slice(SEG * spot, SEG * (spot + 1))
            if spot == LONG:
                chain_stats[:, span] = jnp.zeros((STAT, SEG), F32)
                continue

            @pl.when(spot < length)
            def _():
                pair = stats[spot].astype(F32)
                chain_stats[:, span] = pair[0:STAT] + pair[STAT : 2 * STAT]

            @pl.when(spot >= length)
            def _():
                chain_stats[:, span] = jnp.zeros((STAT, SEG), F32)

        moved = pltpu.roll(chain_stats[...], MEMP, 1)
        column = lax.broadcasted_iota(jnp.int32, (STAT, CAP), 1)
        entry = lax.broadcasted_iota(jnp.int32, (STAT, CAP), 0)
        beyond = jnp.where(entry < H, -NEG, 0.0)
        chain_stats[...] = jnp.where(column < MEMP + SEG * length, moved, beyond)
        lane = lax.broadcasted_iota(jnp.int32, (STAT, PAIR), 1)
        at_front = pltpu.roll(mem_stats[...], MEMP, 1)
        chain_stats[:, 0:PAIR] = jnp.where(lane < MEMP, at_front, chain_stats[:, 0:PAIR])
        for index in range(count):
            wait_chain(meta, pieces, rows_from(index), rows_to(index), sems.at[index])

    place = pl.multiple_of(MEMP + SEG * meta[M_SPOT], MEMP)
    for own, chain in ((qown, qc), (kown, kc), (vown, vc), (down, doc.at[step])):
        own[0:SEG, :] = chain[pl.ds(place, SEG), :]
        own[SEG:OWN, :] = chain[0:MEMP, :]

    def head(index, carry):
        cols = pl.ds(pl.multiple_of((index // 2) * PAIR, PAIR), PAIR)
        number = quad * 4 + index
        lane = lax.broadcasted_iota(jnp.int32, (OWN, PAIR), 1)
        mine = (lane // HD) == (index % 2)
        masked = lambda ref: jnp.where(mine, ref[:, cols], jnp.zeros((OWN, PAIR), BF16))
        query, key, value, grad = masked(qown), masked(kown), masked(vown), masked(down)
        pick = lambda at: jnp.sum(jnp.where(lane == at, own_stats[...], 0.0), axis=1, keepdims=True)
        log_total, delta = pick(number), pick(H + number)
        for acc in (qacc, kacc, vacc):
            acc[...] = jnp.zeros_like(acc)

        def run(first, size):
            span = span_of(first, size)
            keys, values = kc[span, cols], vc[span, cols]
            scores = lax.dot_general(query, keys, LAST, preferred_element_type=F32)
            weights = jnp.exp(scores + bias[0:1, span] - log_total)
            weight_grad = lax.dot_general(grad, values, LAST, preferred_element_type=F32)
            score_grad = (weights * (weight_grad - delta)).astype(BF16)
            qacc[...] += jnp.dot(score_grad, keys, preferred_element_type=F32)

            queries, grads = qc[span, cols], doc[step, span, cols]
            scores = lax.dot_general(key, queries, LAST, preferred_element_type=F32)
            weights = jnp.exp(scores - chain_stats[pl.ds(number, 1), span])
            weight_grad = lax.dot_general(value, grads, LAST, preferred_element_type=F32)
            score_grad = (
                weights * (weight_grad - chain_stats[pl.ds(H + number, 1), span])
            ).astype(BF16)
            vacc[...] += jnp.dot(weights.astype(BF16), grads, preferred_element_type=F32)
            kacc[...] += jnp.dot(score_grad, queries, preferred_element_type=F32)

        by_chunks(meta[M_BLOCKS], run)
        row = lax.broadcasted_iota(jnp.int32, (OWN, PAIR), 0)
        alive = (row < meta[M_USED]) | ((row >= SEG) & (row < SEG + meta[M_MEM]))
        query_sum = qacc[...] * (HD**-0.5)
        key_sum = jnp.where(alive, kacc[...], 0.0)
        value_sum = jnp.where(alive, vacc[...], 0.0)
        for ref, sums in ((dq, query_sum), (dk, key_sum), (dv, value_sum)):
            ref[:, cols] = jnp.where(mine, sums.astype(BF16), ref[:, cols])
        return carry

    lax.fori_loop(0, 4, head, 0)


def attend_backward(meta, pieces, chain, mem_grad, mem_stats, own_stats, start, count):
    width = mem_grad.shape[1]
    whole = lambda shape: pl.BlockSpec(shape, lambda quad, meta: (0,) * len(shape))
    chain_column = pl.BlockSpec((CAP, QUAD), lambda step, meta: (0, start + step))
    own_column = pl.BlockSpec((OWN, QUAD), lambda step, meta: (0, step))
    return pl.pallas_call(
        functools.partial(backward_body, start, count),
        grid_spec=pltpu.PrefetchScalarGridSpec(
            num_scalar_prefetch=1,
            grid=(count,),
            in_specs=[pl.BlockSpec(memory_space=pl.ANY)] * len(pieces)
            + [chain_column] * 3
            + [whole((MEMP, width)), whole((STAT, PAIR)), whole((OWN, PAIR))],
            out_specs=[own_column] * 3,
            scratch_shapes=[
                pltpu.VMEM((count, CAP, QUAD), BF16),
                pltpu.VMEM((LONG, 2 * STAT, SEG), BF16),
                pltpu.VMEM((STAT, CAP), F32),
            ]
            + [pltpu.VMEM((OWN, QUAD), BF16)] * 4
            + [
                pltpu.VMEM((8, CAP), F32),
                pltpu.VMEM((OWN, PAIR), F32),
                pltpu.VMEM((OWN, PAIR), F32),
                pltpu.VMEM((OWN, PAIR), F32),
                pltpu.SemaphoreType.DMA((count, LONG)),
                pltpu.SemaphoreType.DMA((LONG,)),
            ],
        ),
        out_shape=[jax.ShapeDtypeStruct((OWN, count * QUAD), BF16)] * 3,
        compiler_params=pltpu.CompilerParams(vmem_limit_bytes=VMEM_LIMIT),
        cost_estimate=pl.CostEstimate(
            flops=BACK_COST, bytes_accessed=1_000_000, transcendentals=0
        ),
        name="attend_backward",
    )(meta, *pieces, *chain, mem_grad, mem_stats, own_stats)


def norm_stats(values):
    centered = values - jnp.mean(values, axis=-1, keepdims=True)
    scale = lax.rsqrt(jnp.mean(centered * centered, axis=-1, keepdims=True) + EPS)
    return centered * scale, scale


def norm_back(normed, scale, upstream):
    mean = jnp.mean(upstream, axis=-1, keepdims=True)
    along = jnp.mean(upstream * normed, axis=-1, keepdims=True)
    return scale * (upstream - mean - normed * along)


def turned(left, right):
    return lax.dot_general(left, right, LAST, preferred_element_type=F32)


def crossed(left, right):
    return lax.dot_general(left, right, (((0,), (0,)), ((), ())), preferred_element_type=F32)


def middle_body(
    meta, attended, lse, tokens, memory, token_cot, memory_cot,
    wo, bo, gain1, shift1, bi, b2, gain2, shift2, wi_from, w2_from,
    final, final_mem, payload, mem_grad, mem_stats, own_stats, res_grad, rows,
    attended_low, branch_out, first_low, inner_out, active, outer_out, sums, inner_sum,
    wi, w2, first, norm1, scale1, total, second_grad, outer_grad, slope, cots, weight_sems,
):
    width, inner_width = wi.shape
    wi_copy = pltpu.make_async_copy(wi_from, wi, weight_sems.at[0])
    w2_copy = pltpu.make_async_copy(w2_from, w2, weight_sems.at[1])
    wi_copy.start()
    w2_copy.start()
    chain = meta[M_CHAIN]
    lead = jnp.where(meta[M_SPOT] == 0, 1.0, 0.0)
    rows[0:SEG, :] = tokens[...]
    rows[SEG:OWN, :] = memory[chain]
    cots[0:SEG, :] = token_cot[...]
    cots[SEG:OWN, :] = memory_cot[chain]
    attended_low[...] = attended[...].astype(BF16)
    total[...] = jnp.dot(attended_low[...], wo[...], preferred_element_type=F32)
    sums[...] = jnp.zeros_like(sums)
    inner_sum[...] = jnp.zeros_like(inner_sum)
    vector = lambda ref: ref[...].astype(F32)

    def by_rows(run):
        def step(index, carry):
            start = pl.multiple_of(index * ROWS, ROWS)
            row = start + lax.broadcasted_iota(jnp.int32, (ROWS, 1), 0)
            live = (row < meta[M_USED]) | ((row >= SEG) & (row < SEG + meta[M_MEM]))
            counted = jnp.where(row < SEG, 1.0, lead)
            run(pl.ds(start, ROWS), live, counted)
            return carry

        lax.fori_loop(0, OWN // ROWS, step, 0)

    def by_columns(run):
        def step(index, carry):
            run(pl.ds(pl.multiple_of(index * COLS, COLS), COLS))
            return carry

        lax.fori_loop(0, inner_width // COLS, step, 0)

    def add(place, value):
        sums[place : place + 1, :] += jnp.sum(value, axis=0, keepdims=True)

    def first_part(span, live, counted):
        value = rows[span, :].astype(F32) + total[span, :] + vector(bo)
        normed, scale = norm_stats(value)
        norm1[span, :] = normed
        scale1[span, :] = jnp.broadcast_to(scale, (ROWS, PAIR))
        value = normed * vector(gain1) + vector(shift1)
        first[span, :] = value
        first_low[span, :] = value.astype(BF16)

    by_rows(first_part)
    wi_copy.wait()
    w2_copy.wait()
    total[...] = jnp.zeros_like(total)

    def inner_part(cols):
        inner = jnp.dot(first_low[...], wi[:, cols], preferred_element_type=F32)
        inner = inner + bi[:, cols].astype(F32)
        cdf = 0.5 * (1.0 + lax.erf(inner * (2.0**-0.5)))
        density = jnp.exp(-0.5 * inner * inner) * 0.3989422804014327
        slope[:, cols] = cdf + inner * density
        low = (inner * cdf).astype(BF16)
        active[:, cols] = low
        total[...] += jnp.dot(low, w2[cols, :], preferred_element_type=F32)

    by_columns(inner_part)

    def final_part(span, live, counted):
        normed, scale = norm_stats(first[span, :] + total[span, :] + vector(b2))
        value = jnp.where(live, normed * vector(gain2) + vector(shift2), 0.0)
        rows_low = value.astype(BF16)
        outer_out[span, :] = rows_low
        cot = cots[span, :].astype(F32)
        cot = jnp.where(live, cot, 0.0)
        weighted = cot * counted
        add(4, weighted * normed)
        add(5, weighted)
        grad = norm_back(normed, scale, cot * vector(gain2))
        second_grad[span, :] = grad
        outer_grad[span, :] = grad.astype(BF16)
        add(3, grad.astype(BF16).astype(F32) * counted)

    by_rows(final_part)
    final[...] = outer_out[0:SEG, :]
    final_mem[...] = outer_out[SEG:OWN, :]
    outer_out[0:SEG, :] = outer_grad[0:SEG, :]
    outer_out[SEG:OWN, :] = outer_grad[SEG:OWN, :] * lead.astype(BF16)
    total[...] = jnp.zeros_like(total)

    def inner_back(cols):
        grad = (turned(outer_grad[...], w2[cols, :]) * slope[:, cols]).astype(BF16)
        total[...] += turned(grad, wi[:, cols])
        tail = grad[SEG:OWN] * lead.astype(BF16)
        inner_out[0:SEG, cols] = grad[0:SEG]
        inner_out[SEG:OWN, cols] = tail
        inner_sum[:, cols] = jnp.sum(grad[0:SEG].astype(F32), axis=0, keepdims=True) + jnp.sum(
            tail.astype(F32), axis=0, keepdims=True
        )

    by_columns(inner_back)

    def last_part(span, live, counted):
        grad = second_grad[span, :] + total[span, :]
        normed = norm1[span, :]
        weighted = grad * counted
        add(1, weighted * normed)
        add(2, weighted)
        grad = norm_back(normed, scale1[span, 0:1], grad * vector(gain1))
        res_grad[span, :] = grad
        low = grad.astype(BF16)
        outer_grad[span, :] = low
        low = (low.astype(F32) * counted).astype(BF16)
        branch_out[span, :] = low
        add(0, low.astype(F32))

    by_rows(last_part)
    total[...] = turned(outer_grad[...], wo[...])
    feature = lax.broadcasted_iota(jnp.int32, (width, PAIR), 0)
    lane = lax.broadcasted_iota(jnp.int32, (width, PAIR), 1)
    head_of = jnp.where(feature // HD == lane - H, 1.0, 0.0).astype(BF16)

    def delta_part(span, live, counted):
        low = total[span, :].astype(BF16)
        outer_grad[span, :] = low
        product = low.astype(F32) * attended[span, :]
        high = product.astype(BF16)
        rest = (product - high.astype(F32)).astype(BF16)
        delta = jnp.dot(high, head_of, preferred_element_type=F32)
        delta = delta + jnp.dot(rest, head_of, preferred_element_type=F32)
        own_stats[span, :] = lse[span, :] + delta

    by_rows(delta_part)
    payload[0:SEG, :] = outer_grad[0:SEG, :]
    mem_grad[...] = outer_grad[SEG:OWN, :]
    stats = jnp.transpose(own_stats[0:SEG, :])[0:STAT]
    high = stats.astype(BF16)
    rest = (stats - high.astype(F32)).astype(BF16)
    both = jnp.concatenate([high.astype(F32), rest.astype(F32)], 0).astype(BF16)
    payload[SEG : SEG + 2 * STAT, 0:SEG] = both
    payload[SEG : SEG + 2 * STAT, SEG:width] = jnp.zeros((2 * STAT, width - SEG), BF16)
    mem_stats[...] = jnp.transpose(own_stats[OWN - PAIR : OWN, :])[0:STAT]


def middle(meta, attended, lse, tokens, memory, token_cot, memory_cot, weights):
    wo, bo, gain1, shift1, wi, bi, w2, b2, gain2, shift2 = weights
    width, inner_width = wi.shape
    vmem, line = pl.BlockSpec(memory_space=pltpu.VMEM), lambda value: value.reshape(1, -1)
    hbm = pl.BlockSpec(memory_space=pl.ANY)
    shape = jax.ShapeDtypeStruct
    return pl.pallas_call(
        middle_body,
        in_specs=[pl.BlockSpec(memory_space=pltpu.SMEM)] + [vmem] * 14 + [hbm] * 2,
        out_specs=[vmem] * 16,
        out_shape=[
            shape((SEG, width), BF16),
            shape((MEMP, width), BF16),
            shape((SEG + 2 * STAT, width), BF16),
            shape((MEMP, width), BF16),
            shape((STAT, PAIR), F32),
            shape((OWN, PAIR), F32),
            shape((OWN, width), F32),
            shape((OWN, width), BF16),
            shape((OWN, width), BF16),
            shape((OWN, width), BF16),
            shape((OWN, width), BF16),
            shape((OWN, inner_width), BF16),
            shape((OWN, inner_width), BF16),
            shape((OWN, width), BF16),
            shape((8, width), F32),
            shape((1, inner_width), F32),
        ],
        scratch_shapes=[
            pltpu.VMEM((width, inner_width), BF16),
            pltpu.VMEM((inner_width, width), BF16),
            pltpu.VMEM((OWN, width), F32),
            pltpu.VMEM((OWN, width), F32),
            pltpu.VMEM((OWN, PAIR), F32),
            pltpu.VMEM((OWN, width), F32),
            pltpu.VMEM((OWN, width), F32),
            pltpu.VMEM((OWN, width), BF16),
            pltpu.VMEM((OWN, inner_width), F32),
            pltpu.VMEM((OWN, width), BF16),
            pltpu.SemaphoreType.DMA((2,)),
        ],
        compiler_params=pltpu.CompilerParams(vmem_limit_bytes=VMEM_LIMIT),
        cost_estimate=pl.CostEstimate(
            flops=12_000_000_000, bytes_accessed=40_000_000, transcendentals=2_000_000
        ),
        name="middle",
    )(
        meta, attended, lse, tokens, memory, token_cot, memory_cot,
        wo, line(bo), line(gain1), line(shift1), line(bi), line(b2), line(gain2), line(shift2),
        wi, w2,
    )


def late_body(metas, group, *refs, batches, chains, parts):
    refs = list(refs)
    take = lambda count: [refs.pop(0) for _ in range(count)]
    rows, res_mem = take(batches), take(batches)
    grads = [[take(len(parts[b])) for _ in range(3)] for b in range(batches)]
    weights = take(3)
    out, masked = take(2)
    width = weights[0].shape[0]
    out[3 * width :, :] = jnp.zeros((out.shape[0] - 3 * width, width), BF16)
    for b in range(batches):
        lead = jnp.where(metas[b, M_SPOT] == 0, 1.0, 0.0)
        masked[b, 0:SEG, :] = rows[b][0:SEG, :]
        masked[b, SEG:OWN, :] = rows[b][SEG:OWN, :] * lead.astype(BF16)
        grad = res_mem[b][SEG:OWN, :]
        for k in range(3):
            first = 0
            for part, ref in zip(parts[b], grads[b][k]):
                grad = grad + turned(ref[SEG:OWN, :], weights[k][:, first : first + part])
                first += part
        place = ((group[0] * batches + b) * chains + metas[b, M_CHAIN]) * MEMP
        place = pl.multiple_of(3 * width + place, MEMP)
        out[pl.ds(place, MEMP), :] = (grad * lead).astype(BF16)
    cuts = sorted({sum(p[:i]) for p in parts for i in range(len(p) + 1)})
    for k in range(3):
        for low, high in zip(cuts[:-1], cuts[1:]):
            total, line = None, None
            for b in range(batches):
                lead = jnp.where(metas[b, M_SPOT] == 0, 1.0, 0.0)
                first = 0
                for part, ref in zip(parts[b], grads[b][k]):
                    if first <= low and high <= first + part:
                        grad = ref[:, low - first : high - first]
                    first += part
                value = crossed(masked[b], grad)
                total = value if total is None else total + value
                if k != 1:
                    grad = grad.astype(F32)
                    value = jnp.sum(grad[0:SEG], 0, keepdims=True)
                    value = value + jnp.sum(grad[SEG:OWN], 0, keepdims=True) * lead
                    line = value if line is None else line + value
            out[k * width : (k + 1) * width, low:high] = total.astype(BF16)
            if k != 1:
                row = lax.broadcasted_iota(jnp.int32, (16, high - low), 0)
                span = slice(3 * width + MEMP - 16, 3 * width + MEMP)
                old = out[span, low:high].astype(F32)
                line_row = 16 - 2 + k // 2
                out[span, low:high] = jnp.where(row == line_row, line, old).astype(BF16)


def late_sums(metas, group, groups, chains, rows, res, grads, weights):
    batches, width = len(rows), weights[0].shape[0]
    parts = [[part.shape[1] for part in one[0]] for one in grads]
    count = 3 * width + groups * batches * chains * MEMP
    count += -count % LATE_ROWS
    vmem, smem = pl.BlockSpec(memory_space=pltpu.VMEM), pl.BlockSpec(memory_space=pltpu.SMEM)
    flat = [part for one in grads for name in one for part in name]
    return pl.pallas_call(
        functools.partial(late_body, batches=batches, chains=chains, parts=parts),
        in_specs=[smem] * 2 + [vmem] * (2 * batches + len(flat) + 3),
        out_specs=vmem,
        out_shape=jax.ShapeDtypeStruct((count, width), BF16),
        scratch_shapes=[pltpu.VMEM((batches, OWN, width), BF16)],
        compiler_params=pltpu.CompilerParams(vmem_limit_bytes=VMEM_LIMIT),
        name="late_sums",
    )(metas, group.reshape(1), *rows, *res, *flat, *weights)


def weight_grad(left, right):
    return lax.dot_general(left, right, (((0,), (0,)), ((), ())), preferred_element_type=F32)


def swap(value, mask):
    sizes = lax.axis_size("dp") * lax.axis_size("blk")
    return lax.ppermute(value, ("dp", "blk"), [(i, i ^ mask) for i in range(sizes)])


def sum_everywhere(value):
    blk = lax.axis_size("blk")
    place = lax.axis_index("dp") * blk + lax.axis_index("blk")
    groups = [(1,), (2, blk), (4, 8)]
    bit = 2 * blk
    while bit < blk * lax.axis_size("dp"):
        groups.append((bit,))
        bit *= 2
    masks_of = lambda group: [
        sum(bit for i, bit in enumerate(group) if (k >> i) & 1) for k in range(1 << len(group))
    ]
    own_of = lambda group: sum(((place // bit) % 2) << i for i, bit in enumerate(group))
    for group in groups:
        masks, own = masks_of(group), own_of(group)
        size = value.shape[0] // len(masks)
        part = lambda k: lax.dynamic_slice_in_dim(value, (own ^ k) * size, size)
        got = [swap(part(k), mask) for k, mask in enumerate(masks) if k]
        value = sum((g.astype(F32) for g in got), part(0).astype(F32)).astype(BF16)
    for group in reversed(groups):
        masks, own = masks_of(group), own_of(group)
        size = value.shape[0]
        got = [value] + [swap(value, mask) for mask in masks[1:]]
        value = jnp.zeros((size * len(masks), value.shape[1]), BF16)
        for k, part in enumerate(got):
            value = lax.dynamic_update_slice_in_dim(value, part, (own ^ k) * size, 0)
    return value


def local(
    tokens, memory, chain_lengths, last_fill,
    query_proj, query_bias, key_proj, value_proj, value_bias, output_proj, output_bias,
    attn_gain, attn_shift, inner_proj, inner_bias, outer_proj, outer_bias,
    final_gain, final_shift, token_cotangent, memory_cotangent,
):
    own = lax.axis_index("blk").astype(jnp.int32)
    group = lax.axis_index("dp").astype(jnp.int32)
    groups = lax.axis_size("dp")
    batches, _, width = tokens.shape
    chains, mem_rows = memory.shape[1:3]
    pad_mem = ((0, 0), (0, 0), (0, MEMP - mem_rows), (0, 0))
    memory, memory_cotangent = jnp.pad(memory, pad_mem), jnp.pad(memory_cotangent, pad_mem)

    metas = metas_of(own, chain_lengths[:, 0], last_fill[:, 0], mem_rows)
    near, (later, metas) = gather_near(tokens[0], ([tokens[b] for b in range(1, batches)], metas))
    later, near = lax.optimization_barrier((later, near))
    pieces = [near] + [gather_all(part) for part in later]
    meta_of = [metas[b] for b in range(batches)]

    states = []
    for b in range(batches):
        meta = meta_of[b]
        attended, lse, *chain_rows = attend_forward(
            meta, pieces[b], memory[b], (query_proj, query_bias, key_proj, value_proj, value_bias)
        )
        (
            final, final_mem, payload, mem_grad, mem_stats, own_stats, res_grad, rows,
            attended_low, branch, first_low, inner, active, outer, sums, inner_sum,
        ) = middle(
            meta, attended, lse, tokens[b], memory[b], token_cotangent[b], memory_cotangent[b],
            (
                output_proj, output_bias, attn_gain, attn_shift, inner_proj, inner_bias,
                outer_proj, outer_bias, final_gain, final_shift,
            ),
        )
        if b + 1 < batches:
            meta_of[b + 1], payload = lax.optimization_barrier((meta_of[b + 1], payload))
        states.append(
            dict(
                meta=meta, rows=rows, chain_rows=chain_rows, payload=payload, mem_grad=mem_grad,
                mem_stats=mem_stats, own_stats=own_stats, res_grad=res_grad, final=final,
                final_mem=final_mem, attended_low=attended_low, branch=branch,
                first_low=first_low, inner=inner, active=active, outer=outer, sums=sums,
                inner_sum=inner_sum,
            )
        )

    def over_batches(left, right):
        return weight_grad(
            jnp.concatenate([s[left] for s in states], 0),
            jnp.concatenate([s[right] for s in states], 0),
        ).astype(BF16)

    slots = (jnp.arange(groups)[:, None, None, None, None] == group) & (
        jnp.arange(chains)[:, None, None]
        == jnp.where(metas[:, M_SPOT] == 0, metas[:, M_CHAIN], -1)[:, None, None, None]
    )
    final_mem = jnp.stack([s["final_mem"] for s in states])[None, :, None]
    early = (
        over_batches("first_low", "inner"),
        over_batches("active", "outer"),
        over_batches("attended_low", "branch"),
        jnp.concatenate(
            [
                jnp.where(slots, final_mem, 0).astype(BF16).reshape(-1, width),
                sum(s["sums"] for s in states).astype(BF16),
                sum(s["inner_sum"] for s in states).astype(BF16).reshape(-1, width),
            ],
            0,
        ),
    )
    early, *held = lax.optimization_barrier((early, *[s["meta"] for s in states]))
    for s, meta in zip(states, held):
        s["meta"] = meta
        s["gathered"] = gather_all(s["payload"])
    def backward(s, meta):
        return attend_backward(
            meta, s["gathered"], s["chain_rows"], s["mem_grad"], s["mem_stats"],
            s["own_stats"], 0, NQUAD,
        )

    *others, last = states
    for s in others:
        s["grads"] = backward(s, s["meta"])
    got, last["gathered"], early = lax.optimization_barrier(
        ([s["grads"] for s in others], last["gathered"], early)
    )
    for s, grads in zip(others, got):
        s["grads"] = grads
    early = lax.psum(early, ("dp", "blk"))

    def late_part(turn, carry):
        grads = backward(last, last["meta"] + turn)
        every = [s["grads"] for s in others] + [grads]
        late = late_sums(
            metas, group, groups, chains, [s["rows"] for s in states],
            [s["res_grad"] for s in states], [[[part] for part in one] for one in every],
            (query_proj, key_proj, value_proj),
        )
        token_grads = []
        for s, one in zip(states, every):
            grad = s["res_grad"][:SEG]
            for part, weights in zip(one, (query_proj, key_proj, value_proj)):
                grad = grad + turned(part[:SEG], weights)
            token_grads.append(grad.astype(BF16))
        return sum_everywhere(late), token_grads

    once = jnp.minimum(metas[0, M_LEN], 1)
    start = jax.tree.map(
        lambda like: jnp.zeros(like.shape, like.dtype), jax.eval_shape(late_part, once, None)
    )
    late, token_grads = lax.fori_loop(0, once, late_part, start)
    late, early = lax.optimization_barrier((late, early))
    grad_inner, grad_outer, grad_output, rest = early

    def own_slots(rows):
        rows = rows.reshape(groups, batches, chains, MEMP, width)
        return lax.dynamic_index_in_dim(rows, group, keepdims=False)[:, :, :mem_rows]

    grad_query, grad_key, grad_value = (late[i * width : (i + 1) * width] for i in range(3))
    biases = late[3 * width + MEMP - 2 : 3 * width + MEMP].astype(F32)
    count = groups * batches * chains * MEMP
    memory_grad = own_slots(late[3 * width : 3 * width + count])
    memory_out = own_slots(rest[:count])
    sums, inner_sum = rest[count : count + 8], rest[count + 8 :].reshape(1, -1)
    token_outs = [s["final"] for s in states]

    wide = lambda value: value.astype(F32)
    return (
        jnp.stack(token_outs),
        memory_out,
        jnp.stack(token_grads),
        memory_grad,
        wide(grad_query),
        biases[0],
        wide(grad_key),
        wide(grad_value),
        biases[1],
        wide(grad_output),
        wide(sums[0]),
        wide(sums[1]),
        wide(sums[2]),
        wide(grad_inner),
        wide(inner_sum[0]),
        wide(grad_outer),
        wide(sums[3]),
        wide(sums[4]),
        wide(sums[5]),
    )


def solution(mesh):
    row_spec = P(None, ("dp", "blk"), None)
    mem_spec = P(None, "dp", None, None)
    int_spec = P(None, "dp", None)
    in_specs = (row_spec, mem_spec, int_spec, int_spec) + (P(),) * 15 + (row_spec, mem_spec)
    out_specs = (row_spec, mem_spec, row_spec, mem_spec) + (P(),) * 15
    return jax.shard_map(local, mesh=mesh, in_specs=in_specs, out_specs=out_specs, check_vma=False)
```

```python
import functools

import jax
import jax.numpy as jnp
from jax import lax
from jax.experimental import pallas as pl
from jax.experimental.pallas import tpu as pltpu
from jax.sharding import PartitionSpec as P

H = 12
HD = 64
QUAD = 256
NQUAD = 3
PAIR = 128
MEMP = 32
SEG = 512
LONG = 7
NBLK = LONG + 1
CAP = NBLK * SEG
OWN = SEG + MEMP
STAT = 24
BACK_COST = 10_000_000_000
LATE_ROWS = 256
NPIECE = 14
ROWS = 272
COLS = 1024
NEG = -1e30
SHIFT_FREE = 60.0
EPS = 1e-05
F32 = jnp.float32
BF16 = jnp.bfloat16
VMEM_LIMIT = 60 * 2**20
LAST = (((1,), (1,)), ((), ()))

M_LEN, M_ROWS, M_BLOCKS, M_SPOT, M_USED, M_MEM, M_CHAIN, M_START, M_PIECE = range(9)


def plane_moves(shift_of):
    pairs = []
    for plane in range(4):
        for place in range(4):
            target = plane + shift_of(place >> 1)
            if 0 <= target < 4:
                pairs.append((4 * plane + place, 4 * target + place))
    return pairs


UP = plane_moves(lambda side: 1)
DOWN = plane_moves(lambda side: -1)
OUTWARD = plane_moves(lambda side: 1 if side else -1)
SIDE = [(i, i ^ 2) for i in range(16)]
CORE = [(i, i ^ 1) for i in range(16)]


def move(value, pairs):
    return lax.ppermute(value, "blk", pairs)


def gather_near(value, others):
    side = (lax.axis_index("blk") >> 1) & 1
    below, above, beside = move(value, UP), move(value, DOWN), move(value, SIDE)
    below, others = lax.optimization_barrier((below, others))
    far = move(jnp.where(side == 1, below, above), OUTWARD)
    moved = [move(beside, UP), move(beside, DOWN), move(far, SIDE)]
    here = [value, beside, below, above] + moved
    return here + [move(part, CORE) for part in here], others


def gather_all(value):
    return [lax.all_gather(value, "blk")]


def piece_of(own, other):
    plane = (other >> 2) - (own >> 2)
    same_side = ((other >> 1) & 1) == ((own >> 1) & 1)
    on_side = jnp.where(plane == 0, 0, jnp.where(plane < 0, 2, 3))
    off_side = jnp.where(plane == 0, 1, jnp.where(plane == -1, 4, jnp.where(plane == 1, 5, 6)))
    index = jnp.where(same_side, on_side, off_side)
    return index + jnp.where((other & 1) == (own & 1), 0, LONG)


def meta_body(own_ref, lengths, fills, meta, *, batches, chains, mem_rows):
    own = own_ref[0]
    for b in range(batches):
        end = jnp.int32(0)
        length, start, fill, chain = (jnp.int32(0) for _ in range(4))
        for c in range(chains):
            begin = end
            end = end + lengths[b, c]
            inside = (begin <= own) & (own < end)
            length = jnp.where(inside, lengths[b, c], length)
            start = jnp.where(inside, begin, start)
            fill = jnp.where(inside, fills[b, c], fill)
            chain = jnp.where(inside, c, chain)
        rows = MEMP + SEG * (length - 1) + fill
        spot = own - start
        meta[b, M_LEN] = length
        meta[b, M_ROWS] = rows
        meta[b, M_BLOCKS] = (rows + SEG - 1) // SEG
        meta[b, M_SPOT] = spot
        meta[b, M_USED] = jnp.where(spot == length - 1, fill, SEG)
        meta[b, M_MEM] = jnp.int32(mem_rows)
        meta[b, M_CHAIN] = chain
        meta[b, M_START] = start
        for place in range(8):
            meta[b, M_PIECE + place] = piece_of(own, start + place)


def metas_of(own, lengths, fills, mem_rows):
    smem = pl.BlockSpec(memory_space=pltpu.SMEM)
    body = functools.partial(
        meta_body, batches=lengths.shape[0], chains=lengths.shape[1], mem_rows=mem_rows
    )
    return pl.pallas_call(
        body,
        in_specs=[smem] * 3,
        out_specs=smem,
        out_shape=jax.ShapeDtypeStruct((lengths.shape[0], 16), jnp.int32),
        name="find_chain",
    )(own.reshape(1), lengths, fills)


def load_chain(meta, pieces, view_from, view_to, sems):
    length = meta[M_LEN]
    for spot in range(LONG):
        def start(source):
            pltpu.make_async_copy(view_from(source), view_to(spot), sems.at[spot]).start()

        @pl.when(spot < length)
        def _():
            if len(pieces) == 1:
                start(pieces[0].at[meta[M_START] + spot])
                return
            for index in range(len(pieces)):
                @pl.when(meta[M_PIECE + spot] == index)
                def _():
                    start(pieces[index])


def wait_chain(meta, pieces, view_from, view_to, sems):
    length = meta[M_LEN]
    source = pieces[0].at[0] if len(pieces) == 1 else pieces[0]
    for spot in range(LONG):
        @pl.when(spot < length)
        def _():
            pltpu.make_async_copy(view_from(source), view_to(spot), sems.at[spot]).wait()


def key_bias(meta):
    column = lax.broadcasted_iota(jnp.int32, (8, CAP), 1)
    dead = (column >= meta[M_ROWS]) | ((column >= meta[M_MEM]) & (column < MEMP))
    return jnp.where(dead, NEG, 0.0).astype(F32)


def by_chunks(blocks, run):
    def four(index, carry):
        run(index * 4, 4)
        return carry

    lax.fori_loop(0, blocks // 4, four, 0)
    for count in (1, 2, 3):
        @pl.when(blocks % 4 == count)
        def _():
            run((blocks // 4) * 4, count)


def span_of(first, count):
    return pl.ds(pl.multiple_of(first * SEG, SEG), count * SEG)


def forward_body(meta, *refs):
    pieces, refs = refs[:-16], refs[-16:]
    mem, wq, wk, wv, bq, bv, out, lse, kc, vc, qc, rows, qown, extended, acc, sems = refs
    quad = pl.program_id(0)
    width = rows.shape[1]
    length, blocks = meta[M_LEN], meta[M_BLOCKS]
    here = lambda source: source
    there = lambda spot: rows.at[pl.ds(MEMP + SEG * spot, SEG)]

    @pl.when(quad == 0)
    def _():
        load_chain(meta, pieces, here, there, sems)
        rows[0:MEMP, :] = mem[meta[M_CHAIN]]
        lse[...] = jnp.zeros_like(lse)

        @pl.when(blocks > length)
        def _():
            place = pl.multiple_of(MEMP + SEG * length, MEMP)
            rows[pl.ds(place, SEG - MEMP), :] = jnp.zeros((SEG - MEMP, width), BF16)

        wait_chain(meta, pieces, here, there, sems)

    def longest(values):
        halves = [
            jnp.max(jnp.sum(jnp.square(values[:, p : p + PAIR]), axis=1, keepdims=True))
            for p in range(0, QUAD, PAIR)
        ]
        return jnp.maximum(*halves)

    def project(start, count):
        span = pl.ds(pl.multiple_of(start, MEMP), count)
        part = rows[span, :]
        row = start + lax.broadcasted_iota(jnp.int32, (count, QUAD), 0)
        alive = (row < meta[M_ROWS]) & ((row < meta[M_MEM]) | (row >= MEMP))
        lower = (lax.broadcasted_iota(jnp.int32, (count, QUAD), 1) % PAIR) < HD
        key = jnp.dot(part, wk[...], preferred_element_type=F32)
        kc[span, :] = key.astype(BF16)
        value = jnp.dot(part, wv[...], preferred_element_type=F32) + bv[...].astype(F32)
        vc[span, :] = value.astype(BF16)
        value = jnp.where(alive, value, 0.0)
        one = jnp.where(alive, 1.0, 0.0)
        extended[0, span, :] = jnp.where(lower, value, one).astype(BF16)
        extended[1, span, :] = jnp.where(lower, one, value).astype(BF16)
        query = jnp.dot(part, wq[...], preferred_element_type=F32) + bq[...].astype(F32)
        query = query.astype(BF16) * jnp.asarray(HD**-0.5, BF16)
        qc[span, :] = query
        return longest(key)

    def project_block(block, top):
        return jnp.maximum(top, project(block * SEG, SEG))

    key_top = lax.fori_loop(0, blocks, project_block, jnp.float32(0.0))

    @pl.when(blocks == length)
    def _():
        project(length * SEG, MEMP)

    place = pl.multiple_of(MEMP + SEG * meta[M_SPOT], MEMP)
    qown[0:SEG, :] = qc[pl.ds(place, SEG), :]
    qown[SEG:OWN, :] = qc[0:MEMP, :]
    near = longest(qown[...].astype(F32)) * key_top <= SHIFT_FREE**2

    def pair(index, carry):
        cols = pl.ds(pl.multiple_of(index * PAIR, PAIR), PAIR)
        lane = lax.broadcasted_iota(jnp.int32, (OWN, PAIR), 1)
        halves = (0, 1)
        mine = [(lane // HD) == half for half in halves]
        numbers = [lane == quad * 4 + index * 2 + half for half in halves]
        both = qown[:, cols]
        queries = [jnp.where(mine[half], both, jnp.zeros_like(both)) for half in halves]
        acc[...] = jnp.zeros_like(acc)

        def score(half, span):
            return lax.dot_general(queries[half], kc[span, cols], LAST, preferred_element_type=F32)

        def gather(half, span, terms):
            values = extended[half, span, cols]
            return jnp.dot(terms.astype(BF16), values, preferred_element_type=F32)

        @pl.when(near)
        def _():
            def run(first, count):
                span = span_of(first, count)
                for half in halves:
                    acc[half] += gather(half, span, jnp.exp(score(half, span)))

            by_chunks(blocks, run)

        @pl.when(jnp.logical_not(near))
        def _():
            for half in halves:
                def run(block, top):
                    span = span_of(block, 1)
                    column = block * SEG + lax.broadcasted_iota(jnp.int32, (OWN, SEG), 1)
                    dead = (column >= meta[M_ROWS]) | ((column >= meta[M_MEM]) & (column < MEMP))
                    scores = jnp.where(dead, NEG, score(half, span))
                    new = jnp.maximum(top, jnp.max(scores, axis=1, keepdims=True))
                    terms = gather(half, span, jnp.exp(scores - new))
                    acc[half] = acc[half] * jnp.exp(top - new) + terms
                    return new

                top = lax.fori_loop(0, blocks, run, jnp.full((OWN, 1), NEG, F32))
                lse[...] = jnp.where(numbers[half], top, lse[...])

        sums = [acc[half] for half in halves]
        value = jnp.where(mine[0], sums[0], sums[1])
        total = pltpu.roll(jnp.where(mine[0], sums[1], sums[0]), HD, 1)
        out[:, cols] = value * (1.0 / total)
        turned_total = pltpu.roll(total, HD, 1)
        for half in halves:
            spread = jnp.where(mine[half], total, turned_total)
            lse[...] += jnp.where(numbers[half], jnp.log(spread), 0.0)
        return carry

    lax.fori_loop(0, 2, pair, 0)


def attend_forward(meta, pieces, mem, weights):
    wq, bq, wk, wv, bv = weights
    width = wq.shape[0]
    whole = lambda shape: pl.BlockSpec(shape, lambda quad, meta: (0,) * len(shape))
    column = lambda count: pl.BlockSpec((count, QUAD), lambda quad, meta: (0, quad))
    return pl.pallas_call(
        forward_body,
        grid_spec=pltpu.PrefetchScalarGridSpec(
            num_scalar_prefetch=1,
            grid=(NQUAD,),
            in_specs=[pl.BlockSpec(memory_space=pl.ANY)] * len(pieces)
            + [whole((mem.shape[0], MEMP, width))]
            + [column(width)] * 3
            + [column(1)] * 2,
            out_specs=[column(OWN), whole((OWN, PAIR))] + [column(CAP)] * 3,
            scratch_shapes=[
                pltpu.VMEM((CAP, width), BF16),
                pltpu.VMEM((OWN, QUAD), BF16),
                pltpu.VMEM((2, CAP, QUAD), BF16),
                pltpu.VMEM((2, OWN, PAIR), F32),
                pltpu.SemaphoreType.DMA((LONG,)),
            ],
        ),
        out_shape=[
            jax.ShapeDtypeStruct((OWN, width), F32),
            jax.ShapeDtypeStruct((OWN, PAIR), F32),
        ]
        + [jax.ShapeDtypeStruct((CAP, width), BF16)] * 3,
        compiler_params=pltpu.CompilerParams(vmem_limit_bytes=VMEM_LIMIT),
        cost_estimate=pl.CostEstimate(
            flops=40_000_000_000, bytes_accessed=30_000_000, transcendentals=23_000_000
        ),
        name="attend_forward",
    )(meta, *pieces, mem, wq, wk, wv, bq.reshape(1, -1), bv.reshape(1, -1))


def backward_body(start, count, meta, *refs):
    pieces, refs = refs[:-22], refs[-22:]
    (
        kc, vc, qc, mem_grad, mem_stats, own_stats,
        dq, dk, dv,
        doc, stats, chain_stats, qown, kown, vown, down, bias, qacc, kacc, vacc, sems, stat_sems,
    ) = refs
    step = pl.program_id(0)
    quad = start + step
    length = meta[M_LEN]

    @pl.when(step == 0)
    def _():
        rows_from = lambda index: lambda ref: ref.at[0:SEG, pl.ds((start + index) * QUAD, QUAD)]
        rows_to = lambda index: lambda spot: doc.at[index, pl.ds(MEMP + SEG * spot, SEG)]
        stat_from = lambda ref: ref.at[SEG : SEG + 2 * STAT, 0:SEG]
        stat_to = lambda spot: stats.at[spot]
        load_chain(meta, pieces, stat_from, stat_to, stat_sems)
        for index in range(count):
            load_chain(meta, pieces, rows_from(index), rows_to(index), sems.at[index])
        bias[...] = key_bias(meta)
        for index in range(count):
            doc[index, 0:MEMP, :] = mem_grad[:, (start + index) * QUAD : (start + index + 1) * QUAD]

            @pl.when(meta[M_BLOCKS] > length)
            def _():
                place = pl.multiple_of(MEMP + SEG * length, MEMP)
                doc[index, pl.ds(place, SEG - MEMP), :] = jnp.zeros((SEG - MEMP, QUAD), BF16)

        wait_chain(meta, pieces, stat_from, stat_to, stat_sems)
        for spot in range(NBLK):
            span = slice(SEG * spot, SEG * (spot + 1))
            if spot == LONG:
                chain_stats[:, span] = jnp.zeros((STAT, SEG), F32)
                continue

            @pl.when(spot < length)
            def _():
                pair = stats[spot].astype(F32)
                chain_stats[:, span] = pair[0:STAT] + pair[STAT : 2 * STAT]

            @pl.when(spot >= length)
            def _():
                chain_stats[:, span] = jnp.zeros((STAT, SEG), F32)

        moved = pltpu.roll(chain_stats[...], MEMP, 1)
        column = lax.broadcasted_iota(jnp.int32, (STAT, CAP), 1)
        entry = lax.broadcasted_iota(jnp.int32, (STAT, CAP), 0)
        beyond = jnp.where(entry < H, -NEG, 0.0)
        chain_stats[...] = jnp.where(column < MEMP + SEG * length, moved, beyond)
        lane = lax.broadcasted_iota(jnp.int32, (STAT, PAIR), 1)
        at_front = pltpu.roll(mem_stats[...], MEMP, 1)
        chain_stats[:, 0:PAIR] = jnp.where(lane < MEMP, at_front, chain_stats[:, 0:PAIR])
        for index in range(count):
            wait_chain(meta, pieces, rows_from(index), rows_to(index), sems.at[index])

    place = pl.multiple_of(MEMP + SEG * meta[M_SPOT], MEMP)
    for own, chain in ((qown, qc), (kown, kc), (vown, vc), (down, doc.at[step])):
        own[0:SEG, :] = chain[pl.ds(place, SEG), :]
        own[SEG:OWN, :] = chain[0:MEMP, :]

    def head(index, carry):
        cols = pl.ds(pl.multiple_of((index // 2) * PAIR, PAIR), PAIR)
        number = quad * 4 + index
        lane = lax.broadcasted_iota(jnp.int32, (OWN, PAIR), 1)
        mine = (lane // HD) == (index % 2)
        masked = lambda ref: jnp.where(mine, ref[:, cols], jnp.zeros((OWN, PAIR), BF16))
        query, key, value, grad = masked(qown), masked(kown), masked(vown), masked(down)
        pick = lambda at: jnp.sum(jnp.where(lane == at, own_stats[...], 0.0), axis=1, keepdims=True)
        log_total, delta = pick(number), pick(H + number)
        for acc in (qacc, kacc, vacc):
            acc[...] = jnp.zeros_like(acc)

        def run(first, size):
            span = span_of(first, size)
            keys, values = kc[span, cols], vc[span, cols]
            scores = lax.dot_general(query, keys, LAST, preferred_element_type=F32)
            weights = jnp.exp(scores + bias[0:1, span] - log_total)
            weight_grad = lax.dot_general(grad, values, LAST, preferred_element_type=F32)
            score_grad = (weights * (weight_grad - delta)).astype(BF16)
            qacc[...] += jnp.dot(score_grad, keys, preferred_element_type=F32)

            queries, grads = qc[span, cols], doc[step, span, cols]
            scores = lax.dot_general(key, queries, LAST, preferred_element_type=F32)
            weights = jnp.exp(scores - chain_stats[pl.ds(number, 1), span])
            weight_grad = lax.dot_general(value, grads, LAST, preferred_element_type=F32)
            score_grad = (
                weights * (weight_grad - chain_stats[pl.ds(H + number, 1), span])
            ).astype(BF16)
            vacc[...] += jnp.dot(weights.astype(BF16), grads, preferred_element_type=F32)
            kacc[...] += jnp.dot(score_grad, queries, preferred_element_type=F32)

        by_chunks(meta[M_BLOCKS], run)
        row = lax.broadcasted_iota(jnp.int32, (OWN, PAIR), 0)
        alive = (row < meta[M_USED]) | ((row >= SEG) & (row < SEG + meta[M_MEM]))
        query_sum = qacc[...] * (HD**-0.5)
        key_sum = jnp.where(alive, kacc[...], 0.0)
        value_sum = jnp.where(alive, vacc[...], 0.0)
        for ref, sums in ((dq, query_sum), (dk, key_sum), (dv, value_sum)):
            ref[:, cols] = jnp.where(mine, sums.astype(BF16), ref[:, cols])
        return carry

    lax.fori_loop(0, 4, head, 0)


def attend_backward(meta, pieces, chain, mem_grad, mem_stats, own_stats, start, count):
    width = mem_grad.shape[1]
    whole = lambda shape: pl.BlockSpec(shape, lambda quad, meta: (0,) * len(shape))
    chain_column = pl.BlockSpec((CAP, QUAD), lambda step, meta: (0, start + step))
    own_column = pl.BlockSpec((OWN, QUAD), lambda step, meta: (0, step))
    return pl.pallas_call(
        functools.partial(backward_body, start, count),
        grid_spec=pltpu.PrefetchScalarGridSpec(
            num_scalar_prefetch=1,
            grid=(count,),
            in_specs=[pl.BlockSpec(memory_space=pl.ANY)] * len(pieces)
            + [chain_column] * 3
            + [whole((MEMP, width)), whole((STAT, PAIR)), whole((OWN, PAIR))],
            out_specs=[own_column] * 3,
            scratch_shapes=[
                pltpu.VMEM((count, CAP, QUAD), BF16),
                pltpu.VMEM((LONG, 2 * STAT, SEG), BF16),
                pltpu.VMEM((STAT, CAP), F32),
            ]
            + [pltpu.VMEM((OWN, QUAD), BF16)] * 4
            + [
                pltpu.VMEM((8, CAP), F32),
                pltpu.VMEM((OWN, PAIR), F32),
                pltpu.VMEM((OWN, PAIR), F32),
                pltpu.VMEM((OWN, PAIR), F32),
                pltpu.SemaphoreType.DMA((count, LONG)),
                pltpu.SemaphoreType.DMA((LONG,)),
            ],
        ),
        out_shape=[jax.ShapeDtypeStruct((OWN, count * QUAD), BF16)] * 3,
        compiler_params=pltpu.CompilerParams(vmem_limit_bytes=VMEM_LIMIT),
        cost_estimate=pl.CostEstimate(
            flops=BACK_COST, bytes_accessed=1_000_000, transcendentals=0
        ),
        name="attend_backward",
    )(meta, *pieces, *chain, mem_grad, mem_stats, own_stats)


def norm_stats(values):
    centered = values - jnp.mean(values, axis=-1, keepdims=True)
    scale = lax.rsqrt(jnp.mean(centered * centered, axis=-1, keepdims=True) + EPS)
    return centered * scale, scale


def norm_back(normed, scale, upstream):
    mean = jnp.mean(upstream, axis=-1, keepdims=True)
    along = jnp.mean(upstream * normed, axis=-1, keepdims=True)
    return scale * (upstream - mean - normed * along)


def turned(left, right):
    return lax.dot_general(left, right, LAST, preferred_element_type=F32)


def crossed(left, right):
    return lax.dot_general(left, right, (((0,), (0,)), ((), ())), preferred_element_type=F32)


def middle_body(
    meta, attended, lse, tokens, memory, token_cot, memory_cot,
    wo, bo, gain1, shift1, bi, b2, gain2, shift2, wi_from, w2_from,
    final, final_mem, payload, mem_grad, mem_stats, own_stats, res_grad, rows,
    attended_low, branch_out, first_low, inner_out, active, outer_out, sums, inner_sum,
    wi, w2, first, norm1, scale1, total, second_grad, outer_grad, slope, cots, weight_sems,
):
    width, inner_width = wi.shape
    wi_copy = pltpu.make_async_copy(wi_from, wi, weight_sems.at[0])
    w2_copy = pltpu.make_async_copy(w2_from, w2, weight_sems.at[1])
    wi_copy.start()
    w2_copy.start()
    chain = meta[M_CHAIN]
    lead = jnp.where(meta[M_SPOT] == 0, 1.0, 0.0)
    rows[0:SEG, :] = tokens[...]
    rows[SEG:OWN, :] = memory[chain]
    cots[0:SEG, :] = token_cot[...]
    cots[SEG:OWN, :] = memory_cot[chain]
    attended_low[...] = attended[...].astype(BF16)
    total[...] = jnp.dot(attended_low[...], wo[...], preferred_element_type=F32)
    sums[...] = jnp.zeros_like(sums)
    inner_sum[...] = jnp.zeros_like(inner_sum)
    vector = lambda ref: ref[...].astype(F32)

    def by_rows(run):
        def step(index, carry):
            start = pl.multiple_of(index * ROWS, ROWS)
            row = start + lax.broadcasted_iota(jnp.int32, (ROWS, 1), 0)
            live = (row < meta[M_USED]) | ((row >= SEG) & (row < SEG + meta[M_MEM]))
            counted = jnp.where(row < SEG, 1.0, lead)
            run(pl.ds(start, ROWS), live, counted)
            return carry

        lax.fori_loop(0, OWN // ROWS, step, 0)

    def by_columns(run):
        def step(index, carry):
            run(pl.ds(pl.multiple_of(index * COLS, COLS), COLS))
            return carry

        lax.fori_loop(0, inner_width // COLS, step, 0)

    def add(place, value):
        sums[place : place + 1, :] += jnp.sum(value, axis=0, keepdims=True)

    def first_part(span, live, counted):
        value = rows[span, :].astype(F32) + total[span, :] + vector(bo)
        normed, scale = norm_stats(value)
        norm1[span, :] = normed
        scale1[span, :] = jnp.broadcast_to(scale, (ROWS, PAIR))
        value = normed * vector(gain1) + vector(shift1)
        first[span, :] = value
        first_low[span, :] = value.astype(BF16)

    by_rows(first_part)
    wi_copy.wait()
    w2_copy.wait()
    total[...] = jnp.zeros_like(total)

    def inner_part(cols):
        inner = jnp.dot(first_low[...], wi[:, cols], preferred_element_type=F32)
        inner = inner + bi[:, cols].astype(F32)
        cdf = 0.5 * (1.0 + lax.erf(inner * (2.0**-0.5)))
        density = jnp.exp(-0.5 * inner * inner) * 0.3989422804014327
        slope[:, cols] = cdf + inner * density
        low = (inner * cdf).astype(BF16)
        active[:, cols] = low
        total[...] += jnp.dot(low, w2[cols, :], preferred_element_type=F32)

    by_columns(inner_part)

    def final_part(span, live, counted):
        normed, scale = norm_stats(first[span, :] + total[span, :] + vector(b2))
        value = jnp.where(live, normed * vector(gain2) + vector(shift2), 0.0)
        rows_low = value.astype(BF16)
        outer_out[span, :] = rows_low
        cot = cots[span, :].astype(F32)
        cot = jnp.where(live, cot, 0.0)
        weighted = cot * counted
        add(4, weighted * normed)
        add(5, weighted)
        grad = norm_back(normed, scale, cot * vector(gain2))
        second_grad[span, :] = grad
        outer_grad[span, :] = grad.astype(BF16)
        add(3, grad.astype(BF16).astype(F32) * counted)

    by_rows(final_part)
    final[...] = outer_out[0:SEG, :]
    final_mem[...] = outer_out[SEG:OWN, :]
    outer_out[0:SEG, :] = outer_grad[0:SEG, :]
    outer_out[SEG:OWN, :] = outer_grad[SEG:OWN, :] * lead.astype(BF16)
    total[...] = jnp.zeros_like(total)

    def inner_back(cols):
        grad = (turned(outer_grad[...], w2[cols, :]) * slope[:, cols]).astype(BF16)
        total[...] += turned(grad, wi[:, cols])
        tail = grad[SEG:OWN] * lead.astype(BF16)
        inner_out[0:SEG, cols] = grad[0:SEG]
        inner_out[SEG:OWN, cols] = tail
        inner_sum[:, cols] = jnp.sum(grad[0:SEG].astype(F32), axis=0, keepdims=True) + jnp.sum(
            tail.astype(F32), axis=0, keepdims=True
        )

    by_columns(inner_back)

    def last_part(span, live, counted):
        grad = second_grad[span, :] + total[span, :]
        normed = norm1[span, :]
        weighted = grad * counted
        add(1, weighted * normed)
        add(2, weighted)
        grad = norm_back(normed, scale1[span, 0:1], grad * vector(gain1))
        res_grad[span, :] = grad
        low = grad.astype(BF16)
        outer_grad[span, :] = low
        low = (low.astype(F32) * counted).astype(BF16)
        branch_out[span, :] = low
        add(0, low.astype(F32))

    by_rows(last_part)
    total[...] = turned(outer_grad[...], wo[...])
    feature = lax.broadcasted_iota(jnp.int32, (width, PAIR), 0)
    lane = lax.broadcasted_iota(jnp.int32, (width, PAIR), 1)
    head_of = jnp.where(feature // HD == lane - H, 1.0, 0.0).astype(BF16)

    def delta_part(span, live, counted):
        low = total[span, :].astype(BF16)
        outer_grad[span, :] = low
        product = low.astype(F32) * attended[span, :]
        high = product.astype(BF16)
        rest = (product - high.astype(F32)).astype(BF16)
        delta = jnp.dot(high, head_of, preferred_element_type=F32)
        delta = delta + jnp.dot(rest, head_of, preferred_element_type=F32)
        own_stats[span, :] = lse[span, :] + delta

    by_rows(delta_part)
    payload[0:SEG, :] = outer_grad[0:SEG, :]
    mem_grad[...] = outer_grad[SEG:OWN, :]
    stats = jnp.transpose(own_stats[0:SEG, :])[0:STAT]
    high = stats.astype(BF16)
    rest = (stats - high.astype(F32)).astype(BF16)
    both = jnp.concatenate([high.astype(F32), rest.astype(F32)], 0).astype(BF16)
    payload[SEG : SEG + 2 * STAT, 0:SEG] = both
    payload[SEG : SEG + 2 * STAT, SEG:width] = jnp.zeros((2 * STAT, width - SEG), BF16)
    mem_stats[...] = jnp.transpose(own_stats[OWN - PAIR : OWN, :])[0:STAT]


def middle(meta, attended, lse, tokens, memory, token_cot, memory_cot, weights):
    wo, bo, gain1, shift1, wi, bi, w2, b2, gain2, shift2 = weights
    width, inner_width = wi.shape
    vmem, line = pl.BlockSpec(memory_space=pltpu.VMEM), lambda value: value.reshape(1, -1)
    hbm = pl.BlockSpec(memory_space=pl.ANY)
    shape = jax.ShapeDtypeStruct
    return pl.pallas_call(
        middle_body,
        in_specs=[pl.BlockSpec(memory_space=pltpu.SMEM)] + [vmem] * 14 + [hbm] * 2,
        out_specs=[vmem] * 16,
        out_shape=[
            shape((SEG, width), BF16),
            shape((MEMP, width), BF16),
            shape((SEG + 2 * STAT, width), BF16),
            shape((MEMP, width), BF16),
            shape((STAT, PAIR), F32),
            shape((OWN, PAIR), F32),
            shape((OWN, width), F32),
            shape((OWN, width), BF16),
            shape((OWN, width), BF16),
            shape((OWN, width), BF16),
            shape((OWN, width), BF16),
            shape((OWN, inner_width), BF16),
            shape((OWN, inner_width), BF16),
            shape((OWN, width), BF16),
            shape((8, width), F32),
            shape((1, inner_width), F32),
        ],
        scratch_shapes=[
            pltpu.VMEM((width, inner_width), BF16),
            pltpu.VMEM((inner_width, width), BF16),
            pltpu.VMEM((OWN, width), F32),
            pltpu.VMEM((OWN, width), F32),
            pltpu.VMEM((OWN, PAIR), F32),
            pltpu.VMEM((OWN, width), F32),
            pltpu.VMEM((OWN, width), F32),
            pltpu.VMEM((OWN, width), BF16),
            pltpu.VMEM((OWN, inner_width), F32),
            pltpu.VMEM((OWN, width), BF16),
            pltpu.SemaphoreType.DMA((2,)),
        ],
        compiler_params=pltpu.CompilerParams(vmem_limit_bytes=VMEM_LIMIT),
        cost_estimate=pl.CostEstimate(
            flops=12_000_000_000, bytes_accessed=40_000_000, transcendentals=2_000_000
        ),
        name="middle",
    )(
        meta, attended, lse, tokens, memory, token_cot, memory_cot,
        wo, line(bo), line(gain1), line(shift1), line(bi), line(b2), line(gain2), line(shift2),
        wi, w2,
    )


def late_body(metas, group, *refs, batches, chains, parts):
    refs = list(refs)
    take = lambda count: [refs.pop(0) for _ in range(count)]
    rows, res_mem = take(batches), take(batches)
    grads = [[take(len(parts[b])) for _ in range(3)] for b in range(batches)]
    weights = take(3)
    out, masked = take(2)
    width = weights[0].shape[0]
    out[3 * width :, :] = jnp.zeros((out.shape[0] - 3 * width, width), BF16)
    for b in range(batches):
        lead = jnp.where(metas[b, M_SPOT] == 0, 1.0, 0.0)
        masked[b, 0:SEG, :] = rows[b][0:SEG, :]
        masked[b, SEG:OWN, :] = rows[b][SEG:OWN, :] * lead.astype(BF16)
        grad = res_mem[b][SEG:OWN, :]
        for k in range(3):
            first = 0
            for part, ref in zip(parts[b], grads[b][k]):
                grad = grad + turned(ref[SEG:OWN, :], weights[k][:, first : first + part])
                first += part
        place = ((group[0] * batches + b) * chains + metas[b, M_CHAIN]) * MEMP
        place = pl.multiple_of(3 * width + place, MEMP)
        out[pl.ds(place, MEMP), :] = (grad * lead).astype(BF16)
    cuts = sorted({sum(p[:i]) for p in parts for i in range(len(p) + 1)})
    for k in range(3):
        for low, high in zip(cuts[:-1], cuts[1:]):
            total, line = None, None
            for b in range(batches):
                lead = jnp.where(metas[b, M_SPOT] == 0, 1.0, 0.0)
                first = 0
                for part, ref in zip(parts[b], grads[b][k]):
                    if first <= low and high <= first + part:
                        grad = ref[:, low - first : high - first]
                    first += part
                value = crossed(masked[b], grad)
                total = value if total is None else total + value
                if k != 1:
                    grad = grad.astype(F32)
                    value = jnp.sum(grad[0:SEG], 0, keepdims=True)
                    value = value + jnp.sum(grad[SEG:OWN], 0, keepdims=True) * lead
                    line = value if line is None else line + value
            out[k * width : (k + 1) * width, low:high] = total.astype(BF16)
            if k != 1:
                row = lax.broadcasted_iota(jnp.int32, (16, high - low), 0)
                span = slice(3 * width + MEMP - 16, 3 * width + MEMP)
                old = out[span, low:high].astype(F32)
                line_row = 16 - 2 + k // 2
                out[span, low:high] = jnp.where(row == line_row, line, old).astype(BF16)


def late_sums(metas, group, groups, chains, rows, res, grads, weights):
    batches, width = len(rows), weights[0].shape[0]
    parts = [[part.shape[1] for part in one[0]] for one in grads]
    count = 3 * width + groups * batches * chains * MEMP
    count += -count % LATE_ROWS
    vmem, smem = pl.BlockSpec(memory_space=pltpu.VMEM), pl.BlockSpec(memory_space=pltpu.SMEM)
    flat = [part for one in grads for name in one for part in name]
    return pl.pallas_call(
        functools.partial(late_body, batches=batches, chains=chains, parts=parts),
        in_specs=[smem] * 2 + [vmem] * (2 * batches + len(flat) + 3),
        out_specs=vmem,
        out_shape=jax.ShapeDtypeStruct((count, width), BF16),
        scratch_shapes=[pltpu.VMEM((batches, OWN, width), BF16)],
        compiler_params=pltpu.CompilerParams(vmem_limit_bytes=VMEM_LIMIT),
        name="late_sums",
    )(metas, group.reshape(1), *rows, *res, *flat, *weights)


def weight_grad(left, right):
    return lax.dot_general(left, right, (((0,), (0,)), ((), ())), preferred_element_type=F32)


def swap(value, mask):
    sizes = lax.axis_size("dp") * lax.axis_size("blk")
    return lax.ppermute(value, ("dp", "blk"), [(i, i ^ mask) for i in range(sizes)])


def sum_everywhere(value, beside):
    blk = lax.axis_size("blk")
    place = lax.axis_index("dp") * blk + lax.axis_index("blk")
    groups = [(1,), (2, blk), (4, 8)]
    bit = 2 * blk
    while bit < blk * lax.axis_size("dp"):
        groups.append((bit,))
        bit *= 2
    masks_of = lambda group: [
        sum(bit for i, bit in enumerate(group) if (k >> i) & 1) for k in range(1 << len(group))
    ]
    own_of = lambda group: sum(((place // bit) % 2) << i for i, bit in enumerate(group))
    for group in groups:
        masks, own = masks_of(group), own_of(group)
        size = value.shape[0] // len(masks)
        part = lambda k: lax.dynamic_slice_in_dim(value, (own ^ k) * size, size)
        got = [swap(part(k), mask) for k, mask in enumerate(masks) if k]
        if group == groups[1]:
            got[-1], beside = lax.optimization_barrier((got[-1], beside))
        value = sum((g.astype(F32) for g in got), part(0).astype(F32)).astype(BF16)
    for group in reversed(groups):
        masks, own = masks_of(group), own_of(group)
        size = value.shape[0]
        got = [value] + [swap(value, mask) for mask in masks[1:]]
        value = jnp.zeros((size * len(masks), value.shape[1]), BF16)
        for k, part in enumerate(got):
            value = lax.dynamic_update_slice_in_dim(value, part, (own ^ k) * size, 0)
    return value, beside


def local(
    tokens, memory, chain_lengths, last_fill,
    query_proj, query_bias, key_proj, value_proj, value_bias, output_proj, output_bias,
    attn_gain, attn_shift, inner_proj, inner_bias, outer_proj, outer_bias,
    final_gain, final_shift, token_cotangent, memory_cotangent,
):
    own = lax.axis_index("blk").astype(jnp.int32)
    group = lax.axis_index("dp").astype(jnp.int32)
    groups = lax.axis_size("dp")
    batches, _, width = tokens.shape
    chains, mem_rows = memory.shape[1:3]
    pad_mem = ((0, 0), (0, 0), (0, MEMP - mem_rows), (0, 0))
    memory, memory_cotangent = jnp.pad(memory, pad_mem), jnp.pad(memory_cotangent, pad_mem)

    metas = metas_of(own, chain_lengths[:, 0], last_fill[:, 0], mem_rows)
    near, (later, metas) = gather_near(tokens[0], ([tokens[b] for b in range(1, batches)], metas))
    later, near = lax.optimization_barrier((later, near))
    pieces = [near] + [gather_all(part) for part in later]
    meta_of = [metas[b] for b in range(batches)]

    states = []
    for b in range(batches):
        meta = meta_of[b]
        attended, lse, *chain_rows = attend_forward(
            meta, pieces[b], memory[b], (query_proj, query_bias, key_proj, value_proj, value_bias)
        )
        (
            final, final_mem, payload, mem_grad, mem_stats, own_stats, res_grad, rows,
            attended_low, branch, first_low, inner, active, outer, sums, inner_sum,
        ) = middle(
            meta, attended, lse, tokens[b], memory[b], token_cotangent[b], memory_cotangent[b],
            (
                output_proj, output_bias, attn_gain, attn_shift, inner_proj, inner_bias,
                outer_proj, outer_bias, final_gain, final_shift,
            ),
        )
        if b + 1 < batches:
            meta_of[b + 1], payload = lax.optimization_barrier((meta_of[b + 1], payload))
        states.append(
            dict(
                meta=meta, rows=rows, chain_rows=chain_rows, payload=payload, mem_grad=mem_grad,
                mem_stats=mem_stats, own_stats=own_stats, res_grad=res_grad, final=final,
                final_mem=final_mem, attended_low=attended_low, branch=branch,
                first_low=first_low, inner=inner, active=active, outer=outer, sums=sums,
                inner_sum=inner_sum,
            )
        )

    def over_batches(left, right):
        return weight_grad(
            jnp.concatenate([s[left] for s in states], 0),
            jnp.concatenate([s[right] for s in states], 0),
        ).astype(BF16)

    slots = (jnp.arange(groups)[:, None, None, None, None] == group) & (
        jnp.arange(chains)[:, None, None]
        == jnp.where(metas[:, M_SPOT] == 0, metas[:, M_CHAIN], -1)[:, None, None, None]
    )
    final_mem = jnp.stack([s["final_mem"] for s in states])[None, :, None]
    early = (
        over_batches("first_low", "inner"),
        over_batches("active", "outer"),
        over_batches("attended_low", "branch"),
        jnp.concatenate(
            [
                jnp.where(slots, final_mem, 0).astype(BF16).reshape(-1, width),
                sum(s["sums"] for s in states).astype(BF16),
                sum(s["inner_sum"] for s in states).astype(BF16).reshape(-1, width),
            ],
            0,
        ),
    )
    early, *held = lax.optimization_barrier((early, *[s["meta"] for s in states]))
    for s, meta in zip(states, held):
        s["meta"] = meta
        s["gathered"] = gather_all(s["payload"])
    def backward(s, meta):
        return attend_backward(
            meta, s["gathered"], s["chain_rows"], s["mem_grad"], s["mem_stats"],
            s["own_stats"], 0, NQUAD,
        )

    *others, last = states
    for s in others:
        s["grads"] = backward(s, s["meta"])
    got, last["gathered"], early = lax.optimization_barrier(
        ([s["grads"] for s in others], last["gathered"], early)
    )
    for s, grads in zip(others, got):
        s["grads"] = grads
    early = lax.psum(early, ("dp", "blk"))

    def late_part(turn, carry):
        grads = backward(last, last["meta"] + turn)
        every, grads = lax.optimization_barrier(([s["grads"] for s in others], grads))
        every = every + [grads]
        late = late_sums(
            metas, group, groups, chains, [s["rows"] for s in states],
            [s["res_grad"] for s in states], [[[part] for part in one] for one in every],
            (query_proj, key_proj, value_proj),
        )
        token_grads = []
        for s, one in zip(states, every):
            grad = s["res_grad"][:SEG]
            for part, weights in zip(one, (query_proj, key_proj, value_proj)):
                grad = grad + turned(part[:SEG], weights)
            token_grads.append(grad.astype(BF16))
        return sum_everywhere(late, jnp.stack(token_grads))

    once = jnp.minimum(metas[0, M_LEN], 1)
    start = jax.tree.map(
        lambda like: jnp.zeros(like.shape, like.dtype), jax.eval_shape(late_part, once, None)
    )
    late, token_grads = lax.fori_loop(0, once, late_part, start)
    late, early = lax.optimization_barrier((late, early))
    grad_inner, grad_outer, grad_output, rest = early

    def own_slots(rows):
        rows = rows.reshape(groups, batches, chains, MEMP, width)
        return lax.dynamic_index_in_dim(rows, group, keepdims=False)[:, :, :mem_rows]

    grad_query, grad_key, grad_value = (late[i * width : (i + 1) * width] for i in range(3))
    biases = late[3 * width + MEMP - 2 : 3 * width + MEMP].astype(F32)
    count = groups * batches * chains * MEMP
    memory_grad = own_slots(late[3 * width : 3 * width + count])
    memory_out = own_slots(rest[:count])
    sums, inner_sum = rest[count : count + 8], rest[count + 8 :].reshape(1, -1)
    token_outs = [s["final"] for s in states]

    wide = lambda value: value.astype(F32)
    return (
        jnp.stack(token_outs),
        memory_out,
        token_grads,
        memory_grad,
        wide(grad_query),
        biases[0],
        wide(grad_key),
        wide(grad_value),
        biases[1],
        wide(grad_output),
        wide(sums[0]),
        wide(sums[1]),
        wide(sums[2]),
        wide(grad_inner),
        wide(inner_sum[0]),
        wide(grad_outer),
        wide(sums[3]),
        wide(sums[4]),
        wide(sums[5]),
    )


def solution(mesh):
    row_spec = P(None, ("dp", "blk"), None)
    mem_spec = P(None, "dp", None, None)
    int_spec = P(None, "dp", None)
    in_specs = (row_spec, mem_spec, int_spec, int_spec) + (P(),) * 15 + (row_spec, mem_spec)
    out_specs = (row_spec, mem_spec, row_spec, mem_spec) + (P(),) * 15
    return jax.shard_map(local, mesh=mesh, in_specs=in_specs, out_specs=out_specs, check_vma=False)
```
